32 devices in a mesh: seq: 4 (over x, core), clus: 8 (over z, y).
Axes of the slice: x: 2, y: 2, z: 4, core: 2. Of those that a mesh axis runs over, the one named last changes fastest.
Arguments:
- features: bfloat16 [4096, 1024], P(('seq', 'clus')), may hold values from -6 to 6
- shortlist: int32 [4096, 16], P(('seq', 'clus')), may hold values from 0 to 63, all different within a row; in each aligned block of 128 rows (0 to 127, 128 to 255, ...) at most 40 rows name the same one
- positives: int32 [4096, 4], P(('seq', 'clus')), may hold values from 0 to 2047
- cluster_sizes: int32 [64], P('clus'), may hold values from 1 to 128, 6144 in all
- weights: bfloat16 [8192, 1024], P('clus'), may hold values from -0.1875 to 0.1875
Outputs:
- feature_grad: bfloat16 [4096, 1024], P(('seq', 'clus'))
- weight_grad: bfloat16 [8192, 1024], P('clus', 'seq')
The draws below stay inside these ranges and needn't reach their ends.
Inputs may be any that keep to these rules, and one draw needn't show every extreme that they name: `shortlist`: the 16 ids of a row are distinct; within the rows of one device (aligned blocks of 128 rows) no cluster is named by more than 40 rows, a bound that some block reaches. `positives`: a value q names offset q % 128 of the cluster at shortlist place q // 128; values may repeat, and offsets at or past that cluster's size name nothing. `cluster_sizes`: some cluster has exactly 128 labels.
All inputs are finite; a program needn't handle non-finite values.
Results may differ from the reference program's by a relative error of at most 0.018.
Values may be sent and summed in bfloat16 or wider, within the bound.
No kernel may reach another device: no remote copies, remote signals or barrier semaphores. Data moves between devices by JAX's collectives and lax.ppermute only.
A program may use at most 64 MiB of HBM per device.

```python
import math
import jax
import jax.numpy as jnp
import numpy as np
from jax import lax

D = 1024
BLOCK = 128
TOP = 16
NPOS = 4
INST_DEV = 128
INSTANCES = 4096
CLUSTERS = 64
LABELS = 8192
MOST = 40
PAIRS_CL = 1024
N_SEQ = 4
N_CLUS = 8


def set_ends(values, rng, smallest, top_value):
    shape = values.shape
    index_at = [jax.random.randint(jax.random.fold_in(rng, axis), (), 0, shape[axis]) for axis in range(len(shape))]
    values = values.at[tuple(index_at)].set(smallest)
    longest = shape.index(max(shape))
    index_at[longest] = (index_at[longest] + 1) % shape[longest]
    return values.at[tuple(index_at)].set(top_value)


def steps_of(own_key, extent, split, least, top_value):
    loudness, own = 1.0, jax.random.fold_in(own_key, 6)
    for axis_at, shards_of in split:
        steps = jnp.exp(jax.random.uniform(jax.random.fold_in(own, axis_at), (shards_of,), jnp.float32, least / len(split), top_value / len(split)))
        loudness = loudness * jnp.repeat(steps, extent[axis_at] // shards_of).reshape([-1 if axis == axis_at else 1 for axis in range(len(extent))])
    return loudness


def split_up(amount, total, limit, slope):
    portions = [(1 << 20) // math.isqrt(standing ** slope) + 1 for standing in range(2, amount + 1)]
    surplus, given = total - limit - (amount - 1), [1] * (amount - 1)
    while surplus > 0:
        movable = [i for i in range(amount - 1) if given[i] < limit]
        pool, budget = sum([portions[i] for i in movable]), surplus
        for i in movable:
            extra = min(limit - given[i], max(1, budget * portions[i] // pool), surplus)
            given[i] = given[i] + extra
            surplus = surplus - extra
    return np.array([limit] + given)


def ragged(key, amount, total, bound, lean):
    if amount == 2:
        one = jax.random.randint(key, (), max(1, total - bound), min(bound, total - 1) + 1)
        return jnp.stack([one, total - one])
    tallies = jnp.asarray(split_up(amount, total, bound, lean), jnp.int32)
    twos = (amount - 1) // 2
    giver, taker = tallies[1:1 + 2 * twos:2], tallies[2:2 + 2 * twos:2]
    margin = jnp.minimum(giver - 1, bound - taker)
    moved = jax.random.randint(jax.random.fold_in(key, 1), (twos,), 0, 1 << 20) % (margin + 1)
    tallies = tallies.at[1:1 + 2 * twos:2].set(giver - moved).at[2:2 + 2 * twos:2].set(taker + moved)
    return tallies[jax.random.permutation(jax.random.fold_in(key, 2), amount)]


def assign_block(rng, own, number, rows, amount, top, reach, slope):
    order = jax.random.permutation(rng, amount)
    heavy_load, usual = shares(amount, rows * top, reach, slope, True), shares(amount, rows * top, reach, slope, False)
    places = jnp.arange(amount)

    def named(tallies, rotation):
        used = int((tallies > 0).sum())
        fixed = max(1, used // 4)
        shifted = fixed + (places - fixed + rotation * (used - fixed)) % max(1, amount - fixed)
        return jnp.zeros((amount,), jnp.int32).at[order[jnp.where(places < fixed, places, shifted)]].set(jnp.asarray(tallies, jnp.int32))

    tallies = jnp.where(number % 4 == 0, named(heavy_load, number // 4), named(usual, number - number // 4 - 1))
    mixed = jax.random.permutation(jax.random.fold_in(own, 3), amount)
    giver, taker = mixed[0:amount // 2 * 2:2], mixed[1:amount // 2 * 2:2]
    margin = jnp.minimum(tallies[giver] - 1, reach - tallies[taker]) // 2
    margin = jnp.where((giver == order[0]) | (taker == order[0]) | (tallies[taker] == 0), 0, jnp.maximum(margin, 0))
    shifted = jax.random.randint(jax.random.fold_in(own, 4), (amount // 2,), 0, 1 << 20) % (margin + 1)
    tallies = tallies.at[giver].add(-shifted).at[taker].add(shifted)
    members = jnp.searchsorted(jnp.cumsum(tallies), jnp.arange(rows * top), side="right").astype(jnp.int32)
    table = members.reshape(top, rows).T
    table = table[jax.random.permutation(jax.random.fold_in(own, 1), rows)]
    rotation = jax.random.randint(jax.random.fold_in(own, 2), (rows, 1), 0, top)
    return jnp.take_along_axis(table, (jnp.arange(top)[None, :] + rotation) % top, axis=1)


def shares(amount, total, bound, slope, full):
    loads = [(1 << 20) // math.isqrt(rank ** slope) + 1 for rank in range(1, amount + 1)]
    largest = bound if full else min(bound, max(-(-total // amount), total * loads[0] // sum(loads)))
    least = 1 if total - largest >= amount - 1 else 0
    counts, rest = [largest] + [least] * (amount - 1), total - largest - least * (amount - 1)
    while rest > 0:
        free = [i for i in range(1, amount) if counts[i] < largest] or [i for i in range(1, amount) if counts[i] < bound]
        mass, left = sum([loads[i] for i in free]), rest
        for i in free:
            addition = min(bound - counts[i], max(1, left * loads[i] // mass), rest)
            counts[i] = counts[i] + addition
            rest = rest - addition
    return np.array(counts)


def normal_values(rng, shape, width, limit, pieces=(), kind=jnp.bfloat16):
    factor_of = steps_of(rng, shape, pieces, -0.22, 0.18) if pieces else 1.0
    values = jax.random.normal(rng, shape, jnp.float32) * width * factor_of
    return jnp.minimum(jnp.maximum(values, -limit), limit).astype(kind)


def setup_inputs(seed: int = 0) -> dict:
    keys = jax.random.split(jax.random.key(seed), 6)
    features = normal_values(keys[0], (INSTANCES, D), 1.0, 6.0, ((0, 32),))
    shortlist_keys = jax.random.split(jax.random.fold_in(keys[1], 1), INSTANCES // INST_DEV)
    shortlist_turns = jax.random.permutation(jax.random.fold_in(keys[1], 3), INSTANCES // INST_DEV)
    shortlist = jax.vmap(lambda own, number: assign_block(jax.random.fold_in(keys[1], 2), own, number, INST_DEV, CLUSTERS, TOP, MOST, 2))(shortlist_keys, shortlist_turns).reshape((INSTANCES, TOP))
    positives = set_ends(jax.random.randint(keys[2], (INSTANCES, NPOS), 0, TOP * BLOCK), jax.random.fold_in(keys[2], 1), 0, (TOP * BLOCK) - 1).astype(jnp.int32)
    cluster_sizes = ragged(keys[3], CLUSTERS, CLUSTERS * 96, BLOCK, 1).astype(jnp.int32)
    weights = normal_values(keys[4], (LABELS, D), D ** -0.5, 0.1875, ((0, 8),))
    return dict(features=features, shortlist=shortlist, positives=positives, cluster_sizes=cluster_sizes, weights=weights)


def reference(features, shortlist, positives, cluster_sizes, weights):
    group_rows = INST_DEV * N_CLUS
    slot_count = N_CLUS * MOST
    cluster_ids = jnp.arange(CLUSTERS, dtype=jnp.int32)
    label_ids = jnp.arange(BLOCK, dtype=jnp.int32)

    def ranks_of(short_block):
        member = lax.optimization_barrier(jnp.sum((short_block[:, :, None] == cluster_ids[None, None, :]).astype(jnp.int32), axis=1))
        ranking = jnp.cumsum(member, axis=0) - member
        return jnp.take_along_axis(ranking, short_block, axis=1)
    pair_rank = lax.map(ranks_of, shortlist.reshape(-1, INST_DEV, TOP)).reshape(INSTANCES, TOP)
    within = jnp.arange(INSTANCES, dtype=jnp.int32) // INST_DEV % N_CLUS
    slot_table = within[:, None] * MOST + pair_rank
    weight_table = weights.reshape(CLUSTERS, BLOCK, D)
    norm_scale = 1.0 / math.sqrt(PAIRS_CL)

    def per_group(running, group_index):
        start = (group_index * group_rows).astype(jnp.int32)
        feat_group = lax.dynamic_slice_in_dim(features, start, group_rows, 0)
        short_group = lax.dynamic_slice_in_dim(shortlist, start, group_rows, 0)
        pos_group = lax.dynamic_slice_in_dim(positives, start, group_rows, 0)
        slot_group = lax.dynamic_slice_in_dim(slot_table, start, group_rows, 0)
        local_index = jnp.broadcast_to(jnp.arange(group_rows, dtype=jnp.int32)[:, None], (group_rows, TOP))
        short_place = jnp.broadcast_to(jnp.arange(TOP, dtype=jnp.int32)[None, :], (group_rows, TOP))
        slot_owner = jnp.zeros((CLUSTERS, slot_count), jnp.int32).at[short_group, slot_group].set(local_index)
        slot_place = jnp.zeros((CLUSTERS, slot_count), jnp.int32).at[short_group, slot_group].set(short_place)
        slot_filled = jnp.zeros((CLUSTERS, slot_count), jnp.int32).at[short_group, slot_group].set(1)

        def per_cluster(cluster):
            owner_row = slot_owner[cluster]
            filled = slot_filled[cluster]
            tile_rows = feat_group[owner_row] * filled[:, None].astype(jnp.bfloat16)
            pos_rows = pos_group[owner_row]
            matches = (pos_rows // BLOCK == slot_place[cluster][:, None]) & (filled[:, None] > 0)
            targets = jnp.where(matches, pos_rows % BLOCK, -1)
            block_weights = weight_table[cluster]
            logits = jnp.dot(tile_rows, block_weights.T, preferred_element_type=jnp.float32)
            positive = jnp.any(targets[:, :, None] == label_ids[None, None, :], axis=1)
            target_sign = jnp.where(positive, 1.0, -1.0)
            live_entry = (label_ids[None, :] < cluster_sizes[cluster]) & (filled[:, None] > 0)
            hinge_slope = jnp.where(live_entry, -2.0 * target_sign * jnp.maximum(1.0 - target_sign * logits, 0.0), 0.0).astype(jnp.bfloat16)
            pair_grads = jnp.dot(hinge_slope, block_weights, preferred_element_type=jnp.float32).astype(jnp.bfloat16)
            label_part = jnp.dot(hinge_slope.T, tile_rows, preferred_element_type=jnp.float32).astype(jnp.bfloat16)
            return (pair_grads, label_part)
        pair_grads, label_part = lax.map(per_cluster, cluster_ids)
        picked = pair_grads[short_group, slot_group]
        feature_rows = lax.optimization_barrier(jnp.sum(picked.astype(jnp.float32), axis=1)).astype(jnp.bfloat16)
        label_part = lax.optimization_barrier(label_part)
        running = running + label_part.reshape(LABELS, D).astype(jnp.float32)
        return (running, feature_rows)
    running, feature_blocks = lax.scan(per_group, jnp.zeros((LABELS, D), jnp.float32), jnp.arange(N_SEQ, dtype=jnp.int32))
    weight_grad = (running * norm_scale).astype(jnp.bfloat16)
    return (feature_blocks.reshape(INSTANCES, D), weight_grad)
```

```python
import functools
import math

import jax
import jax.numpy as jnp
from jax import lax
from jax.experimental import pallas as pl
from jax.experimental.pallas import tpu as pltpu
from jax.sharding import PartitionSpec as P

BLOCK = 128
LANES = 128
CHUNK = 256
VMEM_LIMIT = 40 * 1024 * 1024


def pack_kernel(all_clusters, feat_ref, short_ref, pos_ref, out_ref):
    rows, width = feat_ref.shape
    top_count, pos_count = short_ref.shape[1], pos_ref.shape[1]
    meta_width = out_ref.shape[1] - width
    out_ref[:, :width] = feat_ref[...]
    short = short_ref[...]
    places = pos_ref[...] // BLOCK
    offsets = pos_ref[...] % BLOCK
    targets = jnp.zeros_like(places)
    for j in range(top_count):
        targets = targets + jnp.where(places == j, short[:, j : j + 1], 0)
    column = lax.broadcasted_iota(jnp.int32, (rows, meta_width), 1)
    meta = jnp.zeros((rows, meta_width), jnp.int32)
    for j in range(top_count):
        meta = jnp.where(column == short[:, j : j + 1], 1, meta)
    for q in range(pos_count):
        meta = jnp.where(column == all_clusters + q, targets[:, q : q + 1], meta)
        meta = jnp.where(column == all_clusters + pos_count + q, offsets[:, q : q + 1], meta)
    out_ref[:, width:] = meta.astype(jnp.float32).astype(jnp.bfloat16)


def pack(features, shortlist, positives, all_clusters):
    rows, width = features.shape
    meta_width = -(-(all_clusters + 2 * positives.shape[1]) // LANES) * LANES
    return pl.pallas_call(
        functools.partial(pack_kernel, all_clusters),
        out_shape=jax.ShapeDtypeStruct((rows, width + meta_width), jnp.bfloat16),
        compiler_params=pltpu.CompilerParams(vmem_limit_bytes=VMEM_LIMIT),
        name="pack",
    )(features, shortlist, positives)


def block_kernel(block_count, all_clusters, pos_count, first_ref, *refs):
    x_refs = refs[:block_count]
    w_ref, live_ref = refs[block_count : block_count + 2]
    grad_refs = refs[block_count + 2 : 2 * block_count + 2]
    slope_refs = refs[2 * block_count + 2 :]
    labels, width = w_ref.shape
    rows = [ref.shape[0] for ref in x_refs]
    starts = [sum(rows[:k]) for k in range(block_count)]

    def joined(values):
        return values[0] if block_count == 1 else jnp.concatenate(values, axis=0)

    x = joined([ref[:, :width] for ref in x_refs])
    meta = joined([ref[:, width:] for ref in x_refs])
    numbers = meta.astype(jnp.float32)
    first = first_ref[0].astype(jnp.float32)
    target = [
        (numbers[:, all_clusters + q : all_clusters + q + 1] - first) * BLOCK
        + numbers[:, all_clusters + pos_count + q : all_clusters + pos_count + q + 1]
        for q in range(pos_count)
    ]
    total = None
    for start in range(0, labels, CHUNK):
        w_part = w_ref[start : start + CHUNK, :]
        logits = lax.dot_general(
            x, w_part, (((1,), (1,)), ((), ())), preferred_element_type=jnp.float32
        )
        live = jnp.dot(
            meta, live_ref[:, start : start + CHUNK], preferred_element_type=jnp.float32
        )
        label = (
            lax.broadcasted_iota(jnp.int32, (1, CHUNK), 1) + start
        ).astype(jnp.float32)
        positive = target[0] == label
        for q in range(1, pos_count):
            positive = positive | (target[q] == label)
        turned = jnp.where(positive, -1.0, 1.0)
        slope = (turned * live * jnp.maximum(1.0 + turned * logits, 0.0)).astype(jnp.bfloat16)
        for ref, at, count in zip(slope_refs, starts, rows):
            ref[:, start : start + CHUNK] = slope[at : at + count]
        part = jnp.dot(slope, w_part, preferred_element_type=jnp.float32)
        total = part if total is None else total + part
    for ref, at, count in zip(grad_refs, starts, rows):
        ref[...] = total[at : at + count].astype(jnp.bfloat16)


def block_work(blocks, weights, live_table, first, all_clusters, pos_count):
    labels, width = weights.shape
    count = len(blocks)
    rows = [block.shape[0] for block in blocks]
    out = pl.pallas_call(
        functools.partial(block_kernel, count, all_clusters, pos_count),
        out_shape=[jax.ShapeDtypeStruct((r, width), jnp.bfloat16) for r in rows]
        + [jax.ShapeDtypeStruct((r, labels), jnp.bfloat16) for r in rows],
        in_specs=[pl.BlockSpec(memory_space=pltpu.SMEM)]
        + [pl.BlockSpec(memory_space=pltpu.VMEM)] * (count + 2),
        compiler_params=pltpu.CompilerParams(vmem_limit_bytes=VMEM_LIMIT),
        cost_estimate=pl.CostEstimate(
            flops=4 * sum(rows) * labels * width,
            bytes_accessed=2 * labels * width + 6 * sum(rows) * width,
            transcendentals=0,
        ),
        name="block_work",
    )(first, *blocks, weights, live_table)
    return out[:count], out[count:]


def weight_kernel(block_count, column_blocks, scale, own_ref, *refs):
    x_refs = refs[:block_count]
    s_refs = refs[block_count : 2 * block_count]
    out_refs = refs[2 * block_count :]
    labels, part_width = out_refs[0].shape
    slopes = jnp.concatenate([ref[...] for ref in s_refs], axis=0)
    for ref, q in zip(out_refs, column_blocks):
        at = pl.multiple_of((own_ref[0] ^ q) * part_width, part_width)
        x = jnp.concatenate([r[:, pl.ds(at, part_width)] for r in x_refs], axis=0)
        part = lax.dot_general(
            slopes, x, (((0,), (0,)), ((), ())), preferred_element_type=jnp.float32
        )
        ref[...] = (part * scale).astype(jnp.bfloat16)


def weight_work(blocks, slopes, own, column_blocks, part_width, scale):
    count = len(blocks)
    labels = slopes[0].shape[1]
    rows = sum(block.shape[0] for block in blocks)
    return pl.pallas_call(
        functools.partial(weight_kernel, count, column_blocks, scale),
        out_shape=[jax.ShapeDtypeStruct((labels, part_width), jnp.bfloat16)] * len(column_blocks),
        in_specs=[pl.BlockSpec(memory_space=pltpu.SMEM)]
        + [pl.BlockSpec(memory_space=pltpu.VMEM)] * (2 * count),
        compiler_params=pltpu.CompilerParams(vmem_limit_bytes=VMEM_LIMIT),
        cost_estimate=pl.CostEstimate(
            flops=2 * rows * labels * part_width * len(column_blocks),
            bytes_accessed=2 * rows * (labels + 1024) + 2 * labels * part_width,
            transcendentals=0,
        ),
        name="weight_work",
    )(own, *blocks, *slopes)


def add(*parts):
    total = parts[0].astype(jnp.float32)
    for part in parts[1:]:
        total = total + part.astype(jnp.float32)
    return total.astype(jnp.bfloat16)


def local(features, shortlist, positives, cluster_sizes, weights):
    inst_rows, width = features.shape
    top_count, pos_count = shortlist.shape[1], positives.shape[1]
    clus_count, seq_count = lax.axis_size("clus"), lax.axis_size("seq")
    local_count = cluster_sizes.shape[0]
    all_clusters = local_count * clus_count
    part_width = width // seq_count
    labels = weights.shape[0]

    ring = list(range(0, clus_count, 2)) + list(range(1, clus_count, 2))[::-1]
    onward = [(ring[k], ring[(k + 1) % clus_count]) for k in range(clus_count)]
    back = [(b, a) for a, b in onward]

    def send(array, pairs):
        return lax.ppermute(array, "clus", pairs)

    packed = pack(features, shortlist, positives, all_clusters)
    first = lax.axis_index("clus") * local_count
    column = jnp.arange(labels, dtype=jnp.int32)
    size = jnp.repeat(cluster_sizes, BLOCK)
    named = jnp.arange(packed.shape[1] - width, dtype=jnp.int32)[:, None] == first + column // BLOCK
    live_table = jnp.where(named & (column % BLOCK < size), 2.0, 0.0).astype(jnp.bfloat16)
    first = first.astype(jnp.int32).reshape(1)

    def work(blocks):
        return block_work(blocks, weights, live_table, first, all_clusters, pos_count)

    half, steps = inst_rows // 2, clus_count // 2
    used, slopes = [packed], []
    parts = {}
    from_back, from_front = packed, packed
    for k in range(1, steps + 1):
        if k == steps:
            from_back, from_front = from_back[:half], from_front[half:]
        arriving = send(from_back, onward), send(from_front, back)
        if k == 1:
            (own_part,), own_slopes = work([packed])
            slopes += own_slopes
        else:
            parts[k - 1], new_slopes = work([from_back_held, from_front_held])
            slopes += new_slopes
        from_back, from_front = arriving
        from_back_held, from_front_held = arriving
        used += [from_back, from_front]
    parts[steps], new_slopes = work([from_back_held, from_front_held])
    slopes += new_slopes

    scale = 1.0 / math.sqrt(inst_rows * seq_count * top_count // local_count)
    own = lax.axis_index("seq").astype(jnp.int32).reshape(1)

    def seq_send(array, bit):
        return lax.ppermute(array, "seq", [(k, k ^ bit) for k in range(seq_count)])

    away = [q for q in range(seq_count) if q & 1]
    kept = [q for q in range(seq_count) if not q & 1]
    slots = dict(zip(away, weight_work(used, slopes, own, away, part_width, scale)))
    slots.update(zip(kept, weight_work(used, slopes, own, kept, part_width, scale)))
    bit = 1
    while bit < seq_count:
        going = [q for q in sorted(slots) if q & bit]
        for q in going:
            slots[q ^ bit] = add(slots[q ^ bit], seq_send(slots.pop(q), bit))
        bit *= 2
    weight_grad = slots[0]

    to_back, to_front = parts[steps]
    for k in range(steps, 0, -1):
        got_back, got_front = send(to_front, onward), send(to_back, back)
        if k == steps:
            near_back, near_front = parts[k - 1] if k > 1 else (own_part, None)
            if k > 1:
                to_back = jnp.concatenate([add(near_back[:half], got_front), near_back[half:]], axis=0)
                to_front = jnp.concatenate([near_front[:half], add(near_front[half:], got_back)], axis=0)
        elif k > 1:
            near_back, near_front = parts[k - 1]
            to_back, to_front = add(near_back, got_front), add(near_front, got_back)
    feature_grad = add(own_part, got_back, got_front)
    return (feature_grad, weight_grad)


def solution(mesh):
    return jax.shard_map(
        local,
        mesh=mesh,
        in_specs=(
            P(("seq", "clus"), None),
            P(("seq", "clus"), None),
            P(("seq", "clus"), None),
            P("clus"),
            P("clus", None),
        ),
        out_specs=(P(("seq", "clus"), None), P("clus", "seq")),
        check_vma=False,
    )
```

```python
import functools
import math

import jax
import jax.numpy as jnp
from jax import lax
from jax.experimental import pallas as pl
from jax.experimental.pallas import tpu as pltpu
from jax.sharding import PartitionSpec as P

BLOCK = 128
LANES = 128
FIELD_ROWS = 8
CHUNK = 256
VMEM_LIMIT = 24 * 1024 * 1024
WHOLE_VMEM = 60 * 1024 * 1024


def pack_kernel(feat_ref, short_ref, pos_ref, a_ref, b_ref, sem_a, sem_b):
    half, width = b_ref.shape
    copy_a = pltpu.make_async_copy(feat_ref.at[pl.ds(0, half)], a_ref.at[pl.ds(0, half)], sem_a)
    copy_b = pltpu.make_async_copy(feat_ref.at[pl.ds(half, half)], b_ref, sem_b)
    copy_a.start()
    copy_b.start()
    top_count, rows = short_ref.shape
    short = short_ref[...]
    places = pos_ref[...] // BLOCK
    offsets = pos_ref[...] % BLOCK
    targets = jnp.zeros_like(places)
    for j in range(top_count):
        targets = targets + jnp.where(places == j, short[j : j + 1, :], 0)
    fields = jnp.concatenate([short, targets, offsets], axis=0)
    groups = [
        fields[at : at + FIELD_ROWS] for at in range(0, fields.shape[0], FIELD_ROWS)
    ]
    groups.append(jnp.zeros((FIELD_ROWS, width - rows * len(groups)), jnp.int32))
    meta = jnp.concatenate(groups, axis=1)
    a_ref[half:, :] = meta.astype(jnp.float32).astype(jnp.bfloat16)
    copy_a.wait()
    copy_b.wait()


def pack(features, shortlist, positives):
    rows, width = features.shape
    half = rows // 2
    return pl.pallas_call(
        pack_kernel,
        out_shape=[
            jax.ShapeDtypeStruct((half + FIELD_ROWS, width), jnp.bfloat16),
            jax.ShapeDtypeStruct((half, width), jnp.bfloat16),
        ],
        in_specs=[
            pl.BlockSpec(memory_space=pltpu.HBM),
            pl.BlockSpec(memory_space=pltpu.VMEM),
            pl.BlockSpec(memory_space=pltpu.VMEM),
        ],
        out_specs=[pl.BlockSpec(memory_space=pltpu.VMEM)] * 2,
        scratch_shapes=[pltpu.SemaphoreType.DMA, pltpu.SemaphoreType.DMA],
        compiler_params=pltpu.CompilerParams(vmem_limit_bytes=WHOLE_VMEM),
        name="pack",
    )(features, shortlist.T, positives.T)


def block_kernel(block_count, top_count, pos_count, first_ref, size_ref, *refs):
    x_refs = refs[: 2 * block_count]
    w_ref = refs[2 * block_count]
    grad_refs = refs[2 * block_count + 1 : 4 * block_count + 1]
    slope_refs = refs[4 * block_count + 1 :]
    labels, width = w_ref.shape
    local_count = labels // BLOCK
    half = grad_refs[0].shape[0]
    rows = 2 * half
    first = first_ref[0].astype(jnp.float32)

    lane = lax.broadcasted_iota(jnp.int32, (LANES, BLOCK), 1)
    row = lax.broadcasted_iota(jnp.int32, (LANES, BLOCK), 0)
    live_table = jnp.concatenate(
        [
            jnp.where((row == c) & (lane < size_ref[c]), 2.0, 0.0).astype(jnp.bfloat16)
            for c in range(local_count)
        ],
        axis=1,
    )

    named, pieces = [], []
    cluster = lax.broadcasted_iota(jnp.int32, (FIELD_ROWS, rows), 0).astype(jnp.float32) + first
    for b in range(block_count):
        a_ref, b_ref = x_refs[2 * b], x_refs[2 * b + 1]
        pieces += [a_ref[:half, :], b_ref[...]]
        groups = -(-(top_count + 2 * pos_count) // FIELD_ROWS)
        meta = a_ref[half:, : groups * rows].astype(jnp.float32)
        field = [
            meta[f % FIELD_ROWS : f % FIELD_ROWS + 1, f // FIELD_ROWS * rows : (f // FIELD_ROWS + 1) * rows]
            for f in range(top_count + 2 * pos_count)
        ]
        member = jnp.zeros((FIELD_ROWS, rows), jnp.float32)
        for j in range(top_count):
            member = jnp.where(cluster == field[j], 1.0, member)
        target = [
            (field[top_count + q] - first) * BLOCK + field[top_count + pos_count + q]
            for q in range(pos_count)
        ]
        rest = jnp.zeros((LANES - FIELD_ROWS - pos_count, rows), jnp.float32)
        named.append(jnp.concatenate([member] + target + [rest], axis=0).T)

    x = jnp.concatenate(pieces, axis=0)
    named = jnp.concatenate(named, axis=0) if block_count > 1 else named[0]
    target = [named[:, FIELD_ROWS + q : FIELD_ROWS + q + 1] for q in range(pos_count)]
    member = jnp.where(
        lax.broadcasted_iota(jnp.int32, named.shape, 1) < FIELD_ROWS, named, 0.0
    ).astype(jnp.bfloat16)
    for start in range(0, labels, CHUNK):
        logits = lax.dot_general(
            x,
            w_ref[start : start + CHUNK, :],
            (((1,), (1,)), ((), ())),
            preferred_element_type=jnp.float32,
        )
        live = jnp.dot(
            member, live_table[:, start : start + CHUNK], preferred_element_type=jnp.float32
        )
        label = (
            lax.broadcasted_iota(jnp.int32, (1, CHUNK), 1) + start
        ).astype(jnp.float32)
        positive = target[0] == label
        for q in range(1, pos_count):
            positive = positive | (target[q] == label)
        turned = jnp.where(positive, -1.0, 1.0)
        slope = (turned * live * jnp.maximum(1.0 + turned * logits, 0.0)).astype(jnp.bfloat16)
        for b, ref in enumerate(slope_refs):
            ref[:, start : start + CHUNK] = slope[b * rows : (b + 1) * rows]
    slope = jnp.concatenate([ref[...] for ref in slope_refs], axis=0)
    for start in range(0, width, CHUNK):
        part = jnp.dot(
            slope, w_ref[:, start : start + CHUNK], preferred_element_type=jnp.float32
        ).astype(jnp.bfloat16)
        for p, ref in enumerate(grad_refs):
            ref[:, start : start + CHUNK] = part[p * half : (p + 1) * half]


def block_work(blocks, weights, first, sizes, top_count, pos_count):
    labels, width = weights.shape
    count = len(blocks)
    half = blocks[0][1].shape[0]
    out = pl.pallas_call(
        functools.partial(block_kernel, count, top_count, pos_count),
        out_shape=[jax.ShapeDtypeStruct((half, width), jnp.bfloat16)] * (2 * count)
        + [jax.ShapeDtypeStruct((2 * half, labels), jnp.bfloat16)] * count,
        in_specs=[pl.BlockSpec(memory_space=pltpu.SMEM)] * 2
        + [pl.BlockSpec(memory_space=pltpu.VMEM)] * (2 * count + 1),
        compiler_params=pltpu.CompilerParams(vmem_limit_bytes=VMEM_LIMIT),
        cost_estimate=pl.CostEstimate(
            flops=8 * count * half * labels * width,
            bytes_accessed=2 * labels * width + 12 * count * half * width,
            transcendentals=0,
        ),
        name="block_work",
    )(first, sizes, *[piece for block in blocks for piece in block], weights)
    grads = [(out[2 * b], out[2 * b + 1]) for b in range(count)]
    return grads, list(out[2 * count :])


def weight_kernel(block_count, column_blocks, scale, own_ref, *refs):
    x_refs = refs[: 2 * block_count]
    s_refs = refs[2 * block_count : 3 * block_count]
    out_refs = refs[3 * block_count :]
    part_width = out_refs[0].shape[1]
    half = x_refs[1].shape[0]
    slopes = jnp.concatenate([ref[...] for ref in s_refs], axis=0)
    for ref, q in zip(out_refs, column_blocks):
        at = pl.multiple_of((own_ref[0] ^ q) * part_width, part_width)
        x = jnp.concatenate([r[:half, pl.ds(at, part_width)] for r in x_refs], axis=0)
        part = lax.dot_general(
            slopes, x, (((0,), (0,)), ((), ())), preferred_element_type=jnp.float32
        )
        ref[...] = (part * scale).astype(jnp.bfloat16)


def weight_work(blocks, slopes, own, column_blocks, part_width, scale):
    count = len(blocks)
    rows, labels = slopes[0].shape
    rows *= count
    return pl.pallas_call(
        functools.partial(weight_kernel, count, column_blocks, scale),
        out_shape=[jax.ShapeDtypeStruct((labels, part_width), jnp.bfloat16)] * len(column_blocks),
        in_specs=[pl.BlockSpec(memory_space=pltpu.SMEM)]
        + [pl.BlockSpec(memory_space=pltpu.VMEM)] * (3 * count),
        compiler_params=pltpu.CompilerParams(vmem_limit_bytes=VMEM_LIMIT),
        cost_estimate=pl.CostEstimate(
            flops=2 * rows * labels * part_width * len(column_blocks),
            bytes_accessed=2 * rows * (labels + 1024) + 2 * labels * part_width,
            transcendentals=0,
        ),
        name="weight_work",
    )(own, *[piece for block in blocks for piece in block], *slopes)


def add(*parts):
    total = parts[0].astype(jnp.float32)
    for part in parts[1:]:
        total = total + part.astype(jnp.float32)
    return total.astype(jnp.bfloat16)


def behind(array, other):
    return lax.optimization_barrier((array, other))[0]


def local(features, shortlist, positives, cluster_sizes, weights):
    inst_rows, width = features.shape
    top_count, pos_count = shortlist.shape[1], positives.shape[1]
    clus_count, seq_count = lax.axis_size("clus"), lax.axis_size("seq")
    local_count = cluster_sizes.shape[0]
    part_width = width // seq_count
    steps = clus_count // 2

    ring = list(range(0, clus_count, 2)) + list(range(1, clus_count, 2))[::-1]
    up = [(ring[k], ring[(k + 1) % clus_count]) for k in range(clus_count)]
    down = [(b, a) for a, b in up]

    def send_up(array):
        return lax.ppermute(array, "clus", up)

    def send_down(array):
        return lax.ppermute(array, "clus", down)

    first = (lax.axis_index("clus") * local_count).astype(jnp.int32).reshape(1)

    def work(blocks):
        return block_work(blocks, weights, first, cluster_sizes, top_count, pos_count)

    own = tuple(pack(features, shortlist, positives))
    below, above = {0: own}, {0: own}
    below_grad, above_grad = {}, {}
    used, slopes = [], []

    def take(blocks):
        grads, found = work(blocks)
        used.extend(blocks)
        slopes.extend(found)
        return grads

    for k in range(1, steps + 1):
        here_below, here_above = below[k - 1], above[k - 1]
        if k > 2:
            here_below = [behind(piece, below_grad[k - 2][0]) for piece in here_below]
            here_above = [behind(piece, below_grad[k - 2][0]) for piece in here_above]
        a_up = send_up(here_below[0])
        b_down = send_down(here_above[1])
        if k < steps:
            b_up = send_up(here_below[1])
            a_down = send_down(here_above[0])
            below[k], above[k] = (a_up, b_up), (a_down, b_down)
        else:
            opposite = (a_up, b_down)
        if k > 1:
            below_grad[k - 1], above_grad[k - 1] = take([below[k - 1], above[k - 1]])

    last = steps - 1
    b_going_down, a_going_up = below_grad[last][1], above_grad[last][0]
    b_from_above, a_from_below = send_down(b_going_down), send_up(a_going_up)
    (far_grad, own_grad) = take([opposite, own])
    a_from_above, b_from_below = send_down(far_grad[0]), send_up(far_grad[1])
    for k in range(last, 0, -1):
        a_down, b_up = add(below_grad[k][0], a_from_above), add(above_grad[k][1], b_from_below)
        if k > 1:
            b_down = add(below_grad[k - 1][1], behind(b_from_above, far_grad[0]))
            a_up = add(above_grad[k - 1][0], behind(a_from_below, far_grad[0]))
            b_from_above, a_from_below = send_down(b_down), send_up(a_up)
        a_from_above, b_from_below = send_down(a_down), send_up(b_up)

    scale = 1.0 / math.sqrt(inst_rows * seq_count * top_count // local_count)
    own_seq = lax.axis_index("seq").astype(jnp.int32).reshape(1)

    def seq_send(array, bit):
        return lax.ppermute(array, "seq", [(k, k ^ bit) for k in range(seq_count)])

    away = [q for q in range(seq_count) if q & 1]
    kept = [q for q in range(seq_count) if not q & 1]
    slots = dict(zip(away, weight_work(used, slopes, own_seq, away, part_width, scale)))
    slots.update(zip(kept, weight_work(used, slopes, own_seq, kept, part_width, scale)))
    bit = 1
    while bit < seq_count:
        for q in [q for q in sorted(slots, reverse=True) if q & bit]:
            slots[q ^ bit] = add(slots[q ^ bit], seq_send(slots.pop(q), bit))
        bit *= 2
    weight_grad = slots[0]

    feature_grad = jnp.concatenate(
        [
            add(behind(own_grad[0], weight_grad), a_from_above, a_from_below),
            add(behind(own_grad[1], weight_grad), b_from_above, b_from_below),
        ],
        axis=0,
    )
    return (feature_grad, weight_grad)


def solution(mesh):
    return jax.shard_map(
        local,
        mesh=mesh,
        in_specs=(
            P(("seq", "clus"), None),
            P(("seq", "clus"), None),
            P(("seq", "clus"), None),
            P("clus"),
            P("clus", None),
        ),
        out_specs=(P(("seq", "clus"), None), P("clus", "seq")),
        check_vma=False,
    )
```

```python
import functools
import math

import jax
import jax.numpy as jnp
from jax import lax
from jax.experimental import pallas as pl
from jax.experimental.pallas import tpu as pltpu
from jax.sharding import PartitionSpec as P

BLOCK = 128
LANES = 128
FIELD_ROWS = 8
CHUNK = 256
VMEM_LIMIT = 24 * 1024 * 1024


def pack_kernel(feat_ref, short_ref, pos_ref, a_ref, b_ref):
    half, width = b_ref.shape
    a_ref[:half, :] = feat_ref[:half, :]
    b_ref[...] = feat_ref[half:, :]
    top_count, rows = short_ref.shape
    short = short_ref[...]
    places = pos_ref[...] // BLOCK
    offsets = pos_ref[...] % BLOCK
    targets = jnp.zeros_like(places)
    for j in range(top_count):
        targets = targets + jnp.where(places == j, short[j : j + 1, :], 0)
    fields = jnp.concatenate([short, targets, offsets], axis=0)
    groups = [
        fields[at : at + FIELD_ROWS] for at in range(0, fields.shape[0], FIELD_ROWS)
    ]
    groups.append(jnp.zeros((FIELD_ROWS, width - rows * len(groups)), jnp.int32))
    meta = jnp.concatenate(groups, axis=1)
    a_ref[half:, :] = meta.astype(jnp.float32).astype(jnp.bfloat16)


def pack(features, shortlist, positives):
    rows, width = features.shape
    half = rows // 2
    return pl.pallas_call(
        pack_kernel,
        out_shape=[
            jax.ShapeDtypeStruct((half + FIELD_ROWS, width), jnp.bfloat16),
            jax.ShapeDtypeStruct((half, width), jnp.bfloat16),
        ],
        in_specs=[pl.BlockSpec(memory_space=pltpu.VMEM)] * 3,
        out_specs=[pl.BlockSpec(memory_space=pltpu.VMEM)] * 2,
        compiler_params=pltpu.CompilerParams(vmem_limit_bytes=VMEM_LIMIT),
        name="pack",
    )(features, shortlist.T, positives.T)


def block_kernel(block_count, top_count, pos_count, first_ref, size_ref, *refs):
    x_refs = refs[: 2 * block_count]
    w_ref = refs[2 * block_count]
    grad_refs = refs[2 * block_count + 1 : 4 * block_count + 1]
    slope_refs = refs[4 * block_count + 1 :]
    labels, width = w_ref.shape
    local_count = labels // BLOCK
    half = grad_refs[0].shape[0]
    rows = 2 * half
    first = first_ref[0].astype(jnp.float32)

    lane = lax.broadcasted_iota(jnp.int32, (LANES, BLOCK), 1)
    row = lax.broadcasted_iota(jnp.int32, (LANES, BLOCK), 0)
    live_table = jnp.concatenate(
        [
            jnp.where((row == c) & (lane < size_ref[c]), 2.0, 0.0).astype(jnp.bfloat16)
            for c in range(local_count)
        ],
        axis=1,
    )

    named, pieces = [], []
    cluster = lax.broadcasted_iota(jnp.int32, (FIELD_ROWS, rows), 0).astype(jnp.float32) + first
    for b in range(block_count):
        a_ref, b_ref = x_refs[2 * b], x_refs[2 * b + 1]
        pieces += [a_ref[:half, :], b_ref[...]]
        groups = -(-(top_count + 2 * pos_count) // FIELD_ROWS)
        meta = a_ref[half:, : groups * rows].astype(jnp.float32)
        field = [
            meta[f % FIELD_ROWS : f % FIELD_ROWS + 1, f // FIELD_ROWS * rows : (f // FIELD_ROWS + 1) * rows]
            for f in range(top_count + 2 * pos_count)
        ]
        member = jnp.zeros((FIELD_ROWS, rows), jnp.float32)
        for j in range(top_count):
            member = jnp.where(cluster == field[j], 1.0, member)
        target = [
            (field[top_count + q] - first) * BLOCK + field[top_count + pos_count + q]
            for q in range(pos_count)
        ]
        rest = jnp.zeros((LANES - FIELD_ROWS - pos_count, rows), jnp.float32)
        named.append(jnp.concatenate([member] + target + [rest], axis=0).T)

    x = jnp.concatenate(pieces, axis=0)
    named = jnp.concatenate(named, axis=0) if block_count > 1 else named[0]
    target = [named[:, FIELD_ROWS + q : FIELD_ROWS + q + 1] for q in range(pos_count)]
    member = jnp.where(
        lax.broadcasted_iota(jnp.int32, named.shape, 1) < FIELD_ROWS, named, 0.0
    ).astype(jnp.bfloat16)
    for start in range(0, labels, CHUNK):
        logits = lax.dot_general(
            x,
            w_ref[start : start + CHUNK, :],
            (((1,), (1,)), ((), ())),
            preferred_element_type=jnp.float32,
        )
        live = jnp.dot(
            member, live_table[:, start : start + CHUNK], preferred_element_type=jnp.float32
        )
        label = (
            lax.broadcasted_iota(jnp.int32, (1, CHUNK), 1) + start
        ).astype(jnp.float32)
        positive = target[0] == label
        for q in range(1, pos_count):
            positive = positive | (target[q] == label)
        turned = jnp.where(positive, -1.0, 1.0)
        slope = (turned * live * jnp.maximum(1.0 + turned * logits, 0.0)).astype(jnp.bfloat16)
        for b, ref in enumerate(slope_refs):
            ref[:, start : start + CHUNK] = slope[b * rows : (b + 1) * rows]
    slope = jnp.concatenate([ref[...] for ref in slope_refs], axis=0)
    for start in range(0, width, CHUNK):
        part = jnp.dot(
            slope, w_ref[:, start : start + CHUNK], preferred_element_type=jnp.float32
        ).astype(jnp.bfloat16)
        for p, ref in enumerate(grad_refs):
            ref[:, start : start + CHUNK] = part[p * half : (p + 1) * half]


def block_work(blocks, weights, first, sizes, top_count, pos_count):
    labels, width = weights.shape
    count = len(blocks)
    half = blocks[0][1].shape[0]
    out = pl.pallas_call(
        functools.partial(block_kernel, count, top_count, pos_count),
        out_shape=[jax.ShapeDtypeStruct((half, width), jnp.bfloat16)] * (2 * count)
        + [jax.ShapeDtypeStruct((2 * half, labels), jnp.bfloat16)] * count,
        in_specs=[pl.BlockSpec(memory_space=pltpu.SMEM)] * 2
        + [pl.BlockSpec(memory_space=pltpu.VMEM)] * (2 * count + 1),
        compiler_params=pltpu.CompilerParams(vmem_limit_bytes=VMEM_LIMIT),
        cost_estimate=pl.CostEstimate(
            flops=8 * count * half * labels * width,
            bytes_accessed=2 * labels * width + 12 * count * half * width,
            transcendentals=0,
        ),
        name="block_work",
    )(first, sizes, *[piece for block in blocks for piece in block], weights)
    grads = [(out[2 * b], out[2 * b + 1]) for b in range(count)]
    return grads, list(out[2 * count :])


def weight_kernel(block_count, column_blocks, scale, own_ref, *refs):
    x_refs = refs[: 2 * block_count]
    s_refs = refs[2 * block_count : 3 * block_count]
    out_refs = refs[3 * block_count :]
    part_width = out_refs[0].shape[1]
    half = x_refs[1].shape[0]
    slopes = jnp.concatenate([ref[...] for ref in s_refs], axis=0)
    for ref, q in zip(out_refs, column_blocks):
        at = pl.multiple_of((own_ref[0] ^ q) * part_width, part_width)
        x = jnp.concatenate([r[:half, pl.ds(at, part_width)] for r in x_refs], axis=0)
        part = lax.dot_general(
            slopes, x, (((0,), (0,)), ((), ())), preferred_element_type=jnp.float32
        )
        ref[...] = (part * scale).astype(jnp.bfloat16)


def weight_work(blocks, slopes, own, column_blocks, part_width, scale):
    count = len(blocks)
    rows, labels = slopes[0].shape
    rows *= count
    return pl.pallas_call(
        functools.partial(weight_kernel, count, column_blocks, scale),
        out_shape=[jax.ShapeDtypeStruct((labels, part_width), jnp.bfloat16)] * len(column_blocks),
        in_specs=[pl.BlockSpec(memory_space=pltpu.SMEM)]
        + [pl.BlockSpec(memory_space=pltpu.VMEM)] * (3 * count),
        compiler_params=pltpu.CompilerParams(vmem_limit_bytes=VMEM_LIMIT),
        cost_estimate=pl.CostEstimate(
            flops=2 * rows * labels * part_width * len(column_blocks),
            bytes_accessed=2 * rows * (labels + 1024) + 2 * labels * part_width,
            transcendentals=0,
        ),
        name="weight_work",
    )(own, *[piece for block in blocks for piece in block], *slopes)


def add(*parts):
    total = parts[0].astype(jnp.float32)
    for part in parts[1:]:
        total = total + part.astype(jnp.float32)
    return total.astype(jnp.bfloat16)


def behind(array, *others):
    return lax.optimization_barrier((array, *others))[0]


class Turn:
    def __init__(self):
        self.before = []

    def passed(self, array):
        self.before.append(array)

    def __call__(self, array):
        if self.before:
            array = behind(array, *self.before)
        self.before = [array]
        return array


def local(features, shortlist, positives, cluster_sizes, weights):
    inst_rows, width = features.shape
    top_count, pos_count = shortlist.shape[1], positives.shape[1]
    clus_count, seq_count = lax.axis_size("clus"), lax.axis_size("seq")
    local_count = cluster_sizes.shape[0]
    part_width = width // seq_count
    steps = clus_count // 2

    ring = list(range(0, clus_count, 2)) + list(range(1, clus_count, 2))[::-1]
    up = [(ring[k], ring[(k + 1) % clus_count]) for k in range(clus_count)]
    down = [(b, a) for a, b in up]

    def send_up(array):
        return lax.ppermute(array, "clus", up)

    def send_down(array):
        return lax.ppermute(array, "clus", down)

    first = (lax.axis_index("clus") * local_count).astype(jnp.int32).reshape(1)

    def work(blocks):
        return block_work(blocks, weights, first, cluster_sizes, top_count, pos_count)

    own = tuple(pack(features, shortlist, positives))
    below, above = {0: own}, {0: own}
    below_grad, above_grad = {}, {}
    used, slopes = [], []
    turn = Turn()

    def take(blocks):
        grads, found = work(blocks)
        used.extend(blocks)
        slopes.extend(found)
        return grads

    for k in range(1, steps + 1):
        here_below, here_above = below[k - 1], above[k - 1]
        if k > 2:
            here_below = [behind(piece, below_grad[k - 2][0]) for piece in here_below]
            here_above = [behind(piece, below_grad[k - 2][0]) for piece in here_above]
        a_up = send_up(here_below[0])
        b_down = send_down(here_above[1])
        if k < steps:
            b_up = send_up(here_below[1])
            a_down = send_down(here_above[0])
            below[k], above[k] = (a_up, b_up), (a_down, b_down)
        else:
            opposite = (a_up, b_down)
        if k > 1:
            below_grad[k - 1], above_grad[k - 1] = take([below[k - 1], above[k - 1]])

    last = steps - 1
    b_from_above = send_down(turn(below_grad[last][1]))
    a_from_below = send_up(turn(above_grad[last][0]))
    (far_grad, own_grad) = take([opposite, own])
    turn.passed(far_grad[0])
    a_from_above = send_down(turn(far_grad[0]))
    b_from_below = send_up(turn(far_grad[1]))
    b_from_above, a_from_below = behind(b_from_above, far_grad[0]), behind(a_from_below, far_grad[0])

    scale = 1.0 / math.sqrt(inst_rows * seq_count * top_count // local_count)
    own_seq = lax.axis_index("seq").astype(jnp.int32).reshape(1)

    def seq_send(array, bit):
        return lax.ppermute(array, "seq", [(k, k ^ bit) for k in range(seq_count)])

    terms = {}

    def weigh(slots):
        parts = weight_work(used, slopes, own_seq, slots, part_width, scale)
        turn.passed(parts[0])
        terms.update({q: [part] for q, part in zip(slots, parts)})

    def halve(bit, slots):
        for q in slots:
            values = terms.pop(q)
            going = turn(add(*values) if len(values) > 1 else values[0])
            terms[q ^ bit].append(seq_send(going, bit))

    near, far = list(range(seq_count // 2)), list(range(seq_count // 2, seq_count))

    def weigh_far():
        weigh(far)
        halve(1, far[1::2])

    def weigh_near():
        weigh(near)
        halve(1, near[1::2])
        bit = 2
        while bit < seq_count:
            halve(bit, [q for q in sorted(terms, reverse=True) if q & bit])
            bit *= 2

    for k in range(last, 0, -1):
        a_down, b_up = (below_grad[k][0], a_from_above), (above_grad[k][1], b_from_below)
        if k > 1:
            b_down, a_up = (below_grad[k - 1][1], b_from_above), (above_grad[k - 1][0], a_from_below)
            b_from_above = send_down(turn(add(*b_down)))
            a_from_below = send_up(turn(add(*a_up)))
        if k == last:
            weigh_far()
        a_from_above = send_down(turn(add(*a_down)))
        b_from_below = send_up(turn(add(*b_up)))
        if k == last:
            weigh_near()
    weight_grad = add(*terms[0])

    feature_grad = jnp.concatenate(
        [
            add(behind(own_grad[0], weight_grad), a_from_above, a_from_below),
            add(behind(own_grad[1], weight_grad), b_from_above, b_from_below),
        ],
        axis=0,
    )
    return (feature_grad, weight_grad)


def solution(mesh):
    return jax.shard_map(
        local,
        mesh=mesh,
        in_specs=(
            P(("seq", "clus"), None),
            P(("seq", "clus"), None),
            P(("seq", "clus"), None),
            P("clus"),
            P("clus", None),
        ),
        out_specs=(P(("seq", "clus"), None), P("clus", "seq")),
        check_vma=False,
    )
```

```python
import functools
import math

import jax
import jax.numpy as jnp
from jax import lax
from jax.experimental import pallas as pl
from jax.experimental.pallas import tpu as pltpu
from jax.sharding import PartitionSpec as P

BLOCK = 128
LANES = 128
FIELD_ROWS = 8
CHUNK = 256
VMEM_LIMIT = 40 * 1024 * 1024


def pack_kernel(feat_ref, short_ref, pos_ref, out_ref):
    rows, width = feat_ref.shape
    out_ref[:rows, :] = feat_ref[...]
    short = short_ref[...]
    places = pos_ref[...] // BLOCK
    offsets = pos_ref[...] % BLOCK
    targets = jnp.zeros_like(places)
    for j in range(short.shape[0]):
        targets = targets + jnp.where(places == j, short[j : j + 1, :], 0)
    fields = jnp.concatenate([short, targets, offsets], axis=0)
    groups = [
        fields[at : at + FIELD_ROWS] for at in range(0, fields.shape[0], FIELD_ROWS)
    ]
    groups.append(jnp.zeros((FIELD_ROWS, width - rows * len(groups)), jnp.int32))
    meta = jnp.concatenate(groups, axis=1)
    out_ref[rows:, :] = meta.astype(jnp.float32).astype(jnp.bfloat16)


def pack(features, shortlist, positives):
    rows, width = features.shape
    return pl.pallas_call(
        pack_kernel,
        out_shape=jax.ShapeDtypeStruct((rows + FIELD_ROWS, width), jnp.bfloat16),
        in_specs=[pl.BlockSpec(memory_space=pltpu.VMEM)] * 3,
        compiler_params=pltpu.CompilerParams(vmem_limit_bytes=VMEM_LIMIT),
        name="pack",
    )(features, shortlist.T, positives.T)


def block_kernel(piece_rows, top_count, pos_count, first_ref, size_ref, *refs):
    block_count = len(piece_rows)
    piece_count = sum(len(pieces) for pieces in piece_rows)
    x_refs = refs[:piece_count]
    w_ref = refs[piece_count]
    grad_refs = refs[piece_count + 1 : 2 * piece_count + 1]
    slope_refs = refs[2 * piece_count + 1 :]
    labels, width = w_ref.shape
    local_count = labels // BLOCK
    rows = slope_refs[0].shape[0]
    first = first_ref[0].astype(jnp.float32)

    lane = lax.broadcasted_iota(jnp.int32, (LANES, BLOCK), 1)
    row = lax.broadcasted_iota(jnp.int32, (LANES, BLOCK), 0)
    live_table = jnp.concatenate(
        [
            jnp.where((row == c) & (lane < size_ref[c]), 2.0, 0.0).astype(jnp.bfloat16)
            for c in range(local_count)
        ],
        axis=1,
    )

    named, pieces = [], []
    cluster = lax.broadcasted_iota(jnp.int32, (FIELD_ROWS, rows), 0).astype(jnp.float32) + first
    at = 0
    for b in range(block_count):
        block_refs = x_refs[at : at + len(piece_rows[b])]
        at += len(piece_rows[b])
        pieces += [ref[:count, :] for ref, count in zip(block_refs, piece_rows[b])]
        groups = -(-(top_count + 2 * pos_count) // FIELD_ROWS)
        meta = block_refs[0][piece_rows[b][0] :, : groups * rows].astype(jnp.float32)
        field = [
            meta[f % FIELD_ROWS : f % FIELD_ROWS + 1, f // FIELD_ROWS * rows : (f // FIELD_ROWS + 1) * rows]
            for f in range(top_count + 2 * pos_count)
        ]
        member = jnp.zeros((FIELD_ROWS, rows), jnp.float32)
        for j in range(top_count):
            member = jnp.where(cluster == field[j], 1.0, member)
        target = [
            (field[top_count + q] - first) * BLOCK + field[top_count + pos_count + q]
            for q in range(pos_count)
        ]
        rest = jnp.zeros((LANES - FIELD_ROWS - pos_count, rows), jnp.float32)
        named.append(jnp.concatenate([member] + target + [rest], axis=0).T)

    x = jnp.concatenate(pieces, axis=0) if len(pieces) > 1 else pieces[0]
    named = jnp.concatenate(named, axis=0) if block_count > 1 else named[0]
    target = [named[:, FIELD_ROWS + q : FIELD_ROWS + q + 1] for q in range(pos_count)]
    member = jnp.where(
        lax.broadcasted_iota(jnp.int32, named.shape, 1) < FIELD_ROWS, named, 0.0
    ).astype(jnp.bfloat16)
    for start in range(0, labels, CHUNK):
        logits = lax.dot_general(
            x,
            w_ref[start : start + CHUNK, :],
            (((1,), (1,)), ((), ())),
            preferred_element_type=jnp.float32,
        )
        live = jnp.dot(
            member, live_table[:, start : start + CHUNK], preferred_element_type=jnp.float32
        )
        label = (
            lax.broadcasted_iota(jnp.int32, (1, CHUNK), 1) + start
        ).astype(jnp.float32)
        positive = target[0] == label
        for q in range(1, pos_count):
            positive = positive | (target[q] == label)
        turned = jnp.where(positive, -1.0, 1.0)
        slope = (turned * live * jnp.maximum(1.0 + turned * logits, 0.0)).astype(jnp.bfloat16)
        for b, ref in enumerate(slope_refs):
            ref[:, start : start + CHUNK] = slope[b * rows : (b + 1) * rows]
    slope = [ref[...] for ref in slope_refs]
    slope = jnp.concatenate(slope, axis=0) if block_count > 1 else slope[0]
    for start in range(0, width, CHUNK):
        part = jnp.dot(
            slope, w_ref[:, start : start + CHUNK], preferred_element_type=jnp.float32
        ).astype(jnp.bfloat16)
        at = 0
        for ref in grad_refs:
            ref[:, start : start + CHUNK] = part[at : at + ref.shape[0]]
            at += ref.shape[0]


def block_work(blocks, weights, first, sizes, top_count, pos_count):
    labels, width = weights.shape
    piece_rows = [
        [piece.shape[0] - (FIELD_ROWS if p == 0 else 0) for p, piece in enumerate(pieces)]
        for pieces in blocks
    ]
    flat_rows = sum(piece_rows, [])
    out = pl.pallas_call(
        functools.partial(block_kernel, piece_rows, top_count, pos_count),
        out_shape=[jax.ShapeDtypeStruct((rows, width), jnp.bfloat16) for rows in flat_rows]
        + [jax.ShapeDtypeStruct((sum(rows), labels), jnp.bfloat16) for rows in piece_rows],
        in_specs=[pl.BlockSpec(memory_space=pltpu.SMEM)] * 2
        + [pl.BlockSpec(memory_space=pltpu.VMEM)] * (len(flat_rows) + 1),
        compiler_params=pltpu.CompilerParams(vmem_limit_bytes=VMEM_LIMIT),
        cost_estimate=pl.CostEstimate(
            flops=4 * sum(flat_rows) * labels * width,
            bytes_accessed=2 * labels * width + 6 * sum(flat_rows) * width,
            transcendentals=0,
        ),
        name="block_work",
    )(first, sizes, *[piece for pieces in blocks for piece in pieces], weights)
    return list(out[: len(flat_rows)]), list(out[len(flat_rows) :])


def weight_kernel(piece_rows, column_blocks, scale, own_ref, *refs):
    piece_count = len(piece_rows)
    out_refs = refs[len(refs) - len(column_blocks) :]
    x_refs, s_refs = refs[:piece_count], refs[piece_count : len(refs) - len(column_blocks)]
    part_width = out_refs[0].shape[1]
    slopes = jnp.concatenate([ref[...] for ref in s_refs], axis=0)
    for ref, q in zip(out_refs, column_blocks):
        at = pl.multiple_of((own_ref[0] ^ q) * part_width, part_width)
        x = jnp.concatenate(
            [r[:rows, pl.ds(at, part_width)] for r, rows in zip(x_refs, piece_rows)], axis=0
        )
        part = lax.dot_general(
            slopes, x, (((0,), (0,)), ((), ())), preferred_element_type=jnp.float32
        )
        ref[...] = (part * scale).astype(jnp.bfloat16)


def weight_work(blocks, slopes, own, column_blocks, part_width, scale):
    pieces = [piece for block in blocks for piece in block]
    piece_rows = [
        piece.shape[0] - (FIELD_ROWS if p == 0 else 0)
        for block in blocks
        for p, piece in enumerate(block)
    ]
    labels = slopes[0].shape[1]
    rows = sum(piece_rows)
    return pl.pallas_call(
        functools.partial(weight_kernel, piece_rows, column_blocks, scale),
        out_shape=[jax.ShapeDtypeStruct((labels, part_width), jnp.bfloat16)] * len(column_blocks),
        in_specs=[pl.BlockSpec(memory_space=pltpu.SMEM)]
        + [pl.BlockSpec(memory_space=pltpu.VMEM)] * (len(pieces) + len(slopes)),
        compiler_params=pltpu.CompilerParams(vmem_limit_bytes=VMEM_LIMIT),
        cost_estimate=pl.CostEstimate(
            flops=2 * rows * labels * part_width * len(column_blocks),
            bytes_accessed=2 * rows * (labels + 1024) + 2 * labels * part_width,
            transcendentals=0,
        ),
        name="weight_work",
    )(own, *pieces, *slopes)


def add(*parts):
    total = parts[0].astype(jnp.float32)
    for part in parts[1:]:
        total = total + part.astype(jnp.float32)
    return total.astype(jnp.bfloat16)


def after(array, *others):
    return lax.optimization_barrier((array, *others))[0]


def local(features, shortlist, positives, cluster_sizes, weights):
    inst_rows, width = features.shape
    top_count, pos_count = shortlist.shape[1], positives.shape[1]
    clus_count, seq_count = lax.axis_size("clus"), lax.axis_size("seq")
    local_count = cluster_sizes.shape[0]
    part_width = width // seq_count
    half, steps = inst_rows // 2, clus_count // 2

    ring = list(range(0, clus_count, 2)) + list(range(1, clus_count, 2))[::-1]
    onward = []
    for s in range(seq_count):
        places = [s * clus_count + c for c in (ring if s % 2 == 0 else ring[::-1])]
        onward += list(zip(places, places[1:] + places[:1]))
    back = [(b, a) for a, b in onward]

    def send(array, pairs):
        return lax.ppermute(array, ("seq", "clus"), pairs)

    first = (lax.axis_index("clus") * local_count).astype(jnp.int32).reshape(1)
    used, slopes = [], []

    def take(*blocks):
        grads, found = block_work(blocks, weights, first, cluster_sizes, top_count, pos_count)
        used.extend(blocks)
        slopes.extend(found)
        return grads

    own = pack(features, shortlist, positives)
    behind_x, front_x = own, own
    parts = {}
    for k in range(1, steps + 1):
        if k > 1:
            behind_x, front_x = after(behind_x, parts[k - 2][0]), after(front_x, parts[k - 2][0])
        if k < steps:
            going = behind_x, front_x
        else:
            going = (
                jnp.concatenate([behind_x[:half], behind_x[inst_rows:]], axis=0),
                front_x[half:inst_rows],
            )
        arriving = send(going[0], onward), send(going[1], back)
        parts[k - 1] = take([own]) if k == 1 else take([behind_x], [front_x])
        behind_x, front_x = arriving
    to_back, to_front = take([after(behind_x, parts[steps - 1][0]), front_x])

    scale = 1.0 / math.sqrt(inst_rows * seq_count * top_count // local_count)
    own_seq = lax.axis_index("seq").astype(jnp.int32).reshape(1)

    def seq_send(array, bit):
        return lax.ppermute(array, "seq", [(k, k ^ bit) for k in range(seq_count)])

    far, near = list(range(seq_count // 2, seq_count)), list(range(seq_count // 2))
    terms = dict(zip(far, weight_work(used, slopes, own_seq, far, part_width, scale)))
    terms.update(zip(near, weight_work(used, slopes, own_seq, near, part_width, scale)))
    terms = {q: [term] for q, term in terms.items()}
    bit = 1
    while bit < seq_count:
        for q in [q for q in sorted(terms, reverse=True) if q & bit]:
            values = terms.pop(q)
            terms[q ^ bit].append(seq_send(add(*values) if len(values) > 1 else values[0], bit))
        bit *= 2
    weight_grad = add(*terms[0])

    for k in range(steps, 0, -1):
        from_front, from_behind = send(to_back, back), send(to_front, onward)
        if k == steps:
            near_behind, near_front = parts[k - 1]
            to_back = jnp.concatenate([add(near_behind[:half], from_front), near_behind[half:]], axis=0)
            to_front = jnp.concatenate([near_front[:half], add(near_front[half:], from_behind)], axis=0)
        elif k > 1:
            near_behind, near_front = parts[k - 1]
            to_back, to_front = add(near_behind, from_front), add(near_front, from_behind)
    feature_grad = add(after(parts[0][0], weight_grad), from_front, from_behind)
    return (feature_grad, weight_grad)


def solution(mesh):
    return jax.shard_map(
        local,
        mesh=mesh,
        in_specs=(
            P(("seq", "clus"), None),
            P(("seq", "clus"), None),
            P(("seq", "clus"), None),
            P("clus"),
            P("clus", None),
        ),
        out_specs=(P(("seq", "clus"), None), P("clus", "seq")),
        check_vma=False,
    )
```

```python
import functools
import math

import jax
import jax.numpy as jnp
from jax import lax
from jax.experimental import pallas as pl
from jax.experimental.pallas import tpu as pltpu
from jax.sharding import PartitionSpec as P

BLOCK = 128
LANES = 128
FIELD_ROWS = 8
CHUNK = 256
VMEM_LIMIT = 40 * 1024 * 1024
WHOLE_VMEM = 60 * 1024 * 1024


def pack_kernel(feat_ref, short_in, pos_in, out_ref, short_ref, pos_ref, meta_ref, sems):
    rows, width = feat_ref.shape
    copies = [
        pltpu.make_async_copy(short_in, short_ref, sems.at[0]),
        pltpu.make_async_copy(pos_in, pos_ref, sems.at[1]),
        pltpu.make_async_copy(feat_ref, out_ref.at[pl.ds(0, rows)], sems.at[2]),
        pltpu.make_async_copy(meta_ref, out_ref.at[pl.ds(rows, FIELD_ROWS)], sems.at[3]),
    ]
    for copy in copies[:3]:
        copy.start()
    copies[0].wait()
    copies[1].wait()
    short = short_ref[...]
    places = pos_ref[...] // BLOCK
    offsets = pos_ref[...] % BLOCK
    targets = jnp.zeros_like(places)
    for j in range(short.shape[0]):
        targets = targets + jnp.where(places == j, short[j : j + 1, :], 0)
    fields = jnp.concatenate([short, targets, offsets], axis=0)
    groups = [
        fields[at : at + FIELD_ROWS] for at in range(0, fields.shape[0], FIELD_ROWS)
    ]
    groups.append(jnp.zeros((FIELD_ROWS, width - rows * len(groups)), jnp.int32))
    meta = jnp.concatenate(groups, axis=1)
    meta_ref[...] = meta.astype(jnp.float32).astype(jnp.bfloat16)
    copies[3].start()
    copies[2].wait()
    copies[3].wait()


def pack(features, shortlist, positives):
    rows, width = features.shape
    return pl.pallas_call(
        pack_kernel,
        out_shape=jax.ShapeDtypeStruct((rows + FIELD_ROWS, width), jnp.bfloat16),
        in_specs=[pl.BlockSpec(memory_space=pl.ANY)] * 3,
        out_specs=pl.BlockSpec(memory_space=pl.ANY),
        scratch_shapes=[
            pltpu.VMEM(shortlist.shape[::-1], jnp.int32),
            pltpu.VMEM(positives.shape[::-1], jnp.int32),
            pltpu.VMEM((FIELD_ROWS, width), jnp.bfloat16),
            pltpu.SemaphoreType.DMA((4,)),
        ],
        compiler_params=pltpu.CompilerParams(vmem_limit_bytes=WHOLE_VMEM),
        name="pack",
    )(features, shortlist.T, positives.T)


def live_kernel(size_ref, x_ref, w_ref, live_ref):
    lane = lax.broadcasted_iota(jnp.int32, (LANES, BLOCK), 1)
    row = lax.broadcasted_iota(jnp.int32, (LANES, BLOCK), 0)
    for c in range(size_ref.shape[0]):
        live = jnp.where((row == c) & (lane < size_ref[c]), 2.0, 0.0)
        live_ref[:, c * BLOCK : (c + 1) * BLOCK] = live.astype(jnp.bfloat16)


def live_labels(cluster_sizes, block, weights):
    return pl.pallas_call(
        live_kernel,
        out_shape=jax.ShapeDtypeStruct((LANES, cluster_sizes.shape[0] * BLOCK), jnp.bfloat16),
        in_specs=[pl.BlockSpec(memory_space=pltpu.SMEM)]
        + [pl.BlockSpec(memory_space=pltpu.VMEM)] * 2,
        compiler_params=pltpu.CompilerParams(vmem_limit_bytes=VMEM_LIMIT),
        name="live_labels",
    )(cluster_sizes, block, weights)


def block_kernel(piece_rows, top_count, pos_count, *refs):
    block_count = len(piece_rows)
    piece_count = sum(len(pieces) for pieces in piece_rows)
    x_refs = refs[:piece_count]
    w_ref, live_ref = refs[piece_count : piece_count + 2]
    grad_refs = refs[piece_count + 2 : 2 * piece_count + 2]
    slope_refs = refs[2 * piece_count + 2 :]
    labels, width = w_ref.shape
    local_count = labels // BLOCK
    rows = slope_refs[0].shape[0]
    first = (lax.axis_index("clus") * local_count).astype(jnp.float32)

    named, pieces = [], []
    cluster = lax.broadcasted_iota(jnp.int32, (FIELD_ROWS, rows), 0).astype(jnp.float32) + first
    at = 0
    for b in range(block_count):
        block_refs = x_refs[at : at + len(piece_rows[b])]
        at += len(piece_rows[b])
        pieces += [ref[:count, :] for ref, count in zip(block_refs, piece_rows[b])]
        groups = -(-(top_count + 2 * pos_count) // FIELD_ROWS)
        meta = block_refs[0][piece_rows[b][0] :, : groups * rows].astype(jnp.float32)
        field = [
            meta[f % FIELD_ROWS : f % FIELD_ROWS + 1, f // FIELD_ROWS * rows : (f // FIELD_ROWS + 1) * rows]
            for f in range(top_count + 2 * pos_count)
        ]
        member = jnp.zeros((FIELD_ROWS, rows), jnp.float32)
        for j in range(top_count):
            member = jnp.where(cluster == field[j], 1.0, member)
        target = [
            (field[top_count + q] - first) * BLOCK + field[top_count + pos_count + q]
            for q in range(pos_count)
        ]
        rest = jnp.zeros((LANES - FIELD_ROWS - pos_count, rows), jnp.float32)
        named.append(jnp.concatenate([member] + target + [rest], axis=0).T)

    x = jnp.concatenate(pieces, axis=0) if len(pieces) > 1 else pieces[0]
    named = jnp.concatenate(named, axis=0) if block_count > 1 else named[0]
    target = [named[:, FIELD_ROWS + q : FIELD_ROWS + q + 1] for q in range(pos_count)]
    member = jnp.where(
        lax.broadcasted_iota(jnp.int32, named.shape, 1) < FIELD_ROWS, named, 0.0
    ).astype(jnp.bfloat16)
    for start in range(0, labels, CHUNK):
        logits = lax.dot_general(
            x,
            w_ref[start : start + CHUNK, :],
            (((1,), (1,)), ((), ())),
            preferred_element_type=jnp.float32,
        )
        live = jnp.dot(
            member, live_ref[:, start : start + CHUNK], preferred_element_type=jnp.float32
        )
        label = (
            lax.broadcasted_iota(jnp.int32, (1, CHUNK), 1) + start
        ).astype(jnp.float32)
        positive = target[0] == label
        for q in range(1, pos_count):
            positive = positive | (target[q] == label)
        turned = jnp.where(positive, -1.0, 1.0)
        slope = (turned * live * jnp.maximum(1.0 + turned * logits, 0.0)).astype(jnp.bfloat16)
        for b, ref in enumerate(slope_refs):
            ref[:, start : start + CHUNK] = slope[b * rows : (b + 1) * rows]
    slope = [ref[...] for ref in slope_refs]
    slope = jnp.concatenate(slope, axis=0) if block_count > 1 else slope[0]
    for start in range(0, width, CHUNK):
        part = jnp.dot(
            slope, w_ref[:, start : start + CHUNK], preferred_element_type=jnp.float32
        ).astype(jnp.bfloat16)
        at = 0
        for ref in grad_refs:
            ref[:, start : start + CHUNK] = part[at : at + ref.shape[0]]
            at += ref.shape[0]


def block_work(blocks, weights, live_table, top_count, pos_count):
    labels, width = weights.shape
    piece_rows = [
        [piece.shape[0] - (FIELD_ROWS if p == 0 else 0) for p, piece in enumerate(pieces)]
        for pieces in blocks
    ]
    flat_rows = sum(piece_rows, [])
    out = pl.pallas_call(
        functools.partial(block_kernel, piece_rows, top_count, pos_count),
        out_shape=[jax.ShapeDtypeStruct((rows, width), jnp.bfloat16) for rows in flat_rows]
        + [jax.ShapeDtypeStruct((sum(rows), labels), jnp.bfloat16) for rows in piece_rows],
        in_specs=[pl.BlockSpec(memory_space=pltpu.VMEM)] * (len(flat_rows) + 2),
        compiler_params=pltpu.CompilerParams(vmem_limit_bytes=VMEM_LIMIT),
        cost_estimate=pl.CostEstimate(
            flops=4 * sum(flat_rows) * labels * width,
            bytes_accessed=2 * labels * width + 6 * sum(flat_rows) * width,
            transcendentals=0,
        ),
        name="block_work",
    )(*[piece for pieces in blocks for piece in pieces], weights, live_table)
    return list(out[: len(flat_rows)]), list(out[len(flat_rows) :])


def weight_kernel(piece_rows, column_blocks, scale, *refs):
    piece_count = len(piece_rows)
    out_refs = refs[len(refs) - len(column_blocks) :]
    x_refs, s_refs = refs[:piece_count], refs[piece_count : len(refs) - len(column_blocks)]
    part_width = out_refs[0].shape[1]
    slopes = jnp.concatenate([ref[...] for ref in s_refs], axis=0)
    for ref, q in zip(out_refs, column_blocks):
        at = pl.multiple_of((lax.axis_index("seq") ^ q) * part_width, part_width)
        x = jnp.concatenate(
            [r[:rows, pl.ds(at, part_width)] for r, rows in zip(x_refs, piece_rows)], axis=0
        )
        part = lax.dot_general(
            slopes, x, (((0,), (0,)), ((), ())), preferred_element_type=jnp.float32
        )
        ref[...] = (part * scale).astype(jnp.bfloat16)


def weight_work(blocks, slopes, column_blocks, part_width, scale):
    pieces = [piece for block in blocks for piece in block]
    piece_rows = [
        piece.shape[0] - (FIELD_ROWS if p == 0 else 0)
        for block in blocks
        for p, piece in enumerate(block)
    ]
    labels = slopes[0].shape[1]
    rows = sum(piece_rows)
    return pl.pallas_call(
        functools.partial(weight_kernel, piece_rows, column_blocks, scale),
        out_shape=[jax.ShapeDtypeStruct((labels, part_width), jnp.bfloat16)] * len(column_blocks),
        in_specs=[pl.BlockSpec(memory_space=pltpu.VMEM)] * (len(pieces) + len(slopes)),
        compiler_params=pltpu.CompilerParams(vmem_limit_bytes=VMEM_LIMIT),
        cost_estimate=pl.CostEstimate(
            flops=2 * rows * labels * part_width * len(column_blocks),
            bytes_accessed=2 * rows * (labels + 1024) + 2 * labels * part_width,
            transcendentals=0,
        ),
        name="weight_work",
    )(*pieces, *slopes)


def add(*parts):
    total = parts[0].astype(jnp.float32)
    for part in parts[1:]:
        total = total + part.astype(jnp.float32)
    return total.astype(jnp.bfloat16)


def after(array, *others):
    return lax.optimization_barrier((array, *others))[0]


def local(features, shortlist, positives, cluster_sizes, weights):
    inst_rows, width = features.shape
    top_count, pos_count = shortlist.shape[1], positives.shape[1]
    clus_count, seq_count = lax.axis_size("clus"), lax.axis_size("seq")
    local_count = cluster_sizes.shape[0]
    part_width = width // seq_count
    half, steps = inst_rows // 2, clus_count // 2

    ring = list(range(0, clus_count, 2)) + list(range(1, clus_count, 2))[::-1]
    onward = list(zip(ring, ring[1:] + ring[:1]))
    back = [(b, a) for a, b in onward]

    def send(array, pairs):
        return lax.ppermute(array, "clus", pairs)

    used, slopes = [], []

    def take(*blocks):
        grads, found = block_work(blocks, weights, live_table, top_count, pos_count)
        used.extend(blocks)
        slopes.extend(found)
        return grads

    own = pack(features, shortlist, positives)
    live_table = live_labels(cluster_sizes, own, weights)
    behind_x, front_x = own, own
    parts = {}
    for k in range(1, steps + 1):
        if k > 1:
            before = live_table if k == 2 else parts[k - 2][0]
            behind_x, front_x = after(behind_x, before), after(front_x, before)
        if k < steps:
            going = behind_x, front_x
        else:
            going = (
                jnp.concatenate([behind_x[:half], behind_x[inst_rows:]], axis=0),
                front_x[half:inst_rows],
            )
        arriving = send(going[0], onward), send(going[1], back)
        if k == 2:
            *parts[1], own_part = take([behind_x], [front_x], [own])
        elif k > 2:
            parts[k - 1] = take([behind_x], [front_x])
        behind_x, front_x = arriving
    to_back, to_front = take([after(behind_x, parts[steps - 1][0]), front_x])

    scale = 1.0 / math.sqrt(inst_rows * seq_count * top_count // local_count)

    def seq_send(array, bit):
        return lax.ppermute(array, "seq", [(k, k ^ bit) for k in range(seq_count)])

    far, near = list(range(seq_count // 2, seq_count)), list(range(seq_count // 2))
    terms = dict(zip(far, weight_work(used, slopes, far, part_width, scale)))
    terms.update(zip(near, weight_work(used, slopes, near, part_width, scale)))
    terms = {q: [term] for q, term in terms.items()}
    bit = 1
    while bit < seq_count:
        for q in [q for q in sorted(terms, reverse=True) if q & bit]:
            values = terms.pop(q)
            terms[q ^ bit].append(seq_send(add(*values) if len(values) > 1 else values[0], bit))
        bit *= 2
    weight_grad = add(*terms[0])

    for k in range(steps, 0, -1):
        from_front, from_behind = send(to_back, back), send(to_front, onward)
        if k == steps:
            near_behind, near_front = parts[k - 1]
            to_back = jnp.concatenate([add(near_behind[:half], from_front), near_behind[half:]], axis=0)
            to_front = jnp.concatenate([near_front[:half], add(near_front[half:], from_behind)], axis=0)
        elif k > 1:
            near_behind, near_front = parts[k - 1]
            to_back, to_front = add(near_behind, from_front), add(near_front, from_behind)
    feature_grad = add(after(own_part, weight_grad), from_front, from_behind)
    return (feature_grad, weight_grad)


def solution(mesh):
    return jax.shard_map(
        local,
        mesh=mesh,
        in_specs=(
            P(("seq", "clus"), None),
            P(("seq", "clus"), None),
            P(("seq", "clus"), None),
            P("clus"),
            P("clus", None),
        ),
        out_specs=(P(("seq", "clus"), None), P("clus", "seq")),
        check_vma=False,
    )
```

```python
import functools
import math

import jax
import jax.numpy as jnp
from jax import lax
from jax.experimental import pallas as pl
from jax.experimental.pallas import tpu as pltpu
from jax.sharding import PartitionSpec as P

BLOCK = 128
LANES = 128
FIELD_ROWS = 8
CHUNK = 256
VMEM_LIMIT = 40 * 1024 * 1024


def pack_kernel(feat_ref, short_ref, pos_ref, a_ref, b_ref):
    half, width = b_ref.shape
    rows = 2 * half
    a_ref[:half, :] = feat_ref[:half, :]
    b_ref[...] = feat_ref[half:, :]
    short = short_ref[...]
    places = pos_ref[...] // BLOCK
    offsets = pos_ref[...] % BLOCK
    targets = jnp.zeros_like(places)
    for j in range(short.shape[0]):
        targets = targets + jnp.where(places == j, short[j : j + 1, :], 0)
    fields = jnp.concatenate([short, targets, offsets], axis=0)
    groups = [
        fields[at : at + FIELD_ROWS] for at in range(0, fields.shape[0], FIELD_ROWS)
    ]
    groups.append(jnp.zeros((FIELD_ROWS, width - rows * len(groups)), jnp.int32))
    meta = jnp.concatenate(groups, axis=1)
    a_ref[half:, :] = meta.astype(jnp.float32).astype(jnp.bfloat16)


def pack(features, shortlist, positives):
    rows, width = features.shape
    half = rows // 2
    return pl.pallas_call(
        pack_kernel,
        out_shape=[
            jax.ShapeDtypeStruct((half + FIELD_ROWS, width), jnp.bfloat16),
            jax.ShapeDtypeStruct((half, width), jnp.bfloat16),
        ],
        in_specs=[pl.BlockSpec(memory_space=pltpu.VMEM)] * 3,
        compiler_params=pltpu.CompilerParams(vmem_limit_bytes=VMEM_LIMIT),
        name="pack",
    )(features, shortlist.T, positives.T)


def live_kernel(size_ref, w_ref, live_ref):
    lane = lax.broadcasted_iota(jnp.int32, (LANES, BLOCK), 1)
    row = lax.broadcasted_iota(jnp.int32, (LANES, BLOCK), 0)
    for c in range(size_ref.shape[0]):
        live = jnp.where((row == c) & (lane < size_ref[c]), 2.0, 0.0)
        live_ref[:, c * BLOCK : (c + 1) * BLOCK] = live.astype(jnp.bfloat16)


def live_labels(cluster_sizes, weights):
    return pl.pallas_call(
        live_kernel,
        out_shape=jax.ShapeDtypeStruct((LANES, cluster_sizes.shape[0] * BLOCK), jnp.bfloat16),
        in_specs=[
            pl.BlockSpec(memory_space=pltpu.SMEM),
            pl.BlockSpec(memory_space=pltpu.VMEM),
        ],
        compiler_params=pltpu.CompilerParams(vmem_limit_bytes=VMEM_LIMIT),
        name="live_labels",
    )(cluster_sizes, weights)


def block_kernel(piece_rows, top_count, pos_count, *refs):
    block_count = len(piece_rows)
    piece_count = sum(len(pieces) for pieces in piece_rows)
    x_refs = refs[:piece_count]
    w_ref, live_ref = refs[piece_count : piece_count + 2]
    grad_refs = refs[piece_count + 2 : 2 * piece_count + 2]
    slope_refs = refs[2 * piece_count + 2 :]
    labels, width = w_ref.shape
    local_count = labels // BLOCK
    rows = slope_refs[0].shape[0]
    first = (lax.axis_index("clus") * local_count).astype(jnp.float32)

    named, pieces = [], []
    cluster = lax.broadcasted_iota(jnp.int32, (FIELD_ROWS, rows), 0).astype(jnp.float32) + first
    at = 0
    for b in range(block_count):
        block_refs = x_refs[at : at + len(piece_rows[b])]
        at += len(piece_rows[b])
        pieces += [ref[:count, :] for ref, count in zip(block_refs, piece_rows[b])]
        groups = -(-(top_count + 2 * pos_count) // FIELD_ROWS)
        meta = block_refs[0][piece_rows[b][0] :, : groups * rows].astype(jnp.float32)
        field = [
            meta[f % FIELD_ROWS : f % FIELD_ROWS + 1, f // FIELD_ROWS * rows : (f // FIELD_ROWS + 1) * rows]
            for f in range(top_count + 2 * pos_count)
        ]
        member = jnp.zeros((FIELD_ROWS, rows), jnp.float32)
        for j in range(top_count):
            member = jnp.where(cluster == field[j], 1.0, member)
        target = [
            (field[top_count + q] - first) * BLOCK + field[top_count + pos_count + q]
            for q in range(pos_count)
        ]
        rest = jnp.zeros((LANES - FIELD_ROWS - pos_count, rows), jnp.float32)
        named.append(jnp.concatenate([member] + target + [rest], axis=0).T)

    x = jnp.concatenate(pieces, axis=0) if len(pieces) > 1 else pieces[0]
    named = jnp.concatenate(named, axis=0) if block_count > 1 else named[0]
    target = [named[:, FIELD_ROWS + q : FIELD_ROWS + q + 1] for q in range(pos_count)]
    member = jnp.where(
        lax.broadcasted_iota(jnp.int32, named.shape, 1) < FIELD_ROWS, named, 0.0
    ).astype(jnp.bfloat16)
    for start in range(0, labels, CHUNK):
        logits = lax.dot_general(
            x,
            w_ref[start : start + CHUNK, :],
            (((1,), (1,)), ((), ())),
            preferred_element_type=jnp.float32,
        )
        live = jnp.dot(
            member, live_ref[:, start : start + CHUNK], preferred_element_type=jnp.float32
        )
        label = (
            lax.broadcasted_iota(jnp.int32, (1, CHUNK), 1) + start
        ).astype(jnp.float32)
        positive = target[0] == label
        for q in range(1, pos_count):
            positive = positive | (target[q] == label)
        turned = jnp.where(positive, -1.0, 1.0)
        slope = (turned * live * jnp.maximum(1.0 + turned * logits, 0.0)).astype(jnp.bfloat16)
        for b, ref in enumerate(slope_refs):
            ref[:, start : start + CHUNK] = slope[b * rows : (b + 1) * rows]
    slope = [ref[...] for ref in slope_refs]
    slope = jnp.concatenate(slope, axis=0) if block_count > 1 else slope[0]
    for start in range(0, width, CHUNK):
        part = jnp.dot(
            slope, w_ref[:, start : start + CHUNK], preferred_element_type=jnp.float32
        ).astype(jnp.bfloat16)
        at = 0
        for ref in grad_refs:
            ref[:, start : start + CHUNK] = part[at : at + ref.shape[0]]
            at += ref.shape[0]


def block_work(blocks, weights, live_table, top_count, pos_count):
    labels, width = weights.shape
    piece_rows = [
        [piece.shape[0] - (FIELD_ROWS if p == 0 else 0) for p, piece in enumerate(pieces)]
        for pieces in blocks
    ]
    flat_rows = sum(piece_rows, [])
    out = pl.pallas_call(
        functools.partial(block_kernel, piece_rows, top_count, pos_count),
        out_shape=[jax.ShapeDtypeStruct((rows, width), jnp.bfloat16) for rows in flat_rows]
        + [jax.ShapeDtypeStruct((sum(rows), labels), jnp.bfloat16) for rows in piece_rows],
        in_specs=[pl.BlockSpec(memory_space=pltpu.VMEM)] * (len(flat_rows) + 2),
        compiler_params=pltpu.CompilerParams(vmem_limit_bytes=VMEM_LIMIT),
        cost_estimate=pl.CostEstimate(
            flops=4 * sum(flat_rows) * labels * width,
            bytes_accessed=2 * labels * width + 6 * sum(flat_rows) * width,
            transcendentals=0,
        ),
        name="block_work",
    )(*[piece for pieces in blocks for piece in pieces], weights, live_table)
    return list(out[: len(flat_rows)]), list(out[len(flat_rows) :])


def weight_kernel(piece_rows, column_blocks, scale, *refs):
    piece_count = len(piece_rows)
    out_refs = refs[len(refs) - len(column_blocks) :]
    x_refs, s_refs = refs[:piece_count], refs[piece_count : len(refs) - len(column_blocks)]
    part_width = out_refs[0].shape[1]
    slopes = jnp.concatenate([ref[...] for ref in s_refs], axis=0)
    for ref, q in zip(out_refs, column_blocks):
        at = pl.multiple_of((lax.axis_index("seq") ^ q) * part_width, part_width)
        x = jnp.concatenate(
            [r[:rows, pl.ds(at, part_width)] for r, rows in zip(x_refs, piece_rows)], axis=0
        )
        part = lax.dot_general(
            slopes, x, (((0,), (0,)), ((), ())), preferred_element_type=jnp.float32
        )
        ref[...] = (part * scale).astype(jnp.bfloat16)


def weight_work(blocks, slopes, column_blocks, part_width, scale):
    pieces = [piece for block in blocks for piece in block]
    piece_rows = [
        piece.shape[0] - (FIELD_ROWS if p == 0 else 0)
        for block in blocks
        for p, piece in enumerate(block)
    ]
    labels = slopes[0].shape[1]
    rows = sum(piece_rows)
    return pl.pallas_call(
        functools.partial(weight_kernel, piece_rows, column_blocks, scale),
        out_shape=[jax.ShapeDtypeStruct((labels, part_width), jnp.bfloat16)] * len(column_blocks),
        in_specs=[pl.BlockSpec(memory_space=pltpu.VMEM)] * (len(pieces) + len(slopes)),
        compiler_params=pltpu.CompilerParams(vmem_limit_bytes=VMEM_LIMIT),
        cost_estimate=pl.CostEstimate(
            flops=2 * rows * labels * part_width * len(column_blocks),
            bytes_accessed=2 * rows * (labels + 1024) + 2 * labels * part_width,
            transcendentals=0,
        ),
        name="weight_work",
    )(*pieces, *slopes)


def add(*parts):
    total = parts[0].astype(jnp.float32)
    for part in parts[1:]:
        total = total + part.astype(jnp.float32)
    return total.astype(jnp.bfloat16)


def after(array, *others):
    return lax.optimization_barrier((array, *others))[0]


class Turn:
    def __init__(self):
        self.before = []

    def passed(self, array):
        self.before.append(array)

    def __call__(self, array):
        if self.before:
            array = after(array, *self.before)
        self.before = [array]
        return array


def local(features, shortlist, positives, cluster_sizes, weights):
    inst_rows, width = features.shape
    top_count, pos_count = shortlist.shape[1], positives.shape[1]
    clus_count, seq_count = lax.axis_size("clus"), lax.axis_size("seq")
    local_count = cluster_sizes.shape[0]
    part_width = width // seq_count
    steps = clus_count // 2
    last = steps - 1

    ring = list(range(0, clus_count, 2)) + list(range(1, clus_count, 2))[::-1]
    up = list(zip(ring, ring[1:] + ring[:1]))
    down = [(b, a) for a, b in up]

    def send_up(array):
        return lax.ppermute(array, "clus", up)

    def send_down(array):
        return lax.ppermute(array, "clus", down)

    used, slopes = [], []

    def take(*blocks):
        grads, found = block_work(blocks, weights, live_table, top_count, pos_count)
        used.extend(blocks)
        slopes.extend(found)
        return [(grads[2 * b], grads[2 * b + 1]) for b in range(len(blocks))]

    own = tuple(pack(features, shortlist, positives))
    live_table = live_labels(cluster_sizes, weights)
    below, above = {0: own}, {0: own}
    below_grad, above_grad = {}, {}
    for k in range(1, steps + 1):
        here_below, here_above = below[k - 1], above[k - 1]
        if k > 1:
            before = live_table if k == 2 else below_grad[k - 2][0]
            here_below = [after(piece, before) for piece in here_below]
            here_above = [after(piece, before) for piece in here_above]
        a_up = send_up(here_below[0])
        b_down = send_down(here_above[1])
        if k < steps:
            b_up = send_up(here_below[1])
            a_down = send_down(here_above[0])
            below[k], above[k] = (a_up, b_up), (a_down, b_down)
        else:
            opposite = (a_up, b_down)
        if k == 2:
            below_grad[1], above_grad[1], own_grad = take(below[1], above[1], own)
        elif k > 2:
            below_grad[k - 1], above_grad[k - 1] = take(below[k - 1], above[k - 1])

    turn = Turn()
    b_from_above = send_down(turn(below_grad[last][1]))
    a_from_below = send_up(turn(above_grad[last][0]))
    (far_grad,) = take(opposite)
    turn.passed(far_grad[0])
    a_from_above = send_down(turn(far_grad[0]))
    b_from_below = send_up(turn(far_grad[1]))
    b_from_above, a_from_below = after(b_from_above, far_grad[0]), after(a_from_below, far_grad[0])

    scale = 1.0 / math.sqrt(inst_rows * seq_count * top_count // local_count)

    def seq_send(array, bit):
        return lax.ppermute(array, "seq", [(k, k ^ bit) for k in range(seq_count)])

    terms = {}

    def weigh(slots):
        parts = weight_work(used, slopes, slots, part_width, scale)
        turn.passed(parts[0])
        terms.update({q: [part] for q, part in zip(slots, parts)})

    def halve(bit, slots):
        for q in slots:
            values = terms.pop(q)
            going = turn(add(*values) if len(values) > 1 else values[0])
            terms[q ^ bit].append(seq_send(going, bit))

    near, far = list(range(seq_count // 2)), list(range(seq_count // 2, seq_count))
    for k in range(last, 0, -1):
        a_down, b_up = (below_grad[k][0], a_from_above), (above_grad[k][1], b_from_below)
        if k > 1:
            b_down, a_up = (below_grad[k - 1][1], b_from_above), (above_grad[k - 1][0], a_from_below)
            b_from_above = send_down(turn(add(*b_down)))
            a_from_below = send_up(turn(add(*a_up)))
        else:
            turn.passed(b_from_above)
            turn.passed(a_from_below)
        if k == last:
            weigh(far)
            halve(1, far[1::2])
        a_from_above = send_down(turn(add(*a_down)))
        b_from_below = send_up(turn(add(*b_up)))
        if k == last:
            weigh(near)
            halve(1, near[1::2])
        if k == max(last - 1, 1):
            bit = 2
            while bit < seq_count:
                halve(bit, [q for q in sorted(terms, reverse=True) if q & bit])
                bit *= 2
    weight_grad = add(*terms[0])

    feature_grad = jnp.concatenate(
        [
            add(after(own_grad[0], weight_grad), a_from_above, a_from_below),
            add(after(own_grad[1], weight_grad), b_from_above, b_from_below),
        ],
        axis=0,
    )
    return (feature_grad, weight_grad)


def solution(mesh):
    return jax.shard_map(
        local,
        mesh=mesh,
        in_specs=(
            P(("seq", "clus"), None),
            P(("seq", "clus"), None),
            P(("seq", "clus"), None),
            P("clus"),
            P("clus", None),
        ),
        out_specs=(P(("seq", "clus"), None), P("clus", "seq")),
        check_vma=False,
    )
```

```python
import functools
import math

import jax
import jax.numpy as jnp
from jax import lax
from jax.experimental import pallas as pl
from jax.experimental.pallas import tpu as pltpu
from jax.sharding import PartitionSpec as P

BLOCK = 128
LANES = 128
FIELD_ROWS = 8
CHUNK = 256
VMEM_LIMIT = 40 * 1024 * 1024


def pack_kernel(feat_ref, short_ref, pos_ref, out_ref):
    rows, width = feat_ref.shape
    out_ref[:rows, :] = feat_ref[...]
    short = short_ref[...]
    places = pos_ref[...] // BLOCK
    offsets = pos_ref[...] % BLOCK
    targets = jnp.zeros_like(places)
    for j in range(short.shape[0]):
        targets = targets + jnp.where(places == j, short[j : j + 1, :], 0)
    fields = jnp.concatenate([short, targets, offsets], axis=0)
    groups = [
        fields[at : at + FIELD_ROWS] for at in range(0, fields.shape[0], FIELD_ROWS)
    ]
    groups.append(jnp.zeros((FIELD_ROWS, width - rows * len(groups)), jnp.int32))
    meta = jnp.concatenate(groups, axis=1)
    out_ref[rows:, :] = meta.astype(jnp.float32).astype(jnp.bfloat16)


def pack(features, shortlist, positives):
    rows, width = features.shape
    return pl.pallas_call(
        pack_kernel,
        out_shape=jax.ShapeDtypeStruct((rows + FIELD_ROWS, width), jnp.bfloat16),
        in_specs=[pl.BlockSpec(memory_space=pltpu.VMEM)] * 3,
        compiler_params=pltpu.CompilerParams(vmem_limit_bytes=VMEM_LIMIT),
        name="pack",
    )(features, shortlist.T, positives.T)


def live_kernel(size_ref, w_ref, live_ref):
    lane = lax.broadcasted_iota(jnp.int32, (LANES, BLOCK), 1)
    row = lax.broadcasted_iota(jnp.int32, (LANES, BLOCK), 0)
    for c in range(size_ref.shape[0]):
        live = jnp.where((row == c) & (lane < size_ref[c]), 2.0, 0.0)
        live_ref[:, c * BLOCK : (c + 1) * BLOCK] = live.astype(jnp.bfloat16)


def live_labels(cluster_sizes, weights):
    return pl.pallas_call(
        live_kernel,
        out_shape=jax.ShapeDtypeStruct((LANES, cluster_sizes.shape[0] * BLOCK), jnp.bfloat16),
        in_specs=[pl.BlockSpec(memory_space=pltpu.SMEM)]
        + [pl.BlockSpec(memory_space=pltpu.VMEM)],
        compiler_params=pltpu.CompilerParams(vmem_limit_bytes=VMEM_LIMIT),
        name="live_labels",
    )(cluster_sizes, weights)


def block_kernel(piece_rows, top_count, pos_count, *refs):
    block_count = len(piece_rows)
    piece_count = sum(len(pieces) for pieces in piece_rows)
    x_refs = refs[:piece_count]
    w_ref, live_ref = refs[piece_count : piece_count + 2]
    grad_refs = refs[piece_count + 2 : piece_count + 2 + 2 * block_count]
    slope_refs = refs[piece_count + 2 + 2 * block_count :]
    labels, width = w_ref.shape
    local_count = labels // BLOCK
    rows = slope_refs[0].shape[0]
    first = (lax.axis_index("clus") * local_count).astype(jnp.float32)

    named, pieces = [], []
    cluster = lax.broadcasted_iota(jnp.int32, (FIELD_ROWS, rows), 0).astype(jnp.float32) + first
    at = 0
    for b in range(block_count):
        block_refs = x_refs[at : at + len(piece_rows[b])]
        at += len(piece_rows[b])
        pieces += [ref[:count, :] for ref, count in zip(block_refs, piece_rows[b])]
        groups = -(-(top_count + 2 * pos_count) // FIELD_ROWS)
        meta = block_refs[0][piece_rows[b][0] :, : groups * rows].astype(jnp.float32)
        field = [
            meta[f % FIELD_ROWS : f % FIELD_ROWS + 1, f // FIELD_ROWS * rows : (f // FIELD_ROWS + 1) * rows]
            for f in range(top_count + 2 * pos_count)
        ]
        member = jnp.zeros((FIELD_ROWS, rows), jnp.float32)
        for j in range(top_count):
            member = jnp.where(cluster == field[j], 1.0, member)
        target = [
            (field[top_count + q] - first) * BLOCK + field[top_count + pos_count + q]
            for q in range(pos_count)
        ]
        rest = jnp.zeros((LANES - FIELD_ROWS - pos_count, rows), jnp.float32)
        named.append(jnp.concatenate([member] + target + [rest], axis=0).T)

    x = jnp.concatenate(pieces, axis=0) if len(pieces) > 1 else pieces[0]
    named = jnp.concatenate(named, axis=0) if block_count > 1 else named[0]
    target = [named[:, FIELD_ROWS + q : FIELD_ROWS + q + 1] for q in range(pos_count)]
    member = jnp.where(
        lax.broadcasted_iota(jnp.int32, named.shape, 1) < FIELD_ROWS, named, 0.0
    ).astype(jnp.bfloat16)
    for start in range(0, labels, CHUNK):
        logits = lax.dot_general(
            x,
            w_ref[start : start + CHUNK, :],
            (((1,), (1,)), ((), ())),
            preferred_element_type=jnp.float32,
        )
        live = jnp.dot(
            member, live_ref[:, start : start + CHUNK], preferred_element_type=jnp.float32
        )
        label = (
            lax.broadcasted_iota(jnp.int32, (1, CHUNK), 1) + start
        ).astype(jnp.float32)
        positive = target[0] == label
        for q in range(1, pos_count):
            positive = positive | (target[q] == label)
        turned = jnp.where(positive, -1.0, 1.0)
        slope = (turned * live * jnp.maximum(1.0 + turned * logits, 0.0)).astype(jnp.bfloat16)
        for b, ref in enumerate(slope_refs):
            ref[:, start : start + CHUNK] = slope[b * rows : (b + 1) * rows]
    slope = [ref[...] for ref in slope_refs]
    slope = jnp.concatenate(slope, axis=0) if block_count > 1 else slope[0]
    for start in range(0, width, CHUNK):
        part = jnp.dot(
            slope, w_ref[:, start : start + CHUNK], preferred_element_type=jnp.float32
        ).astype(jnp.bfloat16)
        at = 0
        for ref in grad_refs:
            ref[:, start : start + CHUNK] = part[at : at + ref.shape[0]]
            at += ref.shape[0]


def block_work(blocks, weights, live_table, top_count, pos_count):
    labels, width = weights.shape
    piece_rows = [
        [piece.shape[0] - (FIELD_ROWS if p == 0 else 0) for p, piece in enumerate(pieces)]
        for pieces in blocks
    ]
    flat_rows = sum(piece_rows, [])
    half = sum(piece_rows[0]) // 2
    out = pl.pallas_call(
        functools.partial(block_kernel, piece_rows, top_count, pos_count),
        out_shape=[jax.ShapeDtypeStruct((half, width), jnp.bfloat16)] * (2 * len(blocks))
        + [jax.ShapeDtypeStruct((sum(rows), labels), jnp.bfloat16) for rows in piece_rows],
        in_specs=[pl.BlockSpec(memory_space=pltpu.VMEM)] * (len(flat_rows) + 2),
        compiler_params=pltpu.CompilerParams(vmem_limit_bytes=VMEM_LIMIT),
        cost_estimate=pl.CostEstimate(
            flops=4 * sum(flat_rows) * labels * width,
            bytes_accessed=2 * labels * width + 6 * sum(flat_rows) * width,
            transcendentals=0,
        ),
        name="block_work",
    )(*[piece for pieces in blocks for piece in pieces], weights, live_table)
    grads = [(out[2 * b], out[2 * b + 1]) for b in range(len(blocks))]
    return grads, list(out[2 * len(blocks) :])


def weight_kernel(piece_rows, column_blocks, scale, *refs):
    piece_count = len(piece_rows)
    out_refs = refs[len(refs) - len(column_blocks) :]
    x_refs, s_refs = refs[:piece_count], refs[piece_count : len(refs) - len(column_blocks)]
    part_width = out_refs[0].shape[1]
    slopes = jnp.concatenate([ref[...] for ref in s_refs], axis=0)
    for ref, q in zip(out_refs, column_blocks):
        at = pl.multiple_of((lax.axis_index("seq") ^ q) * part_width, part_width)
        x = jnp.concatenate(
            [r[:rows, pl.ds(at, part_width)] for r, rows in zip(x_refs, piece_rows)], axis=0
        )
        part = lax.dot_general(
            slopes, x, (((0,), (0,)), ((), ())), preferred_element_type=jnp.float32
        )
        ref[...] = (part * scale).astype(jnp.bfloat16)


def weight_work(blocks, slopes, column_blocks, part_width, scale):
    pieces = [piece for block in blocks for piece in block]
    piece_rows = [
        piece.shape[0] - (FIELD_ROWS if p == 0 else 0)
        for block in blocks
        for p, piece in enumerate(block)
    ]
    labels = slopes[0].shape[1]
    rows = sum(piece_rows)
    return pl.pallas_call(
        functools.partial(weight_kernel, piece_rows, column_blocks, scale),
        out_shape=[jax.ShapeDtypeStruct((labels, part_width), jnp.bfloat16)] * len(column_blocks),
        in_specs=[pl.BlockSpec(memory_space=pltpu.VMEM)] * (len(pieces) + len(slopes)),
        compiler_params=pltpu.CompilerParams(vmem_limit_bytes=VMEM_LIMIT),
        cost_estimate=pl.CostEstimate(
            flops=2 * rows * labels * part_width * len(column_blocks),
            bytes_accessed=2 * rows * (labels + 1024) + 2 * labels * part_width,
            transcendentals=0,
        ),
        name="weight_work",
    )(*pieces, *slopes)


def add(*parts):
    total = parts[0].astype(jnp.float32)
    for part in parts[1:]:
        total = total + part.astype(jnp.float32)
    return total.astype(jnp.bfloat16)


def after(array, *others):
    return lax.optimization_barrier((array, *others))[0]


def local(features, shortlist, positives, cluster_sizes, weights):
    inst_rows, width = features.shape
    top_count, pos_count = shortlist.shape[1], positives.shape[1]
    clus_count, seq_count = lax.axis_size("clus"), lax.axis_size("seq")
    local_count = cluster_sizes.shape[0]
    part_width = width // seq_count
    half, steps = inst_rows // 2, clus_count // 2

    ring = list(range(0, clus_count, 2)) + list(range(1, clus_count, 2))[::-1]
    up = list(zip(ring, ring[1:] + ring[:1]))
    down = [(b, a) for a, b in up]

    def send_up(array):
        return lax.ppermute(array, "clus", up)

    def send_down(array):
        return lax.ppermute(array, "clus", down)

    used, slopes = [], []

    def take(*blocks):
        grads, found = block_work(blocks, weights, live_table, top_count, pos_count)
        used.extend(blocks)
        slopes.extend(found)
        return grads

    own = pack(features, shortlist, positives)
    live_table = live_labels(cluster_sizes, weights)
    (own_grad,) = take([own])
    below, above = own, own
    below_grad, above_grad = {}, {}
    sum_up = sum_down = None

    def advance(j):
        nonlocal sum_up, sum_down
        first = below_grad[j][0] if j in below_grad else above_grad[clus_count - j][0]
        second = above_grad[j][1] if j in above_grad else below_grad[clus_count - j][1]
        if sum_up is not None:
            first, second = add(first, sum_up), add(second, sum_down)
        sum_up, sum_down = send_up(first), send_down(second)

    for k in range(1, steps + 1):
        if k > 1:
            before = own_grad[0] if k == 2 else below_grad[k - 2][0]
            below, above = after(below, before), after(above, before)
        if k < steps:
            arriving = send_up(below), send_down(above)
        else:
            ends = jnp.concatenate([below[:half], below[inst_rows:]], axis=0)
            opposite = [send_up(ends), send_down(above[half:inst_rows])]
        if k > 1:
            below_grad[k - 1], above_grad[k - 1] = take([below], [above])
            advance(k - 1)
        if k < steps:
            below, above = arriving
    (far_grad,) = take([after(opposite[0], below_grad[steps - 1][0]), opposite[1]])
    below_grad[steps] = above_grad[steps] = far_grad
    advance(steps)

    scale = 1.0 / math.sqrt(inst_rows * seq_count * top_count // local_count)

    def seq_send(array, bit):
        return lax.ppermute(array, "seq", [(k, k ^ bit) for k in range(seq_count)])

    far, near = list(range(seq_count // 2, seq_count)), list(range(seq_count // 2))
    terms = dict(zip(far, weight_work(used, slopes, far, part_width, scale)))
    sum_up, sum_down = after(sum_up, terms[far[0]]), after(sum_down, terms[far[0]])
    advance(steps + 1)
    terms.update(zip(near, weight_work(used, slopes, near, part_width, scale)))
    terms = {q: [term] for q, term in terms.items()}
    bit = 1
    while bit < seq_count:
        for q in [q for q in sorted(terms, reverse=True) if q & bit]:
            values = terms.pop(q)
            going = add(*values) if len(values) > 1 else values[0]
            if bit == 2:
                sum_up, sum_down = after(sum_up, going), after(sum_down, going)
            terms[q ^ bit].append(seq_send(going, bit))
        bit *= 2
    weight_grad = add(*terms[0])

    for j in range(steps + 2, clus_count):
        advance(j)
    feature_grad = jnp.concatenate(
        [add(after(own_grad[0], weight_grad), sum_up), add(own_grad[1], sum_down)], axis=0
    )
    return (feature_grad, weight_grad)


def solution(mesh):
    return jax.shard_map(
        local,
        mesh=mesh,
        in_specs=(
            P(("seq", "clus"), None),
            P(("seq", "clus"), None),
            P(("seq", "clus"), None),
            P("clus"),
            P("clus", None),
        ),
        out_specs=(P(("seq", "clus"), None), P("clus", "seq")),
        check_vma=False,
    )
```

```python
import functools
import math

import jax
import jax.numpy as jnp
from jax import lax
from jax.experimental import pallas as pl
from jax.experimental.pallas import tpu as pltpu
from jax.sharding import PartitionSpec as P

BLOCK = 128
LANES = 128
FIELD_ROWS = 8
CHUNK = 256
VMEM_LIMIT = 40 * 1024 * 1024


def ids_kernel(width, short_ref, pos_ref, out_ref):
    rows = short_ref.shape[1]
    short = short_ref[...]
    places = pos_ref[...] // BLOCK
    offsets = pos_ref[...] % BLOCK
    targets = jnp.zeros_like(places)
    for j in range(short.shape[0]):
        targets = targets + jnp.where(places == j, short[j : j + 1, :], 0)
    fields = jnp.concatenate([short, targets, offsets], axis=0)
    groups = [
        fields[at : at + FIELD_ROWS] for at in range(0, fields.shape[0], FIELD_ROWS)
    ]
    groups.append(jnp.zeros((FIELD_ROWS, width - rows * len(groups)), jnp.int32))
    meta = jnp.concatenate(groups, axis=1)
    out_ref[...] = meta.astype(jnp.float32).astype(jnp.bfloat16)


def instance_ids(shortlist, positives, width):
    return pl.pallas_call(
        functools.partial(ids_kernel, width),
        out_shape=jax.ShapeDtypeStruct((FIELD_ROWS, width), jnp.bfloat16),
        in_specs=[pl.BlockSpec(memory_space=pltpu.VMEM)] * 2,
        compiler_params=pltpu.CompilerParams(vmem_limit_bytes=VMEM_LIMIT),
        name="instance_ids",
    )(shortlist.T, positives.T)


def live_kernel(size_ref, live_ref):
    lane = lax.broadcasted_iota(jnp.int32, (LANES, BLOCK), 1)
    row = lax.broadcasted_iota(jnp.int32, (LANES, BLOCK), 0)
    for c in range(size_ref.shape[0]):
        live = jnp.where((row == c) & (lane < size_ref[c]), 2.0, 0.0)
        live_ref[:, c * BLOCK : (c + 1) * BLOCK] = live.astype(jnp.bfloat16)


def live_labels(cluster_sizes):
    return pl.pallas_call(
        live_kernel,
        out_shape=jax.ShapeDtypeStruct((LANES, cluster_sizes.shape[0] * BLOCK), jnp.bfloat16),
        in_specs=[pl.BlockSpec(memory_space=pltpu.SMEM)],
        compiler_params=pltpu.CompilerParams(vmem_limit_bytes=VMEM_LIMIT),
        name="live_labels",
    )(cluster_sizes)


def block_kernel(piece_rows, top_count, pos_count, *refs):
    block_count = len(piece_rows)
    piece_count = sum(len(pieces) for pieces in piece_rows)
    x_refs = refs[:piece_count]
    w_ref, live_ref = refs[piece_count : piece_count + 2]
    grad_refs = refs[piece_count + 2 : piece_count + 2 + 2 * block_count]
    slope_refs = refs[piece_count + 2 + 2 * block_count :]
    labels, width = w_ref.shape
    local_count = labels // BLOCK
    rows = slope_refs[0].shape[0]
    first = (lax.axis_index("clus") * local_count).astype(jnp.float32)

    named, pieces = [], []
    cluster = lax.broadcasted_iota(jnp.int32, (FIELD_ROWS, rows), 0).astype(jnp.float32) + first
    at = 0
    for b in range(block_count):
        block_refs = x_refs[at : at + len(piece_rows[b])]
        at += len(piece_rows[b])
        pieces += [ref[:count, :] for ref, count in zip(block_refs, piece_rows[b])]
        groups = -(-(top_count + 2 * pos_count) // FIELD_ROWS)
        meta = block_refs[0][piece_rows[b][0] :, : groups * rows].astype(jnp.float32)
        field = [
            meta[f % FIELD_ROWS : f % FIELD_ROWS + 1, f // FIELD_ROWS * rows : (f // FIELD_ROWS + 1) * rows]
            for f in range(top_count + 2 * pos_count)
        ]
        member = jnp.zeros((FIELD_ROWS, rows), jnp.float32)
        for j in range(top_count):
            member = jnp.where(cluster == field[j], 1.0, member)
        target = [
            (field[top_count + q] - first) * BLOCK + field[top_count + pos_count + q]
            for q in range(pos_count)
        ]
        rest = jnp.zeros((LANES - FIELD_ROWS - pos_count, rows), jnp.float32)
        named.append(jnp.concatenate([member] + target + [rest], axis=0).T)

    x = jnp.concatenate(pieces, axis=0) if len(pieces) > 1 else pieces[0]
    named = jnp.concatenate(named, axis=0) if block_count > 1 else named[0]
    target = [named[:, FIELD_ROWS + q : FIELD_ROWS + q + 1] for q in range(pos_count)]
    member = jnp.where(
        lax.broadcasted_iota(jnp.int32, named.shape, 1) < FIELD_ROWS, named, 0.0
    ).astype(jnp.bfloat16)
    for start in range(0, labels, CHUNK):
        logits = lax.dot_general(
            x,
            w_ref[start : start + CHUNK, :],
            (((1,), (1,)), ((), ())),
            preferred_element_type=jnp.float32,
        )
        live = jnp.dot(
            member, live_ref[:, start : start + CHUNK], preferred_element_type=jnp.float32
        )
        label = (
            lax.broadcasted_iota(jnp.int32, (1, CHUNK), 1) + start
        ).astype(jnp.float32)
        positive = target[0] == label
        for q in range(1, pos_count):
            positive = positive | (target[q] == label)
        turned = jnp.where(positive, -1.0, 1.0)
        slope = (turned * live * jnp.maximum(1.0 + turned * logits, 0.0)).astype(jnp.bfloat16)
        for b, ref in enumerate(slope_refs):
            ref[:, start : start + CHUNK] = slope[b * rows : (b + 1) * rows]
    slope = [ref[...] for ref in slope_refs]
    slope = jnp.concatenate(slope, axis=0) if block_count > 1 else slope[0]
    for start in range(0, width, CHUNK):
        part = jnp.dot(
            slope, w_ref[:, start : start + CHUNK], preferred_element_type=jnp.float32
        ).astype(jnp.bfloat16)
        at = 0
        for ref in grad_refs:
            ref[:, start : start + CHUNK] = part[at : at + ref.shape[0]]
            at += ref.shape[0]


def block_work(blocks, weights, live_table, top_count, pos_count):
    labels, width = weights.shape
    piece_rows = [
        [piece.shape[0] - (FIELD_ROWS if p == 0 else 0) for p, piece in enumerate(pieces)]
        for pieces in blocks
    ]
    flat_rows = sum(piece_rows, [])
    half = sum(piece_rows[0]) // 2
    out = pl.pallas_call(
        functools.partial(block_kernel, piece_rows, top_count, pos_count),
        out_shape=[jax.ShapeDtypeStruct((half, width), jnp.bfloat16)] * (2 * len(blocks))
        + [jax.ShapeDtypeStruct((sum(rows), labels), jnp.bfloat16) for rows in piece_rows],
        in_specs=[pl.BlockSpec(memory_space=pltpu.VMEM)] * (len(flat_rows) + 2),
        compiler_params=pltpu.CompilerParams(vmem_limit_bytes=VMEM_LIMIT),
        cost_estimate=pl.CostEstimate(
            flops=4 * sum(flat_rows) * labels * width,
            bytes_accessed=2 * labels * width + 6 * sum(flat_rows) * width,
            transcendentals=0,
        ),
        name="block_work",
    )(*[piece for pieces in blocks for piece in pieces], weights, live_table)
    grads = [(out[2 * b], out[2 * b + 1]) for b in range(len(blocks))]
    return grads, list(out[2 * len(blocks) :])


def weight_kernel(piece_rows, column_blocks, scale, *refs):
    piece_count = len(piece_rows)
    out_refs = refs[len(refs) - len(column_blocks) :]
    x_refs, s_refs = refs[:piece_count], refs[piece_count : len(refs) - len(column_blocks)]
    part_width = out_refs[0].shape[1]
    slopes = jnp.concatenate([ref[...] for ref in s_refs], axis=0)
    for ref, q in zip(out_refs, column_blocks):
        at = pl.multiple_of((lax.axis_index("seq") ^ q) * part_width, part_width)
        x = jnp.concatenate(
            [r[:rows, pl.ds(at, part_width)] for r, rows in zip(x_refs, piece_rows)], axis=0
        )
        part = lax.dot_general(
            slopes, x, (((0,), (0,)), ((), ())), preferred_element_type=jnp.float32
        )
        ref[...] = (part * scale).astype(jnp.bfloat16)


def weight_work(blocks, slopes, column_blocks, part_width, scale):
    pieces = [piece for block in blocks for piece in block]
    piece_rows = [
        piece.shape[0] - (FIELD_ROWS if p == 0 else 0)
        for block in blocks
        for p, piece in enumerate(block)
    ]
    labels = slopes[0].shape[1]
    rows = sum(piece_rows)
    return pl.pallas_call(
        functools.partial(weight_kernel, piece_rows, column_blocks, scale),
        out_shape=[jax.ShapeDtypeStruct((labels, part_width), jnp.bfloat16)] * len(column_blocks),
        in_specs=[pl.BlockSpec(memory_space=pltpu.VMEM)] * (len(pieces) + len(slopes)),
        compiler_params=pltpu.CompilerParams(vmem_limit_bytes=VMEM_LIMIT),
        cost_estimate=pl.CostEstimate(
            flops=2 * rows * labels * part_width * len(column_blocks),
            bytes_accessed=2 * rows * (labels + 1024) + 2 * labels * part_width,
            transcendentals=0,
        ),
        name="weight_work",
    )(*pieces, *slopes)


def add(*parts):
    total = parts[0].astype(jnp.float32)
    for part in parts[1:]:
        total = total + part.astype(jnp.float32)
    return total.astype(jnp.bfloat16)


def after(array, *others):
    return lax.optimization_barrier((array, *others))[0]


def local(features, shortlist, positives, cluster_sizes, weights):
    inst_rows, width = features.shape
    top_count, pos_count = shortlist.shape[1], positives.shape[1]
    clus_count, seq_count = lax.axis_size("clus"), lax.axis_size("seq")
    local_count = cluster_sizes.shape[0]
    part_width = width // seq_count
    half, steps = inst_rows // 2, clus_count // 2

    ring = list(range(0, clus_count, 2)) + list(range(1, clus_count, 2))[::-1]
    up = list(zip(ring, ring[1:] + ring[:1]))
    down = [(b, a) for a, b in up]

    def send_up(array):
        return lax.ppermute(array, "clus", up)

    def send_down(array):
        return lax.ppermute(array, "clus", down)

    used, slopes = [], []

    def take(*blocks):
        grads, found = block_work(blocks, weights, live_table, top_count, pos_count)
        used.extend(blocks)
        slopes.extend(found)
        return grads

    ids = instance_ids(shortlist, positives, width)
    live_table = live_labels(cluster_sizes)
    own = jnp.concatenate([features, ids], axis=0)
    below_grad, above_grad = {}, {}
    sum_up = sum_down = last_sent = None

    def advance(j):
        nonlocal sum_up, sum_down, last_sent
        first = below_grad[j][0] if j in below_grad else above_grad[clus_count - j][0]
        second = above_grad[j][1] if j in above_grad else below_grad[clus_count - j][1]
        if sum_up is not None:
            first, second = add(first, sum_up), add(second, sum_down)
        last_sent = first, second
        sum_up, sum_down = send_up(first), send_down(second)

    below, below_ids = send_up(features), send_up(ids)
    above, above_ids = send_down(features), send_down(ids)
    below = jnp.concatenate([below, below_ids], axis=0)
    above = jnp.concatenate([above, above_ids], axis=0)
    for k in range(2, steps + 1):
        if k > 2:
            before = below_grad[k - 2][0]
            below, above = after(below, before), after(above, before)
        if k < steps:
            arriving = send_up(below), send_down(above)
        else:
            ends = jnp.concatenate([below[:half], below[inst_rows:]], axis=0)
            opposite = [send_up(ends), send_down(above[half:inst_rows])]
        if k == 3 or steps < 3:
            below_grad[k - 1], above_grad[k - 1], own_grad = take([below], [above], [own])
        else:
            below_grad[k - 1], above_grad[k - 1] = take([below], [above])
        advance(k - 1)
        if k < steps:
            below, above = arriving
    (far_grad,) = take([after(opposite[0], below_grad[steps - 1][0]), opposite[1]])
    below_grad[steps] = above_grad[steps] = far_grad
    advance(steps)
    slopes[-1] = after(slopes[-1], *last_sent)

    scale = 1.0 / math.sqrt(inst_rows * seq_count * top_count // local_count)

    def seq_send(array, bit):
        return lax.ppermute(array, "seq", [(k, k ^ bit) for k in range(seq_count)])

    far, near = list(range(seq_count // 2, seq_count)), list(range(seq_count // 2))
    terms = dict(zip(far, weight_work(used, slopes, far, part_width, scale)))
    terms.update(zip(near, weight_work(used, slopes, near, part_width, scale)))
    sum_up, sum_down = after(sum_up, terms[near[0]]), after(sum_down, terms[near[0]])
    advance(steps + 1)
    terms = {q: [term] for q, term in terms.items()}
    bit = 1
    while bit < seq_count:
        for q in [q for q in sorted(terms, reverse=True) if q & bit]:
            values = terms.pop(q)
            going = add(*values) if len(values) > 1 else values[0]
            if bit == 2:
                sum_up, sum_down = after(sum_up, going), after(sum_down, going)
            terms[q ^ bit].append(seq_send(going, bit))
        bit *= 2
    weight_grad = add(*terms[0])

    for j in range(steps + 2, clus_count):
        advance(j)
    feature_grad = jnp.concatenate(
        [add(after(own_grad[0], weight_grad), sum_up), add(own_grad[1], sum_down)], axis=0
    )
    return (feature_grad, weight_grad)


def solution(mesh):
    return jax.shard_map(
        local,
        mesh=mesh,
        in_specs=(
            P(("seq", "clus"), None),
            P(("seq", "clus"), None),
            P(("seq", "clus"), None),
            P("clus"),
            P("clus", None),
        ),
        out_specs=(P(("seq", "clus"), None), P("clus", "seq")),
        check_vma=False,
    )
```

```python
import functools
import math

import jax
import jax.numpy as jnp
from jax import lax
from jax.experimental import pallas as pl
from jax.experimental.pallas import tpu as pltpu
from jax.sharding import PartitionSpec as P

BLOCK = 128
LANES = 128
FIELD_ROWS = 8
CHUNK = 256
VMEM_LIMIT = 40 * 1024 * 1024


def ids_kernel(width, short_ref, pos_ref, out_ref):
    rows = short_ref.shape[1]
    short = short_ref[...]
    places = pos_ref[...] // BLOCK
    offsets = pos_ref[...] % BLOCK
    targets = jnp.zeros_like(places)
    for j in range(short.shape[0]):
        targets = targets + jnp.where(places == j, short[j : j + 1, :], 0)
    fields = jnp.concatenate([short, targets, offsets], axis=0)
    groups = [
        fields[at : at + FIELD_ROWS] for at in range(0, fields.shape[0], FIELD_ROWS)
    ]
    groups.append(jnp.zeros((FIELD_ROWS, width - rows * len(groups)), jnp.int32))
    meta = jnp.concatenate(groups, axis=1)
    out_ref[...] = meta.astype(jnp.float32).astype(jnp.bfloat16)


def instance_ids(shortlist, positives, width):
    return pl.pallas_call(
        functools.partial(ids_kernel, width),
        out_shape=jax.ShapeDtypeStruct((FIELD_ROWS, width), jnp.bfloat16),
        in_specs=[pl.BlockSpec(memory_space=pltpu.VMEM)] * 2,
        compiler_params=pltpu.CompilerParams(vmem_limit_bytes=VMEM_LIMIT),
        name="instance_ids",
    )(shortlist.T, positives.T)


def live_kernel(size_ref, w_ref, live_ref):
    lane = lax.broadcasted_iota(jnp.int32, (LANES, BLOCK), 1)
    row = lax.broadcasted_iota(jnp.int32, (LANES, BLOCK), 0)
    for c in range(size_ref.shape[0]):
        live = jnp.where((row == c) & (lane < size_ref[c]), 2.0, 0.0)
        live_ref[:, c * BLOCK : (c + 1) * BLOCK] = live.astype(jnp.bfloat16)


def live_labels(cluster_sizes, weights):
    return pl.pallas_call(
        live_kernel,
        out_shape=jax.ShapeDtypeStruct((LANES, cluster_sizes.shape[0] * BLOCK), jnp.bfloat16),
        in_specs=[
            pl.BlockSpec(memory_space=pltpu.SMEM),
            pl.BlockSpec(memory_space=pltpu.VMEM),
        ],
        compiler_params=pltpu.CompilerParams(vmem_limit_bytes=VMEM_LIMIT),
        name="live_labels",
    )(cluster_sizes, weights)


def block_kernel(piece_rows, top_count, pos_count, *refs):
    block_count = len(piece_rows)
    piece_count = sum(len(pieces) for pieces in piece_rows)
    x_refs = refs[:piece_count]
    w_ref, live_ref = refs[piece_count : piece_count + 2]
    grad_refs = refs[piece_count + 2 : 2 * piece_count + 2]
    slope_refs = refs[2 * piece_count + 2 :]
    labels, width = w_ref.shape
    local_count = labels // BLOCK
    rows = slope_refs[0].shape[0]
    first = (lax.axis_index("clus") * local_count).astype(jnp.float32)

    named, pieces = [], []
    cluster = lax.broadcasted_iota(jnp.int32, (FIELD_ROWS, rows), 0).astype(jnp.float32) + first
    at = 0
    for b in range(block_count):
        block_refs = x_refs[at : at + len(piece_rows[b])]
        at += len(piece_rows[b])
        pieces += [ref[:count, :] for ref, count in zip(block_refs, piece_rows[b])]
        groups = -(-(top_count + 2 * pos_count) // FIELD_ROWS)
        meta = block_refs[0][piece_rows[b][0] :, : groups * rows].astype(jnp.float32)
        field = [
            meta[f % FIELD_ROWS : f % FIELD_ROWS + 1, f // FIELD_ROWS * rows : (f // FIELD_ROWS + 1) * rows]
            for f in range(top_count + 2 * pos_count)
        ]
        member = jnp.zeros((FIELD_ROWS, rows), jnp.float32)
        for j in range(top_count):
            member = jnp.where(cluster == field[j], 1.0, member)
        target = [
            (field[top_count + q] - first) * BLOCK + field[top_count + pos_count + q]
            for q in range(pos_count)
        ]
        rest = jnp.zeros((LANES - FIELD_ROWS - pos_count, rows), jnp.float32)
        named.append(jnp.concatenate([member] + target + [rest], axis=0).T)

    x = jnp.concatenate(pieces, axis=0) if len(pieces) > 1 else pieces[0]
    named = jnp.concatenate(named, axis=0) if block_count > 1 else named[0]
    target = [named[:, FIELD_ROWS + q : FIELD_ROWS + q + 1] for q in range(pos_count)]
    member = jnp.where(
        lax.broadcasted_iota(jnp.int32, named.shape, 1) < FIELD_ROWS, named, 0.0
    ).astype(jnp.bfloat16)
    for start in range(0, labels, CHUNK):
        logits = lax.dot_general(
            x,
            w_ref[start : start + CHUNK, :],
            (((1,), (1,)), ((), ())),
            preferred_element_type=jnp.float32,
        )
        live = jnp.dot(
            member, live_ref[:, start : start + CHUNK], preferred_element_type=jnp.float32
        )
        label = (
            lax.broadcasted_iota(jnp.int32, (1, CHUNK), 1) + start
        ).astype(jnp.float32)
        positive = target[0] == label
        for q in range(1, pos_count):
            positive = positive | (target[q] == label)
        turned = jnp.where(positive, -1.0, 1.0)
        slope = (turned * live * jnp.maximum(1.0 + turned * logits, 0.0)).astype(jnp.bfloat16)
        for b, ref in enumerate(slope_refs):
            ref[:, start : start + CHUNK] = slope[b * rows : (b + 1) * rows]
    slope = [ref[...] for ref in slope_refs]
    slope = jnp.concatenate(slope, axis=0) if block_count > 1 else slope[0]
    for start in range(0, width, CHUNK):
        part = jnp.dot(
            slope, w_ref[:, start : start + CHUNK], preferred_element_type=jnp.float32
        ).astype(jnp.bfloat16)
        at = 0
        for ref in grad_refs:
            ref[:, start : start + CHUNK] = part[at : at + ref.shape[0]]
            at += ref.shape[0]


def block_work(blocks, weights, live_table, top_count, pos_count):
    labels, width = weights.shape
    piece_rows = [
        [piece.shape[0] - (FIELD_ROWS if p == 0 else 0) for p, piece in enumerate(pieces)]
        for pieces in blocks
    ]
    flat_rows = sum(piece_rows, [])
    out = pl.pallas_call(
        functools.partial(block_kernel, piece_rows, top_count, pos_count),
        out_shape=[jax.ShapeDtypeStruct((rows, width), jnp.bfloat16) for rows in flat_rows]
        + [jax.ShapeDtypeStruct((sum(rows), labels), jnp.bfloat16) for rows in piece_rows],
        in_specs=[pl.BlockSpec(memory_space=pltpu.VMEM)] * (len(flat_rows) + 2),
        compiler_params=pltpu.CompilerParams(vmem_limit_bytes=VMEM_LIMIT),
        cost_estimate=pl.CostEstimate(
            flops=4 * sum(flat_rows) * labels * width,
            bytes_accessed=2 * labels * width + 6 * sum(flat_rows) * width,
            transcendentals=0,
        ),
        name="block_work",
    )(*[piece for pieces in blocks for piece in pieces], weights, live_table)
    return list(out[: len(flat_rows)]), list(out[len(flat_rows) :])


def weight_kernel(piece_rows, column_blocks, scale, *refs):
    piece_count = len(piece_rows)
    out_refs = refs[len(refs) - len(column_blocks) :]
    x_refs, s_refs = refs[:piece_count], refs[piece_count : len(refs) - len(column_blocks)]
    part_width = out_refs[0].shape[1]
    slopes = jnp.concatenate([ref[...] for ref in s_refs], axis=0)
    for ref, q in zip(out_refs, column_blocks):
        at = pl.multiple_of((lax.axis_index("seq") ^ q) * part_width, part_width)
        x = jnp.concatenate(
            [r[:rows, pl.ds(at, part_width)] for r, rows in zip(x_refs, piece_rows)], axis=0
        )
        part = lax.dot_general(
            slopes, x, (((0,), (0,)), ((), ())), preferred_element_type=jnp.float32
        )
        ref[...] = (part * scale).astype(jnp.bfloat16)


def weight_work(blocks, slopes, column_blocks, part_width, scale):
    pieces = [piece for block in blocks for piece in block]
    piece_rows = [
        piece.shape[0] - (FIELD_ROWS if p == 0 else 0)
        for block in blocks
        for p, piece in enumerate(block)
    ]
    labels = slopes[0].shape[1]
    rows = sum(piece_rows)
    return pl.pallas_call(
        functools.partial(weight_kernel, piece_rows, column_blocks, scale),
        out_shape=[jax.ShapeDtypeStruct((labels, part_width), jnp.bfloat16)] * len(column_blocks),
        in_specs=[pl.BlockSpec(memory_space=pltpu.VMEM)] * (len(pieces) + len(slopes)),
        compiler_params=pltpu.CompilerParams(vmem_limit_bytes=VMEM_LIMIT),
        cost_estimate=pl.CostEstimate(
            flops=2 * rows * labels * part_width * len(column_blocks),
            bytes_accessed=2 * rows * (labels + 1024) + 2 * labels * part_width,
            transcendentals=0,
        ),
        name="weight_work",
    )(*pieces, *slopes)


def add(*parts):
    total = parts[0].astype(jnp.float32)
    for part in parts[1:]:
        total = total + part.astype(jnp.float32)
    return total.astype(jnp.bfloat16)


def after(array, *others):
    return lax.optimization_barrier((array, *others))[0]


def local(features, shortlist, positives, cluster_sizes, weights):
    inst_rows, width = features.shape
    top_count, pos_count = shortlist.shape[1], positives.shape[1]
    clus_count, seq_count = lax.axis_size("clus"), lax.axis_size("seq")
    local_count = cluster_sizes.shape[0]
    part_width = width // seq_count
    half, steps = inst_rows // 2, clus_count // 2

    ring = list(range(0, clus_count, 2)) + list(range(1, clus_count, 2))[::-1]
    up = list(zip(ring, ring[1:] + ring[:1]))
    down = [(b, a) for a, b in up]

    def send_up(array):
        return lax.ppermute(array, "clus", up)

    def send_down(array):
        return lax.ppermute(array, "clus", down)

    used, slopes = [], []

    def take(*blocks):
        grads, found = block_work(blocks, weights, live_table, top_count, pos_count)
        used.extend(blocks)
        slopes.extend(found)
        return grads

    ids = instance_ids(shortlist, positives, width)
    live_table = live_labels(cluster_sizes, weights)
    own = jnp.concatenate([features, ids], axis=0)
    below, below_ids = send_up(features), send_up(ids)
    above, above_ids = send_down(features), send_down(ids)
    below = jnp.concatenate([after(below, live_table), below_ids], axis=0)
    above = jnp.concatenate([after(above, live_table), above_ids], axis=0)
    below_grad, above_grad = {}, {}
    for k in range(2, steps + 1):
        if k > 2:
            before = below_grad[k - 2]
            below, above = after(below, before), after(above, before)
        if k < steps:
            arriving = send_up(below), send_down(above)
        else:
            ends = jnp.concatenate([below[:half], below[inst_rows:]], axis=0)
            arriving = send_up(ends), send_down(above[half:inst_rows])
        if k == 3 or steps < 3:
            below_grad[k - 1], above_grad[k - 1], own_grad = take([below], [above], [own])
        else:
            below_grad[k - 1], above_grad[k - 1] = take([below], [above])
        below, above = arriving
    to_down, to_up = take([after(below, below_grad[steps - 1]), above])

    scale = 1.0 / math.sqrt(inst_rows * seq_count * top_count // local_count)

    def seq_send(array, bit):
        return lax.ppermute(array, "seq", [(k, k ^ bit) for k in range(seq_count)])

    far, near = list(range(seq_count // 2, seq_count)), list(range(seq_count // 2))
    terms = dict(zip(far, weight_work(used, slopes, far, part_width, scale)))
    terms.update(zip(near, weight_work(used, slopes, near, part_width, scale)))
    terms = {q: [term] for q, term in terms.items()}
    bit = 1
    while bit < seq_count:
        for q in [q for q in sorted(terms, reverse=True) if q & bit]:
            values = terms.pop(q)
            terms[q ^ bit].append(seq_send(add(*values) if len(values) > 1 else values[0], bit))
        bit *= 2

    for k in range(steps, 0, -1):
        from_above, from_below = send_down(to_down), send_up(to_up)
        if k == steps:
            near_below, near_above = below_grad[k - 1], above_grad[k - 1]
            to_down = jnp.concatenate([add(near_below[:half], from_above), near_below[half:]], axis=0)
            to_up = jnp.concatenate([near_above[:half], add(near_above[half:], from_below)], axis=0)
        elif k > 1:
            to_down, to_up = add(below_grad[k - 1], from_above), add(above_grad[k - 1], from_below)
    weight_grad = add(*terms[0])
    feature_grad = add(after(own_grad, weight_grad), from_above, from_below)
    return (feature_grad, weight_grad)


def solution(mesh):
    return jax.shard_map(
        local,
        mesh=mesh,
        in_specs=(
            P(("seq", "clus"), None),
            P(("seq", "clus"), None),
            P(("seq", "clus"), None),
            P("clus"),
            P("clus", None),
        ),
        out_specs=(P(("seq", "clus"), None), P("clus", "seq")),
        check_vma=False,
    )
```

```python
import functools
import math

import jax
import jax.numpy as jnp
from jax import lax
from jax.experimental import pallas as pl
from jax.experimental.pallas import tpu as pltpu
from jax.sharding import PartitionSpec as P

BLOCK = 128
LANES = 128
FIELD_ROWS = 8
CHUNK = 256
VMEM_LIMIT = 40 * 1024 * 1024


def ids_kernel(width, short_ref, pos_ref, out_ref):
    rows = short_ref.shape[1]
    short = short_ref[...]
    places = pos_ref[...] // BLOCK
    offsets = pos_ref[...] % BLOCK
    targets = jnp.zeros_like(places)
    for j in range(short.shape[0]):
        targets = targets + jnp.where(places == j, short[j : j + 1, :], 0)
    fields = jnp.concatenate([short, targets, offsets], axis=0)
    groups = [
        fields[at : at + FIELD_ROWS] for at in range(0, fields.shape[0], FIELD_ROWS)
    ]
    groups.append(jnp.zeros((FIELD_ROWS, width - rows * len(groups)), jnp.int32))
    meta = jnp.concatenate(groups, axis=1)
    out_ref[...] = meta.astype(jnp.float32).astype(jnp.bfloat16)


def instance_ids(shortlist, positives, width):
    return pl.pallas_call(
        functools.partial(ids_kernel, width),
        out_shape=jax.ShapeDtypeStruct((FIELD_ROWS, width), jnp.bfloat16),
        in_specs=[pl.BlockSpec(memory_space=pltpu.VMEM)] * 2,
        compiler_params=pltpu.CompilerParams(vmem_limit_bytes=VMEM_LIMIT),
        name="instance_ids",
    )(shortlist.T, positives.T)


def live_kernel(size_ref, w_ref, live_ref):
    lane = lax.broadcasted_iota(jnp.int32, (LANES, BLOCK), 1)
    row = lax.broadcasted_iota(jnp.int32, (LANES, BLOCK), 0)
    for c in range(size_ref.shape[0]):
        live = jnp.where((row == c) & (lane < size_ref[c]), 2.0, 0.0)
        live_ref[:, c * BLOCK : (c + 1) * BLOCK] = live.astype(jnp.bfloat16)


def live_labels(cluster_sizes, weights):
    return pl.pallas_call(
        live_kernel,
        out_shape=jax.ShapeDtypeStruct((LANES, cluster_sizes.shape[0] * BLOCK), jnp.bfloat16),
        in_specs=[
            pl.BlockSpec(memory_space=pltpu.SMEM),
            pl.BlockSpec(memory_space=pltpu.VMEM),
        ],
        compiler_params=pltpu.CompilerParams(vmem_limit_bytes=VMEM_LIMIT),
        name="live_labels",
    )(cluster_sizes, weights)


def block_kernel(piece_rows, top_count, pos_count, *refs):
    block_count = len(piece_rows)
    piece_count = sum(len(pieces) for pieces in piece_rows)
    x_refs = refs[:piece_count]
    w_ref, live_ref = refs[piece_count : piece_count + 2]
    grad_refs = refs[piece_count + 2 : piece_count + 2 + 2 * block_count]
    slope_refs = refs[piece_count + 2 + 2 * block_count :]
    labels, width = w_ref.shape
    local_count = labels // BLOCK
    rows = slope_refs[0].shape[0]
    first = (lax.axis_index("clus") * local_count).astype(jnp.float32)

    named, pieces = [], []
    cluster = lax.broadcasted_iota(jnp.int32, (FIELD_ROWS, rows), 0).astype(jnp.float32) + first
    at = 0
    for b in range(block_count):
        block_refs = x_refs[at : at + len(piece_rows[b])]
        at += len(piece_rows[b])
        pieces += [ref[:count, :] for ref, count in zip(block_refs, piece_rows[b])]
        groups = -(-(top_count + 2 * pos_count) // FIELD_ROWS)
        meta = block_refs[0][piece_rows[b][0] :, : groups * rows].astype(jnp.float32)
        field = [
            meta[f % FIELD_ROWS : f % FIELD_ROWS + 1, f // FIELD_ROWS * rows : (f // FIELD_ROWS + 1) * rows]
            for f in range(top_count + 2 * pos_count)
        ]
        member = jnp.zeros((FIELD_ROWS, rows), jnp.float32)
        for j in range(top_count):
            member = jnp.where(cluster == field[j], 1.0, member)
        target = [
            (field[top_count + q] - first) * BLOCK + field[top_count + pos_count + q]
            for q in range(pos_count)
        ]
        rest = jnp.zeros((LANES - FIELD_ROWS - pos_count, rows), jnp.float32)
        named.append(jnp.concatenate([member] + target + [rest], axis=0).T)

    x = jnp.concatenate(pieces, axis=0) if len(pieces) > 1 else pieces[0]
    named = jnp.concatenate(named, axis=0) if block_count > 1 else named[0]
    target = [named[:, FIELD_ROWS + q : FIELD_ROWS + q + 1] for q in range(pos_count)]
    member = jnp.where(
        lax.broadcasted_iota(jnp.int32, named.shape, 1) < FIELD_ROWS, named, 0.0
    ).astype(jnp.bfloat16)
    for start in range(0, labels, CHUNK):
        logits = lax.dot_general(
            x,
            w_ref[start : start + CHUNK, :],
            (((1,), (1,)), ((), ())),
            preferred_element_type=jnp.float32,
        )
        live = jnp.dot(
            member, live_ref[:, start : start + CHUNK], preferred_element_type=jnp.float32
        )
        label = (
            lax.broadcasted_iota(jnp.int32, (1, CHUNK), 1) + start
        ).astype(jnp.float32)
        positive = target[0] == label
        for q in range(1, pos_count):
            positive = positive | (target[q] == label)
        turned = jnp.where(positive, -1.0, 1.0)
        slope = (turned * live * jnp.maximum(1.0 + turned * logits, 0.0)).astype(jnp.bfloat16)
        for b, ref in enumerate(slope_refs):
            ref[:, start : start + CHUNK] = slope[b * rows : (b + 1) * rows]
    slope = [ref[...] for ref in slope_refs]
    slope = jnp.concatenate(slope, axis=0) if block_count > 1 else slope[0]
    for start in range(0, width, CHUNK):
        part = jnp.dot(
            slope, w_ref[:, start : start + CHUNK], preferred_element_type=jnp.float32
        ).astype(jnp.bfloat16)
        at = 0
        for ref in grad_refs:
            ref[:, start : start + CHUNK] = part[at : at + ref.shape[0]]
            at += ref.shape[0]


def block_work(blocks, weights, live_table, top_count, pos_count):
    labels, width = weights.shape
    piece_rows = [
        [piece.shape[0] - (FIELD_ROWS if p == 0 else 0) for p, piece in enumerate(pieces)]
        for pieces in blocks
    ]
    flat_rows = sum(piece_rows, [])
    half = sum(piece_rows[0]) // 2
    out = pl.pallas_call(
        functools.partial(block_kernel, piece_rows, top_count, pos_count),
        out_shape=[jax.ShapeDtypeStruct((half, width), jnp.bfloat16)] * (2 * len(blocks))
        + [jax.ShapeDtypeStruct((sum(rows), labels), jnp.bfloat16) for rows in piece_rows],
        in_specs=[pl.BlockSpec(memory_space=pltpu.VMEM)] * (len(flat_rows) + 2),
        compiler_params=pltpu.CompilerParams(vmem_limit_bytes=VMEM_LIMIT),
        cost_estimate=pl.CostEstimate(
            flops=4 * sum(flat_rows) * labels * width,
            bytes_accessed=2 * labels * width + 6 * sum(flat_rows) * width,
            transcendentals=0,
        ),
        name="block_work",
    )(*[piece for pieces in blocks for piece in pieces], weights, live_table)
    grads = [(out[2 * b], out[2 * b + 1]) for b in range(len(blocks))]
    return grads, list(out[2 * len(blocks) :])


def weight_kernel(piece_rows, column_blocks, scale, *refs):
    piece_count = len(piece_rows)
    out_refs = refs[len(refs) - len(column_blocks) :]
    x_refs, s_refs = refs[:piece_count], refs[piece_count : len(refs) - len(column_blocks)]
    part_width = out_refs[0].shape[1]
    slopes = jnp.concatenate([ref[...] for ref in s_refs], axis=0)
    for ref, q in zip(out_refs, column_blocks):
        at = pl.multiple_of((lax.axis_index("seq") ^ q) * part_width, part_width)
        x = jnp.concatenate(
            [r[:rows, pl.ds(at, part_width)] for r, rows in zip(x_refs, piece_rows)], axis=0
        )
        part = lax.dot_general(
            slopes, x, (((0,), (0,)), ((), ())), preferred_element_type=jnp.float32
        )
        ref[...] = (part * scale).astype(jnp.bfloat16)


def weight_work(blocks, slopes, column_blocks, part_width, scale):
    pieces = [piece for block in blocks for piece in block]
    piece_rows = [
        piece.shape[0] - (FIELD_ROWS if p == 0 else 0)
        for block in blocks
        for p, piece in enumerate(block)
    ]
    labels = slopes[0].shape[1]
    rows = sum(piece_rows)
    return pl.pallas_call(
        functools.partial(weight_kernel, piece_rows, column_blocks, scale),
        out_shape=[jax.ShapeDtypeStruct((labels, part_width), jnp.bfloat16)] * len(column_blocks),
        in_specs=[pl.BlockSpec(memory_space=pltpu.VMEM)] * (len(pieces) + len(slopes)),
        compiler_params=pltpu.CompilerParams(vmem_limit_bytes=VMEM_LIMIT),
        cost_estimate=pl.CostEstimate(
            flops=2 * rows * labels * part_width * len(column_blocks),
            bytes_accessed=2 * rows * (labels + 1024) + 2 * labels * part_width,
            transcendentals=0,
        ),
        name="weight_work",
    )(*pieces, *slopes)


def add(*parts):
    total = parts[0].astype(jnp.float32)
    for part in parts[1:]:
        total = total + part.astype(jnp.float32)
    return total.astype(jnp.bfloat16)


def sum_kernel(*refs):
    total = refs[0][...].astype(jnp.float32)
    for ref in refs[1:-1]:
        total = total + ref[...].astype(jnp.float32)
    refs[-1][...] = total.astype(jnp.bfloat16)


def weight_sum(parts):
    return pl.pallas_call(
        sum_kernel,
        out_shape=jax.ShapeDtypeStruct(parts[0].shape, jnp.bfloat16),
        in_specs=[pl.BlockSpec(memory_space=pltpu.VMEM)] * len(parts),
        compiler_params=pltpu.CompilerParams(vmem_limit_bytes=VMEM_LIMIT),
        cost_estimate=pl.CostEstimate(
            flops=8_000_000_000, bytes_accessed=2 * parts[0].size * (len(parts) + 1), transcendentals=0
        ),
        name="weight_sum",
    )(*parts)


def after(array, *others):
    return lax.optimization_barrier((array, *others))[0]


def local(features, shortlist, positives, cluster_sizes, weights):
    inst_rows, width = features.shape
    top_count, pos_count = shortlist.shape[1], positives.shape[1]
    clus_count, seq_count = lax.axis_size("clus"), lax.axis_size("seq")
    local_count = cluster_sizes.shape[0]
    part_width = width // seq_count
    half, steps = inst_rows // 2, clus_count // 2

    ring = list(range(0, clus_count, 2)) + list(range(1, clus_count, 2))[::-1]
    up = list(zip(ring, ring[1:] + ring[:1]))
    down = [(b, a) for a, b in up]

    def send_up(array):
        return lax.ppermute(array, "clus", up)

    def send_down(array):
        return lax.ppermute(array, "clus", down)

    used, slopes = [], []

    def take(*blocks):
        grads, found = block_work(blocks, weights, live_table, top_count, pos_count)
        used.extend(blocks)
        slopes.extend(found)
        return grads

    ids = instance_ids(shortlist, positives, width)
    live_table = live_labels(cluster_sizes, weights)
    own = jnp.concatenate([features, ids], axis=0)
    below, below_ids = send_up(features), send_up(ids)
    above, above_ids = send_down(features), send_down(ids)
    below = jnp.concatenate([after(below, live_table), below_ids], axis=0)
    above = jnp.concatenate([after(above, live_table), above_ids], axis=0)
    below_grad, above_grad = {}, {}
    for k in range(2, steps + 1):
        if k > 2:
            before = below_grad[k - 2][0]
            below, above = after(below, before), after(above, before)
        if k < steps:
            arriving = send_up(below), send_down(above)
        else:
            ends = jnp.concatenate([below[:half], below[inst_rows:]], axis=0)
            arriving = send_up(ends), send_down(above[half:inst_rows])
        if k == 3 or steps < 3:
            below_grad[k - 1], above_grad[k - 1], own_grad = take([below], [above], [own])
        else:
            below_grad[k - 1], above_grad[k - 1] = take([below], [above])
        below, above = arriving
    last = steps - 1
    early_above, early_below = send_down(below_grad[last][1]), send_up(above_grad[last][0])
    (opposite,) = take([after(below, below_grad[last][0]), above])
    from_above, from_below = send_down(opposite[0]), send_up(opposite[1])
    slopes[-1] = after(slopes[-1], *opposite)
    early_above, early_below = after(early_above, opposite[0]), after(early_below, opposite[0])

    scale = 1.0 / math.sqrt(inst_rows * seq_count * top_count // local_count)

    far, near = list(range(seq_count // 2, seq_count)), list(range(seq_count // 2))
    terms, arrived = {}, {}

    def weigh(slots):
        parts = weight_work(used, slopes, slots, part_width, scale)
        terms.update({q: [part] for q, part in zip(slots, parts)})
        return parts[0]

    def halve(bit, slots):
        for q in slots:
            values = terms.pop(q) + arrived.pop(q, [])
            going = add(*values) if len(values) > 1 else values[0]
            sent = lax.ppermute(going, "seq", [(k, k ^ bit) for k in range(seq_count)])
            arrived.setdefault(q ^ bit, []).append(sent)
        return going

    weigh(far)
    halve(1, far[1::2])
    passed = weigh(near)
    halve(1, near[1::2])
    for level in range(last, 0, -1):
        to_down = add(below_grad[level][0], from_above)
        to_up = add(above_grad[level][1], from_below)
        if level > 1:
            to_down = jnp.concatenate([to_down, add(below_grad[level - 1][1], early_above)], axis=0)
            to_up = jnp.concatenate([to_up, add(above_grad[level - 1][0], early_below)], axis=0)
        if level == last:
            bit = 2
            while bit < seq_count:
                going = halve(bit, [q for q in sorted(terms, reverse=True) if q & bit])
                bit *= 2
            to_down, to_up = after(to_down, passed), after(to_up, going)
        if level == 1:
            early_above, early_below = after(early_above, to_down, to_up), after(early_below, to_down, to_up)
        got_above, got_below = send_down(to_down), send_up(to_up)
        from_above, from_below = got_above[:half], got_below[:half]
        if level > 1:
            early_above, early_below = got_above[half:], got_below[half:]
    weight_grad = weight_sum(terms[0] + arrived[0])
    feature_grad = jnp.concatenate(
        [
            add(after(own_grad[0], weight_grad), from_above, early_below),
            add(after(own_grad[1], weight_grad), early_above, from_below),
        ],
        axis=0,
    )
    return (feature_grad, weight_grad)


def solution(mesh):
    return jax.shard_map(
        local,
        mesh=mesh,
        in_specs=(
            P(("seq", "clus"), None),
            P(("seq", "clus"), None),
            P(("seq", "clus"), None),
            P("clus"),
            P("clus", None),
        ),
        out_specs=(P(("seq", "clus"), None), P("clus", "seq")),
        check_vma=False,
    )
```

```python
import functools
import math

import jax
import jax.numpy as jnp
from jax import lax
from jax.experimental import pallas as pl
from jax.experimental.pallas import tpu as pltpu
from jax.sharding import PartitionSpec as P

BLOCK = 128
LANES = 128
FIELD_ROWS = 8
CHUNK = 256
VMEM_LIMIT = 40 * 1024 * 1024


def ids_kernel(width, short_ref, pos_ref, out_ref):
    rows = short_ref.shape[1]
    short = short_ref[...]
    places = pos_ref[...] // BLOCK
    offsets = pos_ref[...] % BLOCK
    targets = jnp.zeros_like(places)
    for j in range(short.shape[0]):
        targets = targets + jnp.where(places == j, short[j : j + 1, :], 0)
    fields = jnp.concatenate([short, targets, offsets], axis=0)
    groups = [
        fields[at : at + FIELD_ROWS] for at in range(0, fields.shape[0], FIELD_ROWS)
    ]
    groups.append(jnp.zeros((FIELD_ROWS, width - rows * len(groups)), jnp.int32))
    meta = jnp.concatenate(groups, axis=1)
    out_ref[...] = meta.astype(jnp.float32).astype(jnp.bfloat16)


def instance_ids(shortlist, positives, width):
    return pl.pallas_call(
        functools.partial(ids_kernel, width),
        out_shape=jax.ShapeDtypeStruct((FIELD_ROWS, width), jnp.bfloat16),
        in_specs=[pl.BlockSpec(memory_space=pltpu.VMEM)] * 2,
        compiler_params=pltpu.CompilerParams(vmem_limit_bytes=VMEM_LIMIT),
        name="instance_ids",
    )(shortlist.T, positives.T)


def live_kernel(size_ref, w_ref, live_ref):
    lane = lax.broadcasted_iota(jnp.int32, (LANES, BLOCK), 1)
    row = lax.broadcasted_iota(jnp.int32, (LANES, BLOCK), 0)
    for c in range(size_ref.shape[0]):
        live = jnp.where((row == c) & (lane < size_ref[c]), 2.0, 0.0)
        live_ref[:, c * BLOCK : (c + 1) * BLOCK] = live.astype(jnp.bfloat16)


def live_labels(cluster_sizes, weights):
    return pl.pallas_call(
        live_kernel,
        out_shape=jax.ShapeDtypeStruct((LANES, cluster_sizes.shape[0] * BLOCK), jnp.bfloat16),
        in_specs=[
            pl.BlockSpec(memory_space=pltpu.SMEM),
            pl.BlockSpec(memory_space=pltpu.VMEM),
        ],
        compiler_params=pltpu.CompilerParams(vmem_limit_bytes=VMEM_LIMIT),
        name="live_labels",
    )(cluster_sizes, weights)


def block_kernel(piece_rows, top_count, pos_count, *refs):
    block_count = len(piece_rows)
    piece_count = sum(len(pieces) for pieces in piece_rows)
    x_refs = refs[:piece_count]
    w_ref, live_ref = refs[piece_count : piece_count + 2]
    grad_refs = refs[piece_count + 2 : 2 * piece_count + 2]
    slope_refs = refs[2 * piece_count + 2 :]
    labels, width = w_ref.shape
    local_count = labels // BLOCK
    rows = slope_refs[0].shape[0]
    first = (lax.axis_index("clus") * local_count).astype(jnp.float32)

    named, pieces = [], []
    cluster = lax.broadcasted_iota(jnp.int32, (FIELD_ROWS, rows), 0).astype(jnp.float32) + first
    at = 0
    for b in range(block_count):
        block_refs = x_refs[at : at + len(piece_rows[b])]
        at += len(piece_rows[b])
        pieces += [ref[:count, :] for ref, count in zip(block_refs, piece_rows[b])]
        groups = -(-(top_count + 2 * pos_count) // FIELD_ROWS)
        meta = block_refs[0][piece_rows[b][0] :, : groups * rows].astype(jnp.float32)
        field = [
            meta[f % FIELD_ROWS : f % FIELD_ROWS + 1, f // FIELD_ROWS * rows : (f // FIELD_ROWS + 1) * rows]
            for f in range(top_count + 2 * pos_count)
        ]
        member = jnp.zeros((FIELD_ROWS, rows), jnp.float32)
        for j in range(top_count):
            member = jnp.where(cluster == field[j], 1.0, member)
        target = [
            (field[top_count + q] - first) * BLOCK + field[top_count + pos_count + q]
            for q in range(pos_count)
        ]
        rest = jnp.zeros((LANES - FIELD_ROWS - pos_count, rows), jnp.float32)
        named.append(jnp.concatenate([member] + target + [rest], axis=0).T)

    x = jnp.concatenate(pieces, axis=0) if len(pieces) > 1 else pieces[0]
    named = jnp.concatenate(named, axis=0) if block_count > 1 else named[0]
    target = [named[:, FIELD_ROWS + q : FIELD_ROWS + q + 1] for q in range(pos_count)]
    member = jnp.where(
        lax.broadcasted_iota(jnp.int32, named.shape, 1) < FIELD_ROWS, named, 0.0
    ).astype(jnp.bfloat16)
    for start in range(0, labels, CHUNK):
        logits = lax.dot_general(
            x,
            w_ref[start : start + CHUNK, :],
            (((1,), (1,)), ((), ())),
            preferred_element_type=jnp.float32,
        )
        live = jnp.dot(
            member, live_ref[:, start : start + CHUNK], preferred_element_type=jnp.float32
        )
        label = (
            lax.broadcasted_iota(jnp.int32, (1, CHUNK), 1) + start
        ).astype(jnp.float32)
        positive = target[0] == label
        for q in range(1, pos_count):
            positive = positive | (target[q] == label)
        turned = jnp.where(positive, -1.0, 1.0)
        slope = (turned * live * jnp.maximum(1.0 + turned * logits, 0.0)).astype(jnp.bfloat16)
        for b, ref in enumerate(slope_refs):
            ref[:, start : start + CHUNK] = slope[b * rows : (b + 1) * rows]
    slope = [ref[...] for ref in slope_refs]
    slope = jnp.concatenate(slope, axis=0) if block_count > 1 else slope[0]
    for start in range(0, width, CHUNK):
        part = jnp.dot(
            slope, w_ref[:, start : start + CHUNK], preferred_element_type=jnp.float32
        ).astype(jnp.bfloat16)
        at = 0
        for ref in grad_refs:
            ref[:, start : start + CHUNK] = part[at : at + ref.shape[0]]
            at += ref.shape[0]


def block_work(blocks, weights, live_table, top_count, pos_count):
    labels, width = weights.shape
    piece_rows = [
        [piece.shape[0] - (FIELD_ROWS if p == 0 else 0) for p, piece in enumerate(pieces)]
        for pieces in blocks
    ]
    flat_rows = sum(piece_rows, [])
    out = pl.pallas_call(
        functools.partial(block_kernel, piece_rows, top_count, pos_count),
        out_shape=[jax.ShapeDtypeStruct((rows, width), jnp.bfloat16) for rows in flat_rows]
        + [jax.ShapeDtypeStruct((sum(rows), labels), jnp.bfloat16) for rows in piece_rows],
        in_specs=[pl.BlockSpec(memory_space=pltpu.VMEM)] * (len(flat_rows) + 2),
        compiler_params=pltpu.CompilerParams(vmem_limit_bytes=VMEM_LIMIT),
        cost_estimate=pl.CostEstimate(
            flops=4 * sum(flat_rows) * labels * width,
            bytes_accessed=2 * labels * width + 6 * sum(flat_rows) * width,
            transcendentals=0,
        ),
        name="block_work",
    )(*[piece for pieces in blocks for piece in pieces], weights, live_table)
    return list(out[: len(flat_rows)]), list(out[len(flat_rows) :])


def weight_kernel(piece_rows, column_blocks, scale, *refs):
    piece_count = len(piece_rows)
    out_refs = refs[len(refs) - len(column_blocks) :]
    x_refs, s_refs = refs[:piece_count], refs[piece_count : len(refs) - len(column_blocks)]
    part_width = out_refs[0].shape[1]
    slopes = jnp.concatenate([ref[...] for ref in s_refs], axis=0)
    for ref, q in zip(out_refs, column_blocks):
        at = pl.multiple_of((lax.axis_index("seq") ^ q) * part_width, part_width)
        x = jnp.concatenate(
            [r[:rows, pl.ds(at, part_width)] for r, rows in zip(x_refs, piece_rows)], axis=0
        )
        part = lax.dot_general(
            slopes, x, (((0,), (0,)), ((), ())), preferred_element_type=jnp.float32
        )
        ref[...] = (part * scale).astype(jnp.bfloat16)


def weight_work(blocks, slopes, column_blocks, part_width, scale):
    pieces = [piece for block in blocks for piece in block]
    piece_rows = [
        piece.shape[0] - (FIELD_ROWS if p == 0 else 0)
        for block in blocks
        for p, piece in enumerate(block)
    ]
    labels = slopes[0].shape[1]
    rows = sum(piece_rows)
    return pl.pallas_call(
        functools.partial(weight_kernel, piece_rows, column_blocks, scale),
        out_shape=[jax.ShapeDtypeStruct((labels, part_width), jnp.bfloat16)] * len(column_blocks),
        in_specs=[pl.BlockSpec(memory_space=pltpu.VMEM)] * (len(pieces) + len(slopes)),
        compiler_params=pltpu.CompilerParams(vmem_limit_bytes=VMEM_LIMIT),
        cost_estimate=pl.CostEstimate(
            flops=2 * rows * labels * part_width * len(column_blocks),
            bytes_accessed=2 * rows * (labels + 1024) + 2 * labels * part_width,
            transcendentals=0,
        ),
        name="weight_work",
    )(*pieces, *slopes)


def add(*parts):
    total = parts[0].astype(jnp.float32)
    for part in parts[1:]:
        total = total + part.astype(jnp.float32)
    return total.astype(jnp.bfloat16)


def after(array, *others):
    return lax.optimization_barrier((array, *others))[0]


def local(features, shortlist, positives, cluster_sizes, weights):
    inst_rows, width = features.shape
    top_count, pos_count = shortlist.shape[1], positives.shape[1]
    clus_count, seq_count = lax.axis_size("clus"), lax.axis_size("seq")
    local_count = cluster_sizes.shape[0]
    part_width = width // seq_count
    half, steps = inst_rows // 2, clus_count // 2

    ring = list(range(0, clus_count, 2)) + list(range(1, clus_count, 2))[::-1]
    up = []
    for s in range(seq_count):
        places = [s * clus_count + c for c in (ring if s % 2 == 0 else ring[::-1])]
        up += list(zip(places, places[1:] + places[:1]))
    down = [(b, a) for a, b in up]

    def send_up(array):
        return lax.ppermute(array, ("seq", "clus"), up)

    def send_down(array):
        return lax.ppermute(array, ("seq", "clus"), down)

    used, slopes = [], []

    def take(*blocks):
        grads, found = block_work(blocks, weights, live_table, top_count, pos_count)
        used.extend(blocks)
        slopes.extend(found)
        return grads

    ids = instance_ids(shortlist, positives, width)
    live_table = live_labels(cluster_sizes, weights)
    own = jnp.concatenate([features, ids], axis=0)
    below, below_ids = send_up(features), send_up(ids)
    above, above_ids = send_down(after(features, live_table)), send_down(ids)
    below = jnp.concatenate([below, below_ids], axis=0)
    above = jnp.concatenate([above, above_ids], axis=0)
    below_grad, above_grad = {}, {}
    for k in range(2, steps + 1):
        if k > 2:
            before = below_grad[k - 2]
            below, above = after(below, before), after(above, before)
        if k < steps:
            arriving = send_up(below), send_down(above)
        else:
            ends = jnp.concatenate([below[:half], below[inst_rows:]], axis=0)
            arriving = send_up(ends), send_down(above[half:inst_rows])
        if k == 3 or steps < 3:
            below_grad[k - 1], above_grad[k - 1], own_grad = take([below], [above], [own])
        else:
            below_grad[k - 1], above_grad[k - 1] = take([below], [above])
        below, above = arriving
    to_down, to_up = take([after(below, below_grad[steps - 1]), above])

    scale = 1.0 / math.sqrt(inst_rows * seq_count * top_count // local_count)

    def seq_send(array, bit):
        return lax.ppermute(array, "seq", [(k, k ^ bit) for k in range(seq_count)])

    far, near = list(range(seq_count // 2, seq_count)), list(range(seq_count // 2))
    terms = dict(zip(far, weight_work(used, slopes, far, part_width, scale)))
    terms.update(zip(near, weight_work(used, slopes, near, part_width, scale)))
    terms = {q: [term] for q, term in terms.items()}
    bit = 1
    while bit < seq_count:
        for q in [q for q in sorted(terms, reverse=True) if q & bit]:
            values = terms.pop(q)
            terms[q ^ bit].append(seq_send(add(*values) if len(values) > 1 else values[0], bit))
        bit *= 2

    for k in range(steps, 0, -1):
        from_above, from_below = send_down(to_down), send_up(to_up)
        if k == steps:
            near_below, near_above = below_grad[k - 1], above_grad[k - 1]
            to_down = jnp.concatenate([add(near_below[:half], from_above), near_below[half:]], axis=0)
            to_up = jnp.concatenate([near_above[:half], add(near_above[half:], from_below)], axis=0)
        elif k > 1:
            to_down, to_up = add(below_grad[k - 1], from_above), add(above_grad[k - 1], from_below)
    weight_grad = add(*terms[0])
    feature_grad = add(after(own_grad, weight_grad), from_above, from_below)
    return (feature_grad, weight_grad)


def solution(mesh):
    return jax.shard_map(
        local,
        mesh=mesh,
        in_specs=(
            P(("seq", "clus"), None),
            P(("seq", "clus"), None),
            P(("seq", "clus"), None),
            P("clus"),
            P("clus", None),
        ),
        out_specs=(P(("seq", "clus"), None), P("clus", "seq")),
        check_vma=False,
    )
```

```python
import functools
import math

import jax
import jax.numpy as jnp
from jax import lax
from jax.experimental import pallas as pl
from jax.experimental.pallas import tpu as pltpu
from jax.sharding import PartitionSpec as P

BLOCK = 128
LANES = 128
FIELD_ROWS = 8
CHUNK = 256
VMEM_LIMIT = 40 * 1024 * 1024


def ids_kernel(width, short_ref, pos_ref, out_ref):
    rows = short_ref.shape[1]
    short = short_ref[...]
    places = pos_ref[...] // BLOCK
    offsets = pos_ref[...] % BLOCK
    targets = jnp.zeros_like(places)
    for j in range(short.shape[0]):
        targets = targets + jnp.where(places == j, short[j : j + 1, :], 0)
    fields = jnp.concatenate([short, targets, offsets], axis=0)
    groups = [
        fields[at : at + FIELD_ROWS] for at in range(0, fields.shape[0], FIELD_ROWS)
    ]
    groups.append(jnp.zeros((FIELD_ROWS, width - rows * len(groups)), jnp.int32))
    meta = jnp.concatenate(groups, axis=1)
    out_ref[...] = meta.astype(jnp.float32).astype(jnp.bfloat16)


def instance_ids(shortlist, positives, width):
    return pl.pallas_call(
        functools.partial(ids_kernel, width),
        out_shape=jax.ShapeDtypeStruct((FIELD_ROWS, width), jnp.bfloat16),
        in_specs=[pl.BlockSpec(memory_space=pltpu.VMEM)] * 2,
        compiler_params=pltpu.CompilerParams(vmem_limit_bytes=VMEM_LIMIT),
        name="instance_ids",
    )(shortlist.T, positives.T)


def live_kernel(size_ref, w_ref, live_ref):
    lane = lax.broadcasted_iota(jnp.int32, (LANES, BLOCK), 1)
    row = lax.broadcasted_iota(jnp.int32, (LANES, BLOCK), 0)
    for c in range(size_ref.shape[0]):
        live = jnp.where((row == c) & (lane < size_ref[c]), 2.0, 0.0)
        live_ref[:, c * BLOCK : (c + 1) * BLOCK] = live.astype(jnp.bfloat16)


def live_labels(cluster_sizes, weights):
    return pl.pallas_call(
        live_kernel,
        out_shape=jax.ShapeDtypeStruct((LANES, cluster_sizes.shape[0] * BLOCK), jnp.bfloat16),
        in_specs=[
            pl.BlockSpec(memory_space=pltpu.SMEM),
            pl.BlockSpec(memory_space=pltpu.VMEM),
        ],
        compiler_params=pltpu.CompilerParams(vmem_limit_bytes=VMEM_LIMIT),
        name="live_labels",
    )(cluster_sizes, weights)


def block_kernel(piece_rows, top_count, pos_count, *refs):
    block_count = len(piece_rows)
    piece_count = sum(len(pieces) for pieces in piece_rows)
    x_refs = refs[:piece_count]
    w_ref, live_ref = refs[piece_count : piece_count + 2]
    grad_refs = refs[piece_count + 2 : 2 * piece_count + 2]
    slope_refs = refs[2 * piece_count + 2 :]
    labels, width = w_ref.shape
    local_count = labels // BLOCK
    rows = slope_refs[0].shape[0]
    first = (lax.axis_index("clus") * local_count).astype(jnp.float32)

    named, pieces = [], []
    cluster = lax.broadcasted_iota(jnp.int32, (FIELD_ROWS, rows), 0).astype(jnp.float32) + first
    at = 0
    for b in range(block_count):
        block_refs = x_refs[at : at + len(piece_rows[b])]
        at += len(piece_rows[b])
        pieces += [ref[:count, :] for ref, count in zip(block_refs, piece_rows[b])]
        groups = -(-(top_count + 2 * pos_count) // FIELD_ROWS)
        meta = block_refs[0][piece_rows[b][0] :, : groups * rows].astype(jnp.float32)
        field = [
            meta[f % FIELD_ROWS : f % FIELD_ROWS + 1, f // FIELD_ROWS * rows : (f // FIELD_ROWS + 1) * rows]
            for f in range(top_count + 2 * pos_count)
        ]
        member = jnp.zeros((FIELD_ROWS, rows), jnp.float32)
        for j in range(top_count):
            member = jnp.where(cluster == field[j], 1.0, member)
        target = [
            (field[top_count + q] - first) * BLOCK + field[top_count + pos_count + q]
            for q in range(pos_count)
        ]
        rest = jnp.zeros((LANES - FIELD_ROWS - pos_count, rows), jnp.float32)
        named.append(jnp.concatenate([member] + target + [rest], axis=0).T)

    x = jnp.concatenate(pieces, axis=0) if len(pieces) > 1 else pieces[0]
    named = jnp.concatenate(named, axis=0) if block_count > 1 else named[0]
    target = [named[:, FIELD_ROWS + q : FIELD_ROWS + q + 1] for q in range(pos_count)]
    member = jnp.where(
        lax.broadcasted_iota(jnp.int32, named.shape, 1) < FIELD_ROWS, named, 0.0
    ).astype(jnp.bfloat16)
    for start in range(0, labels, CHUNK):
        logits = lax.dot_general(
            x,
            w_ref[start : start + CHUNK, :],
            (((1,), (1,)), ((), ())),
            preferred_element_type=jnp.float32,
        )
        live = jnp.dot(
            member, live_ref[:, start : start + CHUNK], preferred_element_type=jnp.float32
        )
        label = (
            lax.broadcasted_iota(jnp.int32, (1, CHUNK), 1) + start
        ).astype(jnp.float32)
        positive = target[0] == label
        for q in range(1, pos_count):
            positive = positive | (target[q] == label)
        turned = jnp.where(positive, -1.0, 1.0)
        slope = (turned * live * jnp.maximum(1.0 + turned * logits, 0.0)).astype(jnp.bfloat16)
        for b, ref in enumerate(slope_refs):
            ref[:, start : start + CHUNK] = slope[b * rows : (b + 1) * rows]
    slope = [ref[...] for ref in slope_refs]
    slope = jnp.concatenate(slope, axis=0) if block_count > 1 else slope[0]
    for start in range(0, width, CHUNK):
        part = jnp.dot(
            slope, w_ref[:, start : start + CHUNK], preferred_element_type=jnp.float32
        ).astype(jnp.bfloat16)
        at = 0
        for ref in grad_refs:
            ref[:, start : start + CHUNK] = part[at : at + ref.shape[0]]
            at += ref.shape[0]


def block_work(blocks, weights, live_table, top_count, pos_count):
    labels, width = weights.shape
    piece_rows = [
        [piece.shape[0] - (FIELD_ROWS if p == 0 else 0) for p, piece in enumerate(pieces)]
        for pieces in blocks
    ]
    flat_rows = sum(piece_rows, [])
    out = pl.pallas_call(
        functools.partial(block_kernel, piece_rows, top_count, pos_count),
        out_shape=[jax.ShapeDtypeStruct((rows, width), jnp.bfloat16) for rows in flat_rows]
        + [jax.ShapeDtypeStruct((sum(rows), labels), jnp.bfloat16) for rows in piece_rows],
        in_specs=[pl.BlockSpec(memory_space=pltpu.VMEM)] * (len(flat_rows) + 2),
        compiler_params=pltpu.CompilerParams(vmem_limit_bytes=VMEM_LIMIT),
        cost_estimate=pl.CostEstimate(
            flops=4 * sum(flat_rows) * labels * width,
            bytes_accessed=2 * labels * width + 6 * sum(flat_rows) * width,
            transcendentals=0,
        ),
        name="block_work",
    )(*[piece for pieces in blocks for piece in pieces], weights, live_table)
    return list(out[: len(flat_rows)]), list(out[len(flat_rows) :])


def weight_kernel(piece_rows, column_blocks, scale, *refs):
    piece_count = len(piece_rows)
    out_refs = refs[len(refs) - len(column_blocks) :]
    x_refs, s_refs = refs[:piece_count], refs[piece_count : len(refs) - len(column_blocks)]
    part_width = out_refs[0].shape[1]
    slopes = jnp.concatenate([ref[...] for ref in s_refs], axis=0)
    for ref, q in zip(out_refs, column_blocks):
        at = pl.multiple_of((lax.axis_index("seq") ^ q) * part_width, part_width)
        x = jnp.concatenate(
            [r[:rows, pl.ds(at, part_width)] for r, rows in zip(x_refs, piece_rows)], axis=0
        )
        part = lax.dot_general(
            slopes, x, (((0,), (0,)), ((), ())), preferred_element_type=jnp.float32
        )
        ref[...] = (part * scale).astype(jnp.bfloat16)


def weight_work(blocks, slopes, column_blocks, part_width, scale):
    pieces = [piece for block in blocks for piece in block]
    piece_rows = [
        piece.shape[0] - (FIELD_ROWS if p == 0 else 0)
        for block in blocks
        for p, piece in enumerate(block)
    ]
    labels = slopes[0].shape[1]
    rows = sum(piece_rows)
    return pl.pallas_call(
        functools.partial(weight_kernel, piece_rows, column_blocks, scale),
        out_shape=[jax.ShapeDtypeStruct((labels, part_width), jnp.bfloat16)] * len(column_blocks),
        in_specs=[pl.BlockSpec(memory_space=pltpu.VMEM)] * (len(pieces) + len(slopes)),
        compiler_params=pltpu.CompilerParams(vmem_limit_bytes=VMEM_LIMIT),
        cost_estimate=pl.CostEstimate(
            flops=2 * rows * labels * part_width * len(column_blocks),
            bytes_accessed=2 * rows * (labels + 1024) + 2 * labels * part_width,
            transcendentals=0,
        ),
        name="weight_work",
    )(*pieces, *slopes)


def add(*parts):
    total = parts[0].astype(jnp.float32)
    for part in parts[1:]:
        total = total + part.astype(jnp.float32)
    return total.astype(jnp.bfloat16)


def sum_kernel(pieces, *refs):
    *in_refs, out_ref, held, sems = refs
    rows = out_ref.shape[0] // pieces
    copies = []
    for p in range(pieces):
        at = pl.ds(p * rows, rows)
        total = in_refs[0][at, :].astype(jnp.float32)
        for ref in in_refs[1:]:
            total = total + ref[at, :].astype(jnp.float32)
        held[at, :] = total.astype(jnp.bfloat16)
        copies.append(pltpu.make_async_copy(held.at[at], out_ref.at[at], sems.at[p]))
        copies[-1].start()
    for copy in copies:
        copy.wait()


def final_sum(parts, pieces):
    shape = parts[0].shape
    return pl.pallas_call(
        functools.partial(sum_kernel, pieces),
        out_shape=jax.ShapeDtypeStruct(shape, jnp.bfloat16),
        in_specs=[pl.BlockSpec(memory_space=pltpu.VMEM)] * len(parts),
        out_specs=pl.BlockSpec(memory_space=pl.ANY),
        scratch_shapes=[
            pltpu.VMEM(shape, jnp.bfloat16),
            pltpu.SemaphoreType.DMA((pieces,)),
        ],
        compiler_params=pltpu.CompilerParams(vmem_limit_bytes=VMEM_LIMIT),
        cost_estimate=pl.CostEstimate(
            flops=len(parts) * parts[0].size,
            bytes_accessed=2 * (len(parts) + 1) * parts[0].size,
            transcendentals=0,
        ),
        name="final_sum",
    )(*parts)


def after(array, *others):
    return lax.optimization_barrier((array, *others))[0]


def local(features, shortlist, positives, cluster_sizes, weights):
    inst_rows, width = features.shape
    top_count, pos_count = shortlist.shape[1], positives.shape[1]
    clus_count, seq_count = lax.axis_size("clus"), lax.axis_size("seq")
    local_count = cluster_sizes.shape[0]
    part_width = width // seq_count
    half, steps = inst_rows // 2, clus_count // 2

    ring = list(range(0, clus_count, 2)) + list(range(1, clus_count, 2))[::-1]
    up = list(zip(ring, ring[1:] + ring[:1]))
    down = [(b, a) for a, b in up]

    def send_up(array):
        return lax.ppermute(array, "clus", up)

    def send_down(array):
        return lax.ppermute(array, "clus", down)

    used, slopes = [], []

    def take(*blocks):
        grads, found = block_work(blocks, weights, live_table, top_count, pos_count)
        used.extend(blocks)
        slopes.extend(found)
        return grads

    ids = instance_ids(shortlist, positives, width)
    live_table = live_labels(cluster_sizes, weights)
    own = jnp.concatenate([features, ids], axis=0)
    below, below_ids = send_up(features), send_up(ids)
    above, above_ids = send_down(features), send_down(ids)
    below = jnp.concatenate([after(below, live_table), below_ids], axis=0)
    above = jnp.concatenate([after(above, live_table), above_ids], axis=0)
    below_grad, above_grad = {}, {}
    for k in range(2, steps + 1):
        if k > 2:
            before = below_grad[k - 2]
            below, above = after(below, before), after(above, before)
        if k < steps:
            arriving = send_up(below), send_down(above)
        else:
            ends = jnp.concatenate([below[:half], below[inst_rows:]], axis=0)
            arriving = send_up(ends), send_down(above[half:inst_rows])
        if k == 3 or steps < 3:
            below_grad[k - 1], above_grad[k - 1], own_grad = take([below], [above], [own])
        else:
            below_grad[k - 1], above_grad[k - 1] = take([below], [above])
        below, above = arriving
    to_down, to_up = take([after(below, below_grad[steps - 1]), above])

    scale = 1.0 / math.sqrt(inst_rows * seq_count * top_count // local_count)

    def seq_send(array, bit):
        return lax.ppermute(array, "seq", [(k, k ^ bit) for k in range(seq_count)])

    slots = list(range(seq_count))[::-1]
    parts = weight_work(used, slopes, slots, part_width, scale)
    terms = {q: [part] for q, part in zip(slots, parts)}
    bit = 1
    while bit < seq_count:
        for q in [q for q in sorted(terms, reverse=True) if q & bit]:
            values = terms.pop(q)
            terms[q ^ bit].append(seq_send(add(*values) if len(values) > 1 else values[0], bit))
        bit *= 2

    for k in range(steps, 0, -1):
        from_above, from_below = send_down(to_down), send_up(to_up)
        if k == steps:
            near_below, near_above = below_grad[k - 1], above_grad[k - 1]
            to_down = jnp.concatenate([add(near_below[:half], from_above), near_below[half:]], axis=0)
            to_up = jnp.concatenate([near_above[:half], add(near_above[half:], from_below)], axis=0)
        elif k > 1:
            to_down, to_up = add(below_grad[k - 1], from_above), add(above_grad[k - 1], from_below)
    weight_grad = final_sum(terms[0], 4)
    feature_grad = final_sum([after(own_grad, weight_grad), from_above, from_below], 4)
    return (feature_grad, weight_grad)


def solution(mesh):
    return jax.shard_map(
        local,
        mesh=mesh,
        in_specs=(
            P(("seq", "clus"), None),
            P(("seq", "clus"), None),
            P(("seq", "clus"), None),
            P("clus"),
            P("clus", None),
        ),
        out_specs=(P(("seq", "clus"), None), P("clus", "seq")),
        check_vma=False,
    )
```

```python
import functools
import math

import jax
import jax.numpy as jnp
from jax import lax
from jax.experimental import pallas as pl
from jax.experimental.pallas import tpu as pltpu
from jax.sharding import PartitionSpec as P

BLOCK = 128
LANES = 128
FIELD_ROWS = 8
CHUNK = 256
VMEM_LIMIT = 40 * 1024 * 1024


def ids_kernel(width, short_ref, pos_ref, out_ref):
    rows = short_ref.shape[1]
    short = short_ref[...]
    places = pos_ref[...] // BLOCK
    offsets = pos_ref[...] % BLOCK
    targets = jnp.zeros_like(places)
    for j in range(short.shape[0]):
        targets = targets + jnp.where(places == j, short[j : j + 1, :], 0)
    fields = jnp.concatenate([short, targets, offsets], axis=0)
    groups = [
        fields[at : at + FIELD_ROWS] for at in range(0, fields.shape[0], FIELD_ROWS)
    ]
    groups.append(jnp.zeros((FIELD_ROWS, width - rows * len(groups)), jnp.int32))
    meta = jnp.concatenate(groups, axis=1)
    out_ref[...] = meta.astype(jnp.float32).astype(jnp.bfloat16)


def instance_ids(shortlist, positives, width):
    return pl.pallas_call(
        functools.partial(ids_kernel, width),
        out_shape=jax.ShapeDtypeStruct((FIELD_ROWS, width), jnp.bfloat16),
        in_specs=[pl.BlockSpec(memory_space=pltpu.VMEM)] * 2,
        compiler_params=pltpu.CompilerParams(vmem_limit_bytes=VMEM_LIMIT),
        name="instance_ids",
    )(shortlist.T, positives.T)


def live_kernel(size_ref, w_ref, live_ref):
    lane = lax.broadcasted_iota(jnp.int32, (LANES, BLOCK), 1)
    row = lax.broadcasted_iota(jnp.int32, (LANES, BLOCK), 0)
    for c in range(size_ref.shape[0]):
        live = jnp.where((row == c) & (lane < size_ref[c]), 2.0, 0.0)
        live_ref[:, c * BLOCK : (c + 1) * BLOCK] = live.astype(jnp.bfloat16)


def live_labels(cluster_sizes, weights):
    return pl.pallas_call(
        live_kernel,
        out_shape=jax.ShapeDtypeStruct((LANES, cluster_sizes.shape[0] * BLOCK), jnp.bfloat16),
        in_specs=[
            pl.BlockSpec(memory_space=pltpu.SMEM),
            pl.BlockSpec(memory_space=pltpu.VMEM),
        ],
        compiler_params=pltpu.CompilerParams(vmem_limit_bytes=VMEM_LIMIT),
        name="live_labels",
    )(cluster_sizes, weights)


def block_kernel(piece_rows, top_count, pos_count, *refs):
    block_count = len(piece_rows)
    piece_count = sum(len(pieces) for pieces in piece_rows)
    x_refs = refs[:piece_count]
    w_ref, live_ref = refs[piece_count : piece_count + 2]
    grad_refs = refs[piece_count + 2 : 2 * piece_count + 2]
    slope_refs = refs[2 * piece_count + 2 :]
    labels, width = w_ref.shape
    local_count = labels // BLOCK
    rows = slope_refs[0].shape[0]
    first = (lax.axis_index("clus") * local_count).astype(jnp.float32)

    named, pieces = [], []
    cluster = lax.broadcasted_iota(jnp.int32, (FIELD_ROWS, rows), 0).astype(jnp.float32) + first
    at = 0
    for b in range(block_count):
        block_refs = x_refs[at : at + len(piece_rows[b])]
        at += len(piece_rows[b])
        pieces += [ref[:count, :] for ref, count in zip(block_refs, piece_rows[b])]
        groups = -(-(top_count + 2 * pos_count) // FIELD_ROWS)
        meta = block_refs[0][piece_rows[b][0] :, : groups * rows].astype(jnp.float32)
        field = [
            meta[f % FIELD_ROWS : f % FIELD_ROWS + 1, f // FIELD_ROWS * rows : (f // FIELD_ROWS + 1) * rows]
            for f in range(top_count + 2 * pos_count)
        ]
        member = jnp.zeros((FIELD_ROWS, rows), jnp.float32)
        for j in range(top_count):
            member = jnp.where(cluster == field[j], 1.0, member)
        target = [
            (field[top_count + q] - first) * BLOCK + field[top_count + pos_count + q]
            for q in range(pos_count)
        ]
        rest = jnp.zeros((LANES - FIELD_ROWS - pos_count, rows), jnp.float32)
        named.append(jnp.concatenate([member] + target + [rest], axis=0).T)

    x = jnp.concatenate(pieces, axis=0) if len(pieces) > 1 else pieces[0]
    named = jnp.concatenate(named, axis=0) if block_count > 1 else named[0]
    target = [named[:, FIELD_ROWS + q : FIELD_ROWS + q + 1] for q in range(pos_count)]
    member = jnp.where(
        lax.broadcasted_iota(jnp.int32, named.shape, 1) < FIELD_ROWS, named, 0.0
    ).astype(jnp.bfloat16)
    for start in range(0, labels, CHUNK):
        logits = lax.dot_general(
            x,
            w_ref[start : start + CHUNK, :],
            (((1,), (1,)), ((), ())),
            preferred_element_type=jnp.float32,
        )
        live = jnp.dot(
            member, live_ref[:, start : start + CHUNK], preferred_element_type=jnp.float32
        )
        label = (
            lax.broadcasted_iota(jnp.int32, (1, CHUNK), 1) + start
        ).astype(jnp.float32)
        positive = target[0] == label
        for q in range(1, pos_count):
            positive = positive | (target[q] == label)
        turned = jnp.where(positive, -1.0, 1.0)
        slope = (turned * live * jnp.maximum(1.0 + turned * logits, 0.0)).astype(jnp.bfloat16)
        for b, ref in enumerate(slope_refs):
            ref[:, start : start + CHUNK] = slope[b * rows : (b + 1) * rows]
    slope = [ref[...] for ref in slope_refs]
    slope = jnp.concatenate(slope, axis=0) if block_count > 1 else slope[0]
    for start in range(0, width, CHUNK):
        part = jnp.dot(
            slope, w_ref[:, start : start + CHUNK], preferred_element_type=jnp.float32
        ).astype(jnp.bfloat16)
        at = 0
        for ref in grad_refs:
            ref[:, start : start + CHUNK] = part[at : at + ref.shape[0]]
            at += ref.shape[0]


def block_work(blocks, weights, live_table, top_count, pos_count):
    labels, width = weights.shape
    piece_rows = [
        [piece.shape[0] - (FIELD_ROWS if p == 0 else 0) for p, piece in enumerate(pieces)]
        for pieces in blocks
    ]
    flat_rows = sum(piece_rows, [])
    out = pl.pallas_call(
        functools.partial(block_kernel, piece_rows, top_count, pos_count),
        out_shape=[jax.ShapeDtypeStruct((rows, width), jnp.bfloat16) for rows in flat_rows]
        + [jax.ShapeDtypeStruct((sum(rows), labels), jnp.bfloat16) for rows in piece_rows],
        in_specs=[pl.BlockSpec(memory_space=pltpu.VMEM)] * (len(flat_rows) + 2),
        compiler_params=pltpu.CompilerParams(vmem_limit_bytes=VMEM_LIMIT),
        cost_estimate=pl.CostEstimate(
            flops=4 * sum(flat_rows) * labels * width,
            bytes_accessed=2 * labels * width + 6 * sum(flat_rows) * width,
            transcendentals=0,
        ),
        name="block_work",
    )(*[piece for pieces in blocks for piece in pieces], weights, live_table)
    return list(out[: len(flat_rows)]), list(out[len(flat_rows) :])


def weight_kernel(piece_rows, column_blocks, scale, *refs):
    piece_count = len(piece_rows)
    out_refs = refs[len(refs) - len(column_blocks) :]
    x_refs, s_refs = refs[:piece_count], refs[piece_count : len(refs) - len(column_blocks)]
    part_width = out_refs[0].shape[1]
    slopes = jnp.concatenate([ref[...] for ref in s_refs], axis=0)
    for ref, q in zip(out_refs, column_blocks):
        at = pl.multiple_of((lax.axis_index("seq") ^ q) * part_width, part_width)
        x = jnp.concatenate(
            [r[:rows, pl.ds(at, part_width)] for r, rows in zip(x_refs, piece_rows)], axis=0
        )
        part = lax.dot_general(
            slopes, x, (((0,), (0,)), ((), ())), preferred_element_type=jnp.float32
        )
        ref[...] = (part * scale).astype(jnp.bfloat16)


def weight_work(blocks, slopes, column_blocks, part_width, scale):
    pieces = [piece for block in blocks for piece in block]
    piece_rows = [
        piece.shape[0] - (FIELD_ROWS if p == 0 else 0)
        for block in blocks
        for p, piece in enumerate(block)
    ]
    labels = slopes[0].shape[1]
    rows = sum(piece_rows)
    return pl.pallas_call(
        functools.partial(weight_kernel, piece_rows, column_blocks, scale),
        out_shape=[jax.ShapeDtypeStruct((labels, part_width), jnp.bfloat16)] * len(column_blocks),
        in_specs=[pl.BlockSpec(memory_space=pltpu.VMEM)] * (len(pieces) + len(slopes)),
        compiler_params=pltpu.CompilerParams(vmem_limit_bytes=VMEM_LIMIT),
        cost_estimate=pl.CostEstimate(
            flops=2 * rows * labels * part_width * len(column_blocks),
            bytes_accessed=2 * rows * (labels + 1024) + 2 * labels * part_width,
            transcendentals=0,
        ),
        name="weight_work",
    )(*pieces, *slopes)


def add(*parts):
    total = parts[0].astype(jnp.float32)
    for part in parts[1:]:
        total = total + part.astype(jnp.float32)
    return total.astype(jnp.bfloat16)


def total_of(refs, at):
    total = refs[0][at, :].astype(jnp.float32)
    for ref in refs[1:]:
        total = total + ref[at, :].astype(jnp.float32)
    return total.astype(jnp.bfloat16)


def sum_kernel(*refs):
    *in_refs, out_ref = refs
    out_ref[...] = total_of(in_refs, slice(None))


def weight_sum(parts):
    return pl.pallas_call(
        sum_kernel,
        out_shape=jax.ShapeDtypeStruct(parts[0].shape, jnp.bfloat16),
        in_specs=[pl.BlockSpec(memory_space=pltpu.VMEM)] * len(parts),
        compiler_params=pltpu.CompilerParams(vmem_limit_bytes=VMEM_LIMIT),
        cost_estimate=pl.CostEstimate(
            flops=4_000_000_000, bytes_accessed=2 * (len(parts) + 1) * parts[0].size, transcendentals=0
        ),
        name="weight_sum",
    )(*parts)


def final_kernel(pieces, weight_ref, *refs):
    *in_refs, feature_out, weight_out, held, sems = refs
    copies = [pltpu.make_async_copy(weight_ref, weight_out, sems.at[pieces])]
    copies[0].start()
    rows = held.shape[0] // pieces
    for p in range(pieces):
        at = pl.ds(p * rows, rows)
        held[at, :] = total_of(in_refs, at)
        copies.append(pltpu.make_async_copy(held.at[at], feature_out.at[at], sems.at[p]))
        copies[-1].start()
    for copy in copies:
        copy.wait()


def finish(weight_grad, parts, pieces):
    shape = parts[0].shape
    return pl.pallas_call(
        functools.partial(final_kernel, pieces),
        out_shape=[
            jax.ShapeDtypeStruct(shape, jnp.bfloat16),
            jax.ShapeDtypeStruct(weight_grad.shape, jnp.bfloat16),
        ],
        in_specs=[pl.BlockSpec(memory_space=pltpu.VMEM)] * (len(parts) + 1),
        out_specs=[pl.BlockSpec(memory_space=pl.ANY)] * 2,
        scratch_shapes=[
            pltpu.VMEM(shape, jnp.bfloat16),
            pltpu.SemaphoreType.DMA((pieces + 1,)),
        ],
        compiler_params=pltpu.CompilerParams(vmem_limit_bytes=VMEM_LIMIT),
        cost_estimate=pl.CostEstimate(
            flops=len(parts) * parts[0].size,
            bytes_accessed=2 * (len(parts) + 1) * parts[0].size + 4 * weight_grad.size,
            transcendentals=0,
        ),
        name="finish",
    )(weight_grad, *parts)


def after(array, *others):
    return lax.optimization_barrier((array, *others))[0]


def local(features, shortlist, positives, cluster_sizes, weights):
    inst_rows, width = features.shape
    top_count, pos_count = shortlist.shape[1], positives.shape[1]
    clus_count, seq_count = lax.axis_size("clus"), lax.axis_size("seq")
    local_count = cluster_sizes.shape[0]
    part_width = width // seq_count
    split, steps = inst_rows * 5 // 8, clus_count // 2

    ring = list(range(0, clus_count, 2)) + list(range(1, clus_count, 2))[::-1]
    up = list(zip(ring, ring[1:] + ring[:1]))
    down = [(b, a) for a, b in up]

    def send_up(array):
        return lax.ppermute(array, "clus", up)

    def send_down(array):
        return lax.ppermute(array, "clus", down)

    used, slopes = [], []

    def take(*blocks):
        grads, found = block_work(blocks, weights, live_table, top_count, pos_count)
        used.extend(blocks)
        slopes.extend(found)
        return grads

    ids = instance_ids(shortlist, positives, width)
    live_table = live_labels(cluster_sizes, weights)
    own = jnp.concatenate([features, ids], axis=0)
    below, below_ids = send_up(features), send_up(ids)
    above, above_ids = send_down(features), send_down(ids)
    below = jnp.concatenate([after(below, live_table), below_ids], axis=0)
    above = jnp.concatenate([after(above, live_table), above_ids], axis=0)
    below_grad, above_grad = {}, {}
    for k in range(2, steps + 1):
        if k > 2:
            before = below_grad[k - 2]
            below, above = after(below, before), after(above, before)
        if k < steps:
            arriving = send_up(below), send_down(above)
        else:
            ends = jnp.concatenate([below[:split], below[inst_rows:]], axis=0)
            arriving = send_up(ends), send_down(above[split:inst_rows])
        if k == 3 or steps < 3:
            below_grad[k - 1], above_grad[k - 1], own_grad = take([below], [above], [own])
        else:
            below_grad[k - 1], above_grad[k - 1] = take([below], [above])
        below, above = arriving
    to_down, to_up = take([after(below, below_grad[steps - 1]), above])

    scale = 1.0 / math.sqrt(inst_rows * seq_count * top_count // local_count)

    def seq_send(array, bit):
        return lax.ppermute(array, "seq", [(k, k ^ bit) for k in range(seq_count)])

    slots = list(range(seq_count))[::-1]
    parts = weight_work(used, slopes, slots, part_width, scale)
    terms = {q: [part] for q, part in zip(slots, parts)}
    bit = 1
    while bit < seq_count:
        for q in [q for q in sorted(terms, reverse=True) if q & bit]:
            values = terms.pop(q)
            terms[q ^ bit].append(seq_send(add(*values) if len(values) > 1 else values[0], bit))
        bit *= 2

    for k in range(steps, 0, -1):
        from_above, from_below = send_down(to_down), send_up(to_up)
        if k == steps:
            near_below, near_above = below_grad[k - 1], above_grad[k - 1]
            to_down = jnp.concatenate([add(near_below[:split], from_above), near_below[split:]], axis=0)
            to_up = jnp.concatenate([near_above[:split], add(near_above[split:], from_below)], axis=0)
        elif k > 1:
            to_down, to_up = add(below_grad[k - 1], from_above), add(above_grad[k - 1], from_below)
    feature_grad, weight_grad = finish(weight_sum(terms[0]), [own_grad, from_above, from_below], 2)
    return (feature_grad, weight_grad)


def solution(mesh):
    return jax.shard_map(
        local,
        mesh=mesh,
        in_specs=(
            P(("seq", "clus"), None),
            P(("seq", "clus"), None),
            P(("seq", "clus"), None),
            P("clus"),
            P("clus", None),
        ),
        out_specs=(P(("seq", "clus"), None), P("clus", "seq")),
        check_vma=False,
    )
```

```python
import functools
import math

import jax
import jax.numpy as jnp
from jax import lax
from jax.experimental import pallas as pl
from jax.experimental.pallas import tpu as pltpu
from jax.sharding import PartitionSpec as P

BLOCK = 128
LANES = 128
FIELD_ROWS = 8
CHUNK = 256
VMEM_LIMIT = 40 * 1024 * 1024


def ids_kernel(width, short_ref, pos_ref, out_ref):
    rows = short_ref.shape[1]
    short = short_ref[...]
    places = pos_ref[...] // BLOCK
    offsets = pos_ref[...] % BLOCK
    targets = jnp.zeros_like(places)
    for j in range(short.shape[0]):
        targets = targets + jnp.where(places == j, short[j : j + 1, :], 0)
    fields = jnp.concatenate([short, targets, offsets], axis=0)
    groups = [
        fields[at : at + FIELD_ROWS] for at in range(0, fields.shape[0], FIELD_ROWS)
    ]
    groups.append(jnp.zeros((FIELD_ROWS, width - rows * len(groups)), jnp.int32))
    meta = jnp.concatenate(groups, axis=1)
    out_ref[...] = meta.astype(jnp.float32).astype(jnp.bfloat16)


def instance_ids(shortlist, positives, width):
    return pl.pallas_call(
        functools.partial(ids_kernel, width),
        out_shape=jax.ShapeDtypeStruct((FIELD_ROWS, width), jnp.bfloat16),
        in_specs=[pl.BlockSpec(memory_space=pltpu.VMEM)] * 2,
        compiler_params=pltpu.CompilerParams(vmem_limit_bytes=VMEM_LIMIT),
        name="instance_ids",
    )(shortlist.T, positives.T)


def live_kernel(size_ref, w_ref, live_ref):
    lane = lax.broadcasted_iota(jnp.int32, (LANES, BLOCK), 1)
    row = lax.broadcasted_iota(jnp.int32, (LANES, BLOCK), 0)
    for c in range(size_ref.shape[0]):
        live = jnp.where((row == c) & (lane < size_ref[c]), 2.0, 0.0)
        live_ref[:, c * BLOCK : (c + 1) * BLOCK] = live.astype(jnp.bfloat16)


def live_labels(cluster_sizes, weights):
    return pl.pallas_call(
        live_kernel,
        out_shape=jax.ShapeDtypeStruct((LANES, cluster_sizes.shape[0] * BLOCK), jnp.bfloat16),
        in_specs=[
            pl.BlockSpec(memory_space=pltpu.SMEM),
            pl.BlockSpec(memory_space=pltpu.VMEM),
        ],
        compiler_params=pltpu.CompilerParams(vmem_limit_bytes=VMEM_LIMIT),
        name="live_labels",
    )(cluster_sizes, weights)


def block_kernel(piece_rows, top_count, pos_count, *refs):
    block_count = len(piece_rows)
    piece_count = sum(len(pieces) for pieces in piece_rows)
    x_refs = refs[:piece_count]
    w_ref, live_ref = refs[piece_count : piece_count + 2]
    grad_refs = refs[piece_count + 2 : 2 * piece_count + 2]
    slope_refs = refs[2 * piece_count + 2 :]
    labels, width = w_ref.shape
    local_count = labels // BLOCK
    rows = slope_refs[0].shape[0]
    first = (lax.axis_index("clus") * local_count).astype(jnp.float32)

    named, pieces = [], []
    cluster = lax.broadcasted_iota(jnp.int32, (FIELD_ROWS, rows), 0).astype(jnp.float32) + first
    at = 0
    for b in range(block_count):
        block_refs = x_refs[at : at + len(piece_rows[b])]
        at += len(piece_rows[b])
        pieces += [ref[:count, :] for ref, count in zip(block_refs, piece_rows[b])]
        groups = -(-(top_count + 2 * pos_count) // FIELD_ROWS)
        meta = block_refs[0][piece_rows[b][0] :, : groups * rows].astype(jnp.float32)
        field = [
            meta[f % FIELD_ROWS : f % FIELD_ROWS + 1, f // FIELD_ROWS * rows : (f // FIELD_ROWS + 1) * rows]
            for f in range(top_count + 2 * pos_count)
        ]
        member = jnp.zeros((FIELD_ROWS, rows), jnp.float32)
        for j in range(top_count):
            member = jnp.where(cluster == field[j], 1.0, member)
        target = [
            (field[top_count + q] - first) * BLOCK + field[top_count + pos_count + q]
            for q in range(pos_count)
        ]
        rest = jnp.zeros((LANES - FIELD_ROWS - pos_count, rows), jnp.float32)
        named.append(jnp.concatenate([member] + target + [rest], axis=0).T)

    x = jnp.concatenate(pieces, axis=0) if len(pieces) > 1 else pieces[0]
    named = jnp.concatenate(named, axis=0) if block_count > 1 else named[0]
    target = [named[:, FIELD_ROWS + q : FIELD_ROWS + q + 1] for q in range(pos_count)]
    member = jnp.where(
        lax.broadcasted_iota(jnp.int32, named.shape, 1) < FIELD_ROWS, named, 0.0
    ).astype(jnp.bfloat16)
    for start in range(0, labels, CHUNK):
        logits = lax.dot_general(
            x,
            w_ref[start : start + CHUNK, :],
            (((1,), (1,)), ((), ())),
            preferred_element_type=jnp.float32,
        )
        live = jnp.dot(
            member, live_ref[:, start : start + CHUNK], preferred_element_type=jnp.float32
        )
        label = (
            lax.broadcasted_iota(jnp.int32, (1, CHUNK), 1) + start
        ).astype(jnp.float32)
        positive = target[0] == label
        for q in range(1, pos_count):
            positive = positive | (target[q] == label)
        turned = jnp.where(positive, -1.0, 1.0)
        slope = (turned * live * jnp.maximum(1.0 + turned * logits, 0.0)).astype(jnp.bfloat16)
        for b, ref in enumerate(slope_refs):
            ref[:, start : start + CHUNK] = slope[b * rows : (b + 1) * rows]
    slope = [ref[...] for ref in slope_refs]
    slope = jnp.concatenate(slope, axis=0) if block_count > 1 else slope[0]
    for start in range(0, width, CHUNK):
        part = jnp.dot(
            slope, w_ref[:, start : start + CHUNK], preferred_element_type=jnp.float32
        ).astype(jnp.bfloat16)
        at = 0
        for ref in grad_refs:
            ref[:, start : start + CHUNK] = part[at : at + ref.shape[0]]
            at += ref.shape[0]


def block_work(blocks, weights, live_table, top_count, pos_count):
    labels, width = weights.shape
    piece_rows = [
        [piece.shape[0] - (FIELD_ROWS if p == 0 else 0) for p, piece in enumerate(pieces)]
        for pieces in blocks
    ]
    flat_rows = sum(piece_rows, [])
    out = pl.pallas_call(
        functools.partial(block_kernel, piece_rows, top_count, pos_count),
        out_shape=[jax.ShapeDtypeStruct((rows, width), jnp.bfloat16) for rows in flat_rows]
        + [jax.ShapeDtypeStruct((sum(rows), labels), jnp.bfloat16) for rows in piece_rows],
        in_specs=[pl.BlockSpec(memory_space=pltpu.VMEM)] * (len(flat_rows) + 2),
        compiler_params=pltpu.CompilerParams(vmem_limit_bytes=VMEM_LIMIT),
        cost_estimate=pl.CostEstimate(
            flops=4 * sum(flat_rows) * labels * width,
            bytes_accessed=2 * labels * width + 6 * sum(flat_rows) * width,
            transcendentals=0,
        ),
        name="block_work",
    )(*[piece for pieces in blocks for piece in pieces], weights, live_table)
    return list(out[: len(flat_rows)]), list(out[len(flat_rows) :])


def weight_kernel(piece_rows, column_blocks, scale, *refs):
    piece_count = len(piece_rows)
    out_refs = refs[len(refs) - len(column_blocks) :]
    x_refs, s_refs = refs[:piece_count], refs[piece_count : len(refs) - len(column_blocks)]
    part_width = out_refs[0].shape[1]
    slopes = jnp.concatenate([ref[...] for ref in s_refs], axis=0)
    for ref, q in zip(out_refs, column_blocks):
        at = pl.multiple_of((lax.axis_index("seq") ^ q) * part_width, part_width)
        x = jnp.concatenate(
            [r[:rows, pl.ds(at, part_width)] for r, rows in zip(x_refs, piece_rows)], axis=0
        )
        part = lax.dot_general(
            slopes, x, (((0,), (0,)), ((), ())), preferred_element_type=jnp.float32
        )
        ref[...] = (part * scale).astype(jnp.bfloat16)


def weight_work(blocks, slopes, column_blocks, part_width, scale):
    pieces = [piece for block in blocks for piece in block]
    piece_rows = [
        piece.shape[0] - (FIELD_ROWS if p == 0 else 0)
        for block in blocks
        for p, piece in enumerate(block)
    ]
    labels = slopes[0].shape[1]
    rows = sum(piece_rows)
    return pl.pallas_call(
        functools.partial(weight_kernel, piece_rows, column_blocks, scale),
        out_shape=[jax.ShapeDtypeStruct((labels, part_width), jnp.bfloat16)] * len(column_blocks),
        in_specs=[pl.BlockSpec(memory_space=pltpu.VMEM)] * (len(pieces) + len(slopes)),
        compiler_params=pltpu.CompilerParams(vmem_limit_bytes=VMEM_LIMIT),
        cost_estimate=pl.CostEstimate(
            flops=2 * rows * labels * part_width * len(column_blocks),
            bytes_accessed=2 * rows * (labels + 1024) + 2 * labels * part_width,
            transcendentals=0,
        ),
        name="weight_work",
    )(*pieces, *slopes)


def add(*parts):
    total = parts[0].astype(jnp.float32)
    for part in parts[1:]:
        total = total + part.astype(jnp.float32)
    return total.astype(jnp.bfloat16)


def total_of(refs, at):
    total = refs[0][at, :].astype(jnp.float32)
    for ref in refs[1:]:
        total = total + ref[at, :].astype(jnp.float32)
    return total.astype(jnp.bfloat16)


def sum_kernel(*refs):
    *in_refs, out_ref = refs
    out_ref[...] = total_of(in_refs, slice(None))


def weight_sum(parts):
    return pl.pallas_call(
        sum_kernel,
        out_shape=jax.ShapeDtypeStruct(parts[0].shape, jnp.bfloat16),
        in_specs=[pl.BlockSpec(memory_space=pltpu.VMEM)] * len(parts),
        compiler_params=pltpu.CompilerParams(vmem_limit_bytes=VMEM_LIMIT),
        cost_estimate=pl.CostEstimate(
            flops=len(parts) * parts[0].size,
            bytes_accessed=2 * (len(parts) + 1) * parts[0].size,
            transcendentals=0,
        ),
        name="weight_sum",
    )(*parts)


def final_kernel(pieces, weight_ref, *refs):
    *in_refs, feature_out, weight_out, held, sems = refs
    copies = [pltpu.make_async_copy(weight_ref, weight_out, sems.at[pieces])]
    copies[0].start()
    rows = held.shape[0] // pieces
    for p in range(pieces):
        at = pl.ds(p * rows, rows)
        held[at, :] = total_of(in_refs, at)
        copies.append(pltpu.make_async_copy(held.at[at], feature_out.at[at], sems.at[p]))
        copies[-1].start()
    for copy in copies:
        copy.wait()


def finish(weight_grad, parts, pieces):
    shape = parts[0].shape
    return pl.pallas_call(
        functools.partial(final_kernel, pieces),
        out_shape=[
            jax.ShapeDtypeStruct(shape, jnp.bfloat16),
            jax.ShapeDtypeStruct(weight_grad.shape, jnp.bfloat16),
        ],
        in_specs=[pl.BlockSpec(memory_space=pltpu.VMEM)] * (len(parts) + 1),
        out_specs=[pl.BlockSpec(memory_space=pl.ANY)] * 2,
        scratch_shapes=[
            pltpu.VMEM(shape, jnp.bfloat16),
            pltpu.SemaphoreType.DMA((pieces + 1,)),
        ],
        compiler_params=pltpu.CompilerParams(vmem_limit_bytes=VMEM_LIMIT),
        cost_estimate=pl.CostEstimate(
            flops=len(parts) * parts[0].size,
            bytes_accessed=2 * (len(parts) + 1) * parts[0].size + 4 * weight_grad.size,
            transcendentals=0,
        ),
        name="finish",
    )(weight_grad, *parts)


def after(array, *others):
    return lax.optimization_barrier((array, *others))[0]


def local(features, shortlist, positives, cluster_sizes, weights):
    inst_rows, width = features.shape
    top_count, pos_count = shortlist.shape[1], positives.shape[1]
    clus_count, seq_count = lax.axis_size("clus"), lax.axis_size("seq")
    local_count = cluster_sizes.shape[0]
    part_width = width // seq_count
    split, steps = inst_rows * 5 // 8, clus_count // 2

    ring = list(range(0, clus_count, 2)) + list(range(1, clus_count, 2))[::-1]
    up = list(zip(ring, ring[1:] + ring[:1]))
    down = [(b, a) for a, b in up]

    def send_up(array):
        return lax.ppermute(array, "clus", up)

    def send_down(array):
        return lax.ppermute(array, "clus", down)

    used, slopes = [], []

    def take(*blocks):
        grads, found = block_work(blocks, weights, live_table, top_count, pos_count)
        used.extend(blocks)
        slopes.extend(found)
        return grads

    ids = instance_ids(shortlist, positives, width)
    live_table = live_labels(cluster_sizes, weights)
    own = jnp.concatenate([features, ids], axis=0)
    below, below_ids = send_up(features), send_up(ids)
    above, above_ids = send_down(features), send_down(ids)
    below = jnp.concatenate([after(below, live_table), below_ids], axis=0)
    above = jnp.concatenate([after(above, live_table), above_ids], axis=0)
    below_grad, above_grad = {}, {}
    for k in range(2, steps + 1):
        if k > 2:
            before = below_grad[k - 2]
            below, above = after(below, before), after(above, before)
        if k < steps:
            arriving = send_up(below), send_down(above)
        else:
            ends = jnp.concatenate([below[:split], below[inst_rows:]], axis=0)
            arriving = send_up(ends), send_down(above[split:inst_rows])
        if k == 3 or steps < 3:
            below_grad[k - 1], above_grad[k - 1], own_grad = take([below], [above], [own])
        else:
            below_grad[k - 1], above_grad[k - 1] = take([below], [above])
        below, above = arriving
    to_down, to_up = take([after(below, below_grad[steps - 1]), above])

    scale = 1.0 / math.sqrt(inst_rows * seq_count * top_count // local_count)

    def seq_send(array, bit):
        return lax.ppermute(array, "seq", [(k, k ^ bit) for k in range(seq_count)])

    slots = list(range(seq_count))[::-1]
    parts = weight_work(used, slopes, slots, part_width, scale)
    terms = {q: [part] for q, part in zip(slots, parts)}
    bit = 1
    while bit < seq_count:
        for q in [q for q in sorted(terms, reverse=True) if q & bit]:
            values = terms.pop(q)
            terms[q ^ bit].append(seq_send(add(*values) if len(values) > 1 else values[0], bit))
        bit *= 2

    for k in range(steps, 0, -1):
        from_above, from_below = send_down(to_down), send_up(to_up)
        if k == steps:
            near_below, near_above = below_grad[k - 1], above_grad[k - 1]
            to_down = jnp.concatenate([add(near_below[:split], from_above), near_below[split:]], axis=0)
            to_up = jnp.concatenate([near_above[:split], add(near_above[split:], from_below)], axis=0)
        elif k > 1:
            to_down, to_up = add(below_grad[k - 1], from_above), add(above_grad[k - 1], from_below)
    feature_grad, weight_grad = finish(weight_sum(terms[0]), [own_grad, from_above, from_below], 2)
    return (feature_grad, weight_grad)


def solution(mesh):
    return jax.shard_map(
        local,
        mesh=mesh,
        in_specs=(
            P(("seq", "clus"), None),
            P(("seq", "clus"), None),
            P(("seq", "clus"), None),
            P("clus"),
            P("clus", None),
        ),
        out_specs=(P(("seq", "clus"), None), P("clus", "seq")),
        check_vma=False,
    )
```

```python
import functools
import math

import jax
import jax.numpy as jnp
from jax import lax
from jax.experimental import pallas as pl
from jax.experimental.pallas import tpu as pltpu
from jax.sharding import PartitionSpec as P

BLOCK = 128
LANES = 128
FIELD_ROWS = 8
CHUNK = 256
VMEM_LIMIT = 40 * 1024 * 1024


def ids_kernel(width, short_ref, pos_ref, out_ref):
    rows = short_ref.shape[1]
    short = short_ref[...]
    places = pos_ref[...] // BLOCK
    offsets = pos_ref[...] % BLOCK
    targets = jnp.zeros_like(places)
    for j in range(short.shape[0]):
        targets = targets + jnp.where(places == j, short[j : j + 1, :], 0)
    fields = jnp.concatenate([short, targets, offsets], axis=0)
    groups = [
        fields[at : at + FIELD_ROWS] for at in range(0, fields.shape[0], FIELD_ROWS)
    ]
    groups.append(jnp.zeros((FIELD_ROWS, width - rows * len(groups)), jnp.int32))
    meta = jnp.concatenate(groups, axis=1)
    out_ref[...] = meta.astype(jnp.float32).astype(jnp.bfloat16)


def instance_ids(shortlist, positives, width):
    return pl.pallas_call(
        functools.partial(ids_kernel, width),
        out_shape=jax.ShapeDtypeStruct((FIELD_ROWS, width), jnp.bfloat16),
        in_specs=[pl.BlockSpec(memory_space=pltpu.VMEM)] * 2,
        compiler_params=pltpu.CompilerParams(vmem_limit_bytes=VMEM_LIMIT),
        name="instance_ids",
    )(shortlist.T, positives.T)


def live_kernel(size_ref, w_ref, live_ref):
    lane = lax.broadcasted_iota(jnp.int32, (LANES, BLOCK), 1)
    row = lax.broadcasted_iota(jnp.int32, (LANES, BLOCK), 0)
    for c in range(size_ref.shape[0]):
        live = jnp.where((row == c) & (lane < size_ref[c]), 2.0, 0.0)
        live_ref[:, c * BLOCK : (c + 1) * BLOCK] = live.astype(jnp.bfloat16)


def live_labels(cluster_sizes, weights):
    return pl.pallas_call(
        live_kernel,
        out_shape=jax.ShapeDtypeStruct((LANES, cluster_sizes.shape[0] * BLOCK), jnp.bfloat16),
        in_specs=[
            pl.BlockSpec(memory_space=pltpu.SMEM),
            pl.BlockSpec(memory_space=pltpu.VMEM),
        ],
        compiler_params=pltpu.CompilerParams(vmem_limit_bytes=VMEM_LIMIT),
        name="live_labels",
    )(cluster_sizes, weights)


def block_kernel(piece_rows, top_count, pos_count, *refs):
    block_count = len(piece_rows)
    piece_count = sum(len(pieces) for pieces in piece_rows)
    x_refs = refs[:piece_count]
    w_ref, live_ref = refs[piece_count : piece_count + 2]
    grad_refs = refs[piece_count + 2 : 2 * piece_count + 2]
    slope_refs = refs[2 * piece_count + 2 :]
    labels, width = w_ref.shape
    local_count = labels // BLOCK
    rows = slope_refs[0].shape[0]
    first = (lax.axis_index("clus") * local_count).astype(jnp.float32)

    named, pieces = [], []
    cluster = lax.broadcasted_iota(jnp.int32, (FIELD_ROWS, rows), 0).astype(jnp.float32) + first
    at = 0
    for b in range(block_count):
        block_refs = x_refs[at : at + len(piece_rows[b])]
        at += len(piece_rows[b])
        pieces += [ref[:count, :] for ref, count in zip(block_refs, piece_rows[b])]
        groups = -(-(top_count + 2 * pos_count) // FIELD_ROWS)
        meta = block_refs[0][piece_rows[b][0] :, : groups * rows].astype(jnp.float32)
        field = [
            meta[f % FIELD_ROWS : f % FIELD_ROWS + 1, f // FIELD_ROWS * rows : (f // FIELD_ROWS + 1) * rows]
            for f in range(top_count + 2 * pos_count)
        ]
        member = jnp.zeros((FIELD_ROWS, rows), jnp.float32)
        for j in range(top_count):
            member = jnp.where(cluster == field[j], 1.0, member)
        target = [
            (field[top_count + q] - first) * BLOCK + field[top_count + pos_count + q]
            for q in range(pos_count)
        ]
        rest = jnp.zeros((LANES - FIELD_ROWS - pos_count, rows), jnp.float32)
        named.append(jnp.concatenate([member] + target + [rest], axis=0).T)

    x = jnp.concatenate(pieces, axis=0) if len(pieces) > 1 else pieces[0]
    named = jnp.concatenate(named, axis=0) if block_count > 1 else named[0]
    target = [named[:, FIELD_ROWS + q : FIELD_ROWS + q + 1] for q in range(pos_count)]
    member = jnp.where(
        lax.broadcasted_iota(jnp.int32, named.shape, 1) < FIELD_ROWS, named, 0.0
    ).astype(jnp.bfloat16)
    for start in range(0, labels, CHUNK):
        logits = lax.dot_general(
            x,
            w_ref[start : start + CHUNK, :],
            (((1,), (1,)), ((), ())),
            preferred_element_type=jnp.float32,
        )
        live = jnp.dot(
            member, live_ref[:, start : start + CHUNK], preferred_element_type=jnp.float32
        )
        label = (
            lax.broadcasted_iota(jnp.int32, (1, CHUNK), 1) + start
        ).astype(jnp.float32)
        positive = target[0] == label
        for q in range(1, pos_count):
            positive = positive | (target[q] == label)
        turned = jnp.where(positive, -1.0, 1.0)
        slope = (turned * live * jnp.maximum(1.0 + turned * logits, 0.0)).astype(jnp.bfloat16)
        for b, ref in enumerate(slope_refs):
            ref[:, start : start + CHUNK] = slope[b * rows : (b + 1) * rows]
    slope = [ref[...] for ref in slope_refs]
    slope = jnp.concatenate(slope, axis=0) if block_count > 1 else slope[0]
    for start in range(0, width, CHUNK):
        part = jnp.dot(
            slope, w_ref[:, start : start + CHUNK], preferred_element_type=jnp.float32
        ).astype(jnp.bfloat16)
        at = 0
        for ref in grad_refs:
            ref[:, start : start + CHUNK] = part[at : at + ref.shape[0]]
            at += ref.shape[0]


def block_work(blocks, weights, live_table, top_count, pos_count):
    labels, width = weights.shape
    piece_rows = [
        [piece.shape[0] - (FIELD_ROWS if p == 0 else 0) for p, piece in enumerate(pieces)]
        for pieces in blocks
    ]
    flat_rows = sum(piece_rows, [])
    out = pl.pallas_call(
        functools.partial(block_kernel, piece_rows, top_count, pos_count),
        out_shape=[jax.ShapeDtypeStruct((rows, width), jnp.bfloat16) for rows in flat_rows]
        + [jax.ShapeDtypeStruct((sum(rows), labels), jnp.bfloat16) for rows in piece_rows],
        in_specs=[pl.BlockSpec(memory_space=pltpu.VMEM)] * (len(flat_rows) + 2),
        compiler_params=pltpu.CompilerParams(vmem_limit_bytes=VMEM_LIMIT),
        cost_estimate=pl.CostEstimate(
            flops=4 * sum(flat_rows) * labels * width,
            bytes_accessed=2 * labels * width + 6 * sum(flat_rows) * width,
            transcendentals=0,
        ),
        name="block_work",
    )(*[piece for pieces in blocks for piece in pieces], weights, live_table)
    return list(out[: len(flat_rows)]), list(out[len(flat_rows) :])


def weight_kernel(piece_rows, column_blocks, scale, *refs):
    piece_count = len(piece_rows)
    out_refs = refs[len(refs) - len(column_blocks) :]
    x_refs, s_refs = refs[:piece_count], refs[piece_count : len(refs) - len(column_blocks)]
    part_width = out_refs[0].shape[1]
    slopes = jnp.concatenate([ref[...] for ref in s_refs], axis=0)
    for ref, q in zip(out_refs, column_blocks):
        at = pl.multiple_of((lax.axis_index("seq") ^ q) * part_width, part_width)
        x = jnp.concatenate(
            [r[:rows, pl.ds(at, part_width)] for r, rows in zip(x_refs, piece_rows)], axis=0
        )
        part = lax.dot_general(
            slopes, x, (((0,), (0,)), ((), ())), preferred_element_type=jnp.float32
        )
        ref[...] = (part * scale).astype(jnp.bfloat16)


def weight_work(blocks, slopes, column_blocks, part_width, scale):
    pieces = [piece for block in blocks for piece in block]
    piece_rows = [
        piece.shape[0] - (FIELD_ROWS if p == 0 else 0)
        for block in blocks
        for p, piece in enumerate(block)
    ]
    labels = slopes[0].shape[1]
    rows = sum(piece_rows)
    return pl.pallas_call(
        functools.partial(weight_kernel, piece_rows, column_blocks, scale),
        out_shape=[jax.ShapeDtypeStruct((labels, part_width), jnp.bfloat16)] * len(column_blocks),
        in_specs=[pl.BlockSpec(memory_space=pltpu.VMEM)] * (len(pieces) + len(slopes)),
        compiler_params=pltpu.CompilerParams(vmem_limit_bytes=VMEM_LIMIT),
        cost_estimate=pl.CostEstimate(
            flops=2 * rows * labels * part_width * len(column_blocks),
            bytes_accessed=2 * rows * (labels + 1024) + 2 * labels * part_width,
            transcendentals=0,
        ),
        name="weight_work",
    )(*pieces, *slopes)


def add(*parts):
    total = parts[0].astype(jnp.float32)
    for part in parts[1:]:
        total = total + part.astype(jnp.float32)
    return total.astype(jnp.bfloat16)


def sum_kernel(*refs):
    total = refs[0][...].astype(jnp.float32)
    for ref in refs[1:-1]:
        total = total + ref[...].astype(jnp.float32)
    refs[-1][...] = total.astype(jnp.bfloat16)


def kernel_sum(*parts):
    return pl.pallas_call(
        sum_kernel,
        out_shape=jax.ShapeDtypeStruct(parts[0].shape, jnp.bfloat16),
        in_specs=[pl.BlockSpec(memory_space=pltpu.VMEM)] * len(parts),
        compiler_params=pltpu.CompilerParams(vmem_limit_bytes=VMEM_LIMIT),
        cost_estimate=pl.CostEstimate(
            flops=len(parts) * parts[0].size,
            bytes_accessed=2 * (len(parts) + 1) * parts[0].size,
            transcendentals=0,
        ),
        name="kernel_sum",
    )(*parts)


def final_kernel(weight_ref, own_ref, *refs):
    *in_refs, feature_out, weight_out, held, sems = refs
    pieces = len(in_refs) // 2
    copies = [pltpu.make_async_copy(weight_ref, weight_out, sems.at[pieces])]
    copies[0].start()
    rows = held.shape[0] // pieces
    for p in range(pieces):
        at = pl.ds(p * rows, rows)
        total = own_ref[at, :].astype(jnp.float32) + in_refs[p][...].astype(jnp.float32)
        held[at, :] = (total + in_refs[pieces + p][...].astype(jnp.float32)).astype(jnp.bfloat16)
        copies.append(pltpu.make_async_copy(held.at[at], feature_out.at[at], sems.at[p]))
        copies[-1].start()
    for copy in copies:
        copy.wait()


def finish(weight_grad, own_grad, from_above, from_below):
    shape = own_grad.shape
    return pl.pallas_call(
        final_kernel,
        out_shape=[
            jax.ShapeDtypeStruct(shape, jnp.bfloat16),
            jax.ShapeDtypeStruct(weight_grad.shape, jnp.bfloat16),
        ],
        in_specs=[pl.BlockSpec(memory_space=pltpu.VMEM)] * (2 + 2 * len(from_above)),
        out_specs=[pl.BlockSpec(memory_space=pl.ANY)] * 2,
        scratch_shapes=[
            pltpu.VMEM(shape, jnp.bfloat16),
            pltpu.SemaphoreType.DMA((len(from_above) + 1,)),
        ],
        compiler_params=pltpu.CompilerParams(vmem_limit_bytes=VMEM_LIMIT),
        cost_estimate=pl.CostEstimate(
            flops=3 * own_grad.size,
            bytes_accessed=8 * own_grad.size + 4 * weight_grad.size,
            transcendentals=0,
        ),
        name="finish",
    )(weight_grad, own_grad, *from_above, *from_below)


def after(array, *others):
    return lax.optimization_barrier((array, *others))[0]


def local(features, shortlist, positives, cluster_sizes, weights):
    inst_rows, width = features.shape
    top_count, pos_count = shortlist.shape[1], positives.shape[1]
    clus_count, seq_count = lax.axis_size("clus"), lax.axis_size("seq")
    local_count = cluster_sizes.shape[0]
    part_width = width // seq_count
    split, steps = inst_rows // 2, clus_count // 2

    ring = list(range(0, clus_count, 2)) + list(range(1, clus_count, 2))[::-1]
    up = list(zip(ring, ring[1:] + ring[:1]))
    down = [(b, a) for a, b in up]

    def send_up(array):
        return lax.ppermute(array, "clus", up)

    def send_down(array):
        return lax.ppermute(array, "clus", down)

    used, slopes = [], []

    def take(*blocks):
        grads, found = block_work(blocks, weights, live_table, top_count, pos_count)
        used.extend(blocks)
        slopes.extend(found)
        return grads

    ids = instance_ids(shortlist, positives, width)
    live_table = live_labels(cluster_sizes, weights)
    own = jnp.concatenate([features, ids], axis=0)
    below, below_ids = send_up(features), send_up(ids)
    above, above_ids = send_down(features), send_down(ids)
    below = jnp.concatenate([after(below, live_table), below_ids], axis=0)
    above = jnp.concatenate([after(above, live_table), above_ids], axis=0)
    below_grad, above_grad = {}, {}
    for k in range(2, steps + 1):
        if k > 2:
            before = below_grad[k - 2]
            below, above = after(below, before), after(above, before)
        if k < steps:
            arriving = send_up(below), send_down(above)
        else:
            ends = jnp.concatenate([below[:split], below[inst_rows:]], axis=0)
            arriving = send_up(ends), send_down(above[split:inst_rows])
        if k == 3 or steps < 3:
            below_grad[k - 1], above_grad[k - 1], own_grad = take([below], [above], [own])
        else:
            below_grad[k - 1], above_grad[k - 1] = take([below], [above])
        below, above = arriving
    to_down, to_up = take([after(below, below_grad[steps - 1]), above])

    scale = 1.0 / math.sqrt(inst_rows * seq_count * top_count // local_count)

    def seq_send(array, bit):
        return lax.ppermute(array, "seq", [(k, k ^ bit) for k in range(seq_count)])

    slots = list(range(seq_count))[::-1]
    parts = weight_work(used, slopes, slots, part_width, scale)
    terms = {q: [part] for q, part in zip(slots, parts)}
    bit = 1
    while bit < seq_count:
        for q in [q for q in sorted(terms, reverse=True) if q & bit]:
            values = terms.pop(q)
            terms[q ^ bit].append(seq_send(add(*values) if len(values) > 1 else values[0], bit))
        bit *= 2

    last = steps - 1

    def halves(array):
        return array[:split], array[split:]

    from_above, from_below = send_down(to_down), send_up(to_up)
    low, high = halves(below_grad[last])
    going_down = [kernel_sum(low, from_above), after(high, to_down, to_up)]
    low, high = halves(above_grad[last])
    going_up = [after(low, to_down, to_up), kernel_sum(high, from_below)]
    for k in range(last, 0, -1):
        from_above, from_below = [send_down(part) for part in going_down], [send_up(part) for part in going_up]
        if k > 1:
            going_down = [kernel_sum(*pair) for pair in zip(halves(below_grad[k - 1]), from_above)]
            going_up = [kernel_sum(*pair) for pair in zip(halves(above_grad[k - 1]), from_below)]
    feature_grad, weight_grad = finish(kernel_sum(*terms[0]), own_grad, from_above, from_below)
    return (feature_grad, weight_grad)


def solution(mesh):
    return jax.shard_map(
        local,
        mesh=mesh,
        in_specs=(
            P(("seq", "clus"), None),
            P(("seq", "clus"), None),
            P(("seq", "clus"), None),
            P("clus"),
            P("clus", None),
        ),
        out_specs=(P(("seq", "clus"), None), P("clus", "seq")),
        check_vma=False,
    )
```

```python
import functools
import math

import jax
import jax.numpy as jnp
from jax import lax
from jax.experimental import pallas as pl
from jax.experimental.pallas import tpu as pltpu
from jax.sharding import PartitionSpec as P

BLOCK = 128
LANES = 128
FIELD_ROWS = 8
CHUNK = 256
VMEM_LIMIT = 40 * 1024 * 1024


def ids_kernel(width, short_ref, pos_ref, out_ref):
    rows = short_ref.shape[1]
    short = short_ref[...]
    places = pos_ref[...] // BLOCK
    offsets = pos_ref[...] % BLOCK
    targets = jnp.zeros_like(places)
    for j in range(short.shape[0]):
        targets = targets + jnp.where(places == j, short[j : j + 1, :], 0)
    fields = jnp.concatenate([short, targets, offsets], axis=0)
    groups = [
        fields[at : at + FIELD_ROWS] for at in range(0, fields.shape[0], FIELD_ROWS)
    ]
    groups.append(jnp.zeros((FIELD_ROWS, width - rows * len(groups)), jnp.int32))
    meta = jnp.concatenate(groups, axis=1)
    out_ref[...] = meta.astype(jnp.float32).astype(jnp.bfloat16)


def instance_ids(shortlist, positives, width):
    return pl.pallas_call(
        functools.partial(ids_kernel, width),
        out_shape=jax.ShapeDtypeStruct((FIELD_ROWS, width), jnp.bfloat16),
        in_specs=[pl.BlockSpec(memory_space=pltpu.VMEM)] * 2,
        compiler_params=pltpu.CompilerParams(vmem_limit_bytes=VMEM_LIMIT),
        name="instance_ids",
    )(shortlist.T, positives.T)


def live_kernel(size_ref, w_ref, live_ref):
    lane = lax.broadcasted_iota(jnp.int32, (LANES, BLOCK), 1)
    row = lax.broadcasted_iota(jnp.int32, (LANES, BLOCK), 0)
    for c in range(size_ref.shape[0]):
        live = jnp.where((row == c) & (lane < size_ref[c]), 2.0, 0.0)
        live_ref[:, c * BLOCK : (c + 1) * BLOCK] = live.astype(jnp.bfloat16)


def live_labels(cluster_sizes, weights):
    return pl.pallas_call(
        live_kernel,
        out_shape=jax.ShapeDtypeStruct((LANES, cluster_sizes.shape[0] * BLOCK), jnp.bfloat16),
        in_specs=[
            pl.BlockSpec(memory_space=pltpu.SMEM),
            pl.BlockSpec(memory_space=pltpu.VMEM),
        ],
        compiler_params=pltpu.CompilerParams(vmem_limit_bytes=VMEM_LIMIT),
        name="live_labels",
    )(cluster_sizes, weights)


def block_kernel(piece_rows, top_count, pos_count, *refs):
    block_count = len(piece_rows)
    piece_count = sum(len(pieces) for pieces in piece_rows)
    x_refs = refs[:piece_count]
    w_ref, live_ref = refs[piece_count : piece_count + 2]
    grad_refs = refs[piece_count + 2 : len(refs) - block_count]
    slope_refs = refs[len(refs) - block_count :]
    labels, width = w_ref.shape
    local_count = labels // BLOCK
    rows = slope_refs[0].shape[0]
    first = (lax.axis_index("clus") * local_count).astype(jnp.float32)

    named, pieces = [], []
    cluster = lax.broadcasted_iota(jnp.int32, (FIELD_ROWS, rows), 0).astype(jnp.float32) + first
    at = 0
    for b in range(block_count):
        block_refs = x_refs[at : at + len(piece_rows[b])]
        at += len(piece_rows[b])
        pieces += [ref[:count, :] for ref, count in zip(block_refs, piece_rows[b])]
        groups = -(-(top_count + 2 * pos_count) // FIELD_ROWS)
        meta = block_refs[0][piece_rows[b][0] :, : groups * rows].astype(jnp.float32)
        field = [
            meta[f % FIELD_ROWS : f % FIELD_ROWS + 1, f // FIELD_ROWS * rows : (f // FIELD_ROWS + 1) * rows]
            for f in range(top_count + 2 * pos_count)
        ]
        member = jnp.zeros((FIELD_ROWS, rows), jnp.float32)
        for j in range(top_count):
            member = jnp.where(cluster == field[j], 1.0, member)
        target = [
            (field[top_count + q] - first) * BLOCK + field[top_count + pos_count + q]
            for q in range(pos_count)
        ]
        rest = jnp.zeros((LANES - FIELD_ROWS - pos_count, rows), jnp.float32)
        named.append(jnp.concatenate([member] + target + [rest], axis=0).T)

    x = jnp.concatenate(pieces, axis=0) if len(pieces) > 1 else pieces[0]
    named = jnp.concatenate(named, axis=0) if block_count > 1 else named[0]
    target = [named[:, FIELD_ROWS + q : FIELD_ROWS + q + 1] for q in range(pos_count)]
    member = jnp.where(
        lax.broadcasted_iota(jnp.int32, named.shape, 1) < FIELD_ROWS, named, 0.0
    ).astype(jnp.bfloat16)
    for start in range(0, labels, CHUNK):
        logits = lax.dot_general(
            x,
            w_ref[start : start + CHUNK, :],
            (((1,), (1,)), ((), ())),
            preferred_element_type=jnp.float32,
        )
        live = jnp.dot(
            member, live_ref[:, start : start + CHUNK], preferred_element_type=jnp.float32
        )
        label = (
            lax.broadcasted_iota(jnp.int32, (1, CHUNK), 1) + start
        ).astype(jnp.float32)
        positive = target[0] == label
        for q in range(1, pos_count):
            positive = positive | (target[q] == label)
        turned = jnp.where(positive, -1.0, 1.0)
        slope = (turned * live * jnp.maximum(1.0 + turned * logits, 0.0)).astype(jnp.bfloat16)
        for b, ref in enumerate(slope_refs):
            ref[:, start : start + CHUNK] = slope[b * rows : (b + 1) * rows]
    slope = [ref[...] for ref in slope_refs]
    slope = jnp.concatenate(slope, axis=0) if block_count > 1 else slope[0]
    for start in range(0, width, CHUNK):
        part = jnp.dot(
            slope, w_ref[:, start : start + CHUNK], preferred_element_type=jnp.float32
        ).astype(jnp.bfloat16)
        at = 0
        for ref in grad_refs:
            ref[:, start : start + CHUNK] = part[at : at + ref.shape[0]]
            at += ref.shape[0]


def block_work(blocks, weights, live_table, top_count, pos_count, grad_rows=None):
    labels, width = weights.shape
    piece_rows = [
        [piece.shape[0] - (FIELD_ROWS if p == 0 else 0) for p, piece in enumerate(pieces)]
        for pieces in blocks
    ]
    flat_rows = sum(piece_rows, [])
    grad_rows = grad_rows or flat_rows
    out = pl.pallas_call(
        functools.partial(block_kernel, piece_rows, top_count, pos_count),
        out_shape=[jax.ShapeDtypeStruct((rows, width), jnp.bfloat16) for rows in grad_rows]
        + [jax.ShapeDtypeStruct((sum(rows), labels), jnp.bfloat16) for rows in piece_rows],
        in_specs=[pl.BlockSpec(memory_space=pltpu.VMEM)] * (len(flat_rows) + 2),
        compiler_params=pltpu.CompilerParams(vmem_limit_bytes=VMEM_LIMIT),
        cost_estimate=pl.CostEstimate(
            flops=4 * sum(flat_rows) * labels * width,
            bytes_accessed=2 * labels * width + 6 * sum(flat_rows) * width,
            transcendentals=0,
        ),
        name="block_work",
    )(*[piece for pieces in blocks for piece in pieces], weights, live_table)
    return list(out[: len(grad_rows)]), list(out[len(grad_rows) :])


def weight_kernel(piece_rows, column_blocks, scale, *refs):
    piece_count = len(piece_rows)
    out_refs = refs[len(refs) - len(column_blocks) :]
    x_refs, s_refs = refs[:piece_count], refs[piece_count : len(refs) - len(column_blocks)]
    part_width = out_refs[0].shape[1]
    slopes = jnp.concatenate([ref[...] for ref in s_refs], axis=0)
    for ref, q in zip(out_refs, column_blocks):
        at = pl.multiple_of((lax.axis_index("seq") ^ q) * part_width, part_width)
        x = jnp.concatenate(
            [r[:rows, pl.ds(at, part_width)] for r, rows in zip(x_refs, piece_rows)], axis=0
        )
        part = lax.dot_general(
            slopes, x, (((0,), (0,)), ((), ())), preferred_element_type=jnp.float32
        )
        ref[...] = (part * scale).astype(jnp.bfloat16)


def weight_work(blocks, slopes, column_blocks, part_width, scale):
    pieces = [piece for block in blocks for piece in block]
    piece_rows = [
        piece.shape[0] - (FIELD_ROWS if p == 0 else 0)
        for block in blocks
        for p, piece in enumerate(block)
    ]
    labels = slopes[0].shape[1]
    rows = sum(piece_rows)
    return pl.pallas_call(
        functools.partial(weight_kernel, piece_rows, column_blocks, scale),
        out_shape=[jax.ShapeDtypeStruct((labels, part_width), jnp.bfloat16)] * len(column_blocks),
        in_specs=[pl.BlockSpec(memory_space=pltpu.VMEM)] * (len(pieces) + len(slopes)),
        compiler_params=pltpu.CompilerParams(vmem_limit_bytes=VMEM_LIMIT),
        cost_estimate=pl.CostEstimate(
            flops=2 * rows * labels * part_width * len(column_blocks),
            bytes_accessed=2 * rows * (labels + 1024) + 2 * labels * part_width,
            transcendentals=0,
        ),
        name="weight_work",
    )(*pieces, *slopes)


def add(*parts):
    total = parts[0].astype(jnp.float32)
    for part in parts[1:]:
        total = total + part.astype(jnp.float32)
    return total.astype(jnp.bfloat16)


def total_of(refs, at):
    total = refs[0][at, :].astype(jnp.float32)
    for ref in refs[1:]:
        total = total + ref[at, :].astype(jnp.float32)
    return total.astype(jnp.bfloat16)


def sum_kernel(*refs):
    *in_refs, out_ref = refs
    out_ref[...] = total_of(in_refs, slice(None))


def weight_sum(parts):
    return pl.pallas_call(
        sum_kernel,
        out_shape=jax.ShapeDtypeStruct(parts[0].shape, jnp.bfloat16),
        in_specs=[pl.BlockSpec(memory_space=pltpu.VMEM)] * len(parts),
        compiler_params=pltpu.CompilerParams(vmem_limit_bytes=VMEM_LIMIT),
        cost_estimate=pl.CostEstimate(
            flops=len(parts) * parts[0].size,
            bytes_accessed=2 * (len(parts) + 1) * parts[0].size,
            transcendentals=0,
        ),
        name="weight_sum",
    )(*parts)


def final_kernel(pieces, weight_ref, *refs):
    *in_refs, feature_out, weight_out, held, sems = refs
    copies = [pltpu.make_async_copy(weight_ref, weight_out, sems.at[pieces])]
    copies[0].start()
    rows = held.shape[0] // pieces
    for p in range(pieces):
        at = pl.ds(p * rows, rows)
        held[at, :] = total_of(in_refs, at)
        copies.append(pltpu.make_async_copy(held.at[at], feature_out.at[at], sems.at[p]))
        copies[-1].start()
    for copy in copies:
        copy.wait()


def finish(weight_grad, parts, pieces):
    shape = parts[0].shape
    return pl.pallas_call(
        functools.partial(final_kernel, pieces),
        out_shape=[
            jax.ShapeDtypeStruct(shape, jnp.bfloat16),
            jax.ShapeDtypeStruct(weight_grad.shape, jnp.bfloat16),
        ],
        in_specs=[pl.BlockSpec(memory_space=pltpu.VMEM)] * (len(parts) + 1),
        out_specs=[pl.BlockSpec(memory_space=pl.ANY)] * 2,
        scratch_shapes=[
            pltpu.VMEM(shape, jnp.bfloat16),
            pltpu.SemaphoreType.DMA((pieces + 1,)),
        ],
        compiler_params=pltpu.CompilerParams(vmem_limit_bytes=VMEM_LIMIT),
        cost_estimate=pl.CostEstimate(
            flops=len(parts) * parts[0].size,
            bytes_accessed=2 * (len(parts) + 1) * parts[0].size + 4 * weight_grad.size,
            transcendentals=0,
        ),
        name="finish",
    )(weight_grad, *parts)


def after(array, *others):
    return lax.optimization_barrier((array, *others))[0]


def local(features, shortlist, positives, cluster_sizes, weights):
    inst_rows, width = features.shape
    top_count, pos_count = shortlist.shape[1], positives.shape[1]
    clus_count, seq_count = lax.axis_size("clus"), lax.axis_size("seq")
    local_count = cluster_sizes.shape[0]
    part_width = width // seq_count
    first_part, half, steps = inst_rows * 5 // 8, inst_rows // 2, clus_count // 2

    ring = list(range(0, clus_count, 2)) + list(range(1, clus_count, 2))[::-1]
    up = list(zip(ring, ring[1:] + ring[:1]))
    down = [(b, a) for a, b in up]

    def send_up(array):
        return lax.ppermute(array, "clus", up)

    def send_down(array):
        return lax.ppermute(array, "clus", down)

    used, slopes = [], []

    def take(*blocks, grad_rows=None):
        grads, found = block_work(blocks, weights, live_table, top_count, pos_count, grad_rows)
        used.extend(blocks)
        slopes.extend(found)
        return grads

    ids = instance_ids(shortlist, positives, width)
    live_table = live_labels(cluster_sizes, weights)
    own = jnp.concatenate([features, ids], axis=0)
    below, below_ids = send_up(features), send_up(ids)
    above, above_ids = send_down(features), send_down(ids)
    below = jnp.concatenate([after(below, live_table), below_ids], axis=0)
    above = jnp.concatenate([after(above, live_table), above_ids], axis=0)
    below_grad, above_grad = {}, {}
    for k in range(2, steps + 1):
        if k > 2:
            before = below_grad[k - 2]
            below, above = after(below, before), after(above, before)
        if k < steps:
            arriving = send_up(below), send_down(above)
        else:
            ends = jnp.concatenate([below[:first_part], below[inst_rows:]], axis=0)
            arriving = send_up(ends), send_down(above[first_part:inst_rows])
        if k == 3 or steps < 3:
            below_grad[k - 1], above_grad[k - 1], own_grad = take([below], [above], [own])
        else:
            below_grad[k - 1], above_grad[k - 1] = take([below], [above])
        below, above = arriving
    opposite = [after(below, below_grad[steps - 1]), above]
    to_down, to_up = take(opposite, grad_rows=[half, half])

    scale = 1.0 / math.sqrt(inst_rows * seq_count * top_count // local_count)

    def seq_send(array, bit):
        return lax.ppermute(array, "seq", [(k, k ^ bit) for k in range(seq_count)])

    slots = list(range(seq_count))[::-1]
    parts = weight_work(used, slopes, slots, part_width, scale)
    terms = {q: [part] for q, part in zip(slots, parts)}
    bit = 1
    while bit < seq_count:
        for q in [q for q in sorted(terms, reverse=True) if q & bit]:
            values = terms.pop(q)
            terms[q ^ bit].append(seq_send(add(*values) if len(values) > 1 else values[0], bit))
        bit *= 2

    for k in range(steps, 0, -1):
        from_above, from_below = send_down(to_down), send_up(to_up)
        if k == steps:
            near_below, near_above = below_grad[k - 1], above_grad[k - 1]
            to_down = jnp.concatenate([add(near_below[:half], from_above), near_below[half:]], axis=0)
            to_up = jnp.concatenate([near_above[:half], add(near_above[half:], from_below)], axis=0)
        elif k > 1:
            to_down, to_up = add(below_grad[k - 1], from_above), add(above_grad[k - 1], from_below)
    feature_grad, weight_grad = finish(weight_sum(terms[0]), [own_grad, from_above, from_below], 2)
    return (feature_grad, weight_grad)


def solution(mesh):
    return jax.shard_map(
        local,
        mesh=mesh,
        in_specs=(
            P(("seq", "clus"), None),
            P(("seq", "clus"), None),
            P(("seq", "clus"), None),
            P("clus"),
            P("clus", None),
        ),
        out_specs=(P(("seq", "clus"), None), P("clus", "seq")),
        check_vma=False,
    )
```

```python
import functools
import math

import jax
import jax.numpy as jnp
from jax import lax
from jax.experimental import pallas as pl
from jax.experimental.pallas import tpu as pltpu
from jax.sharding import PartitionSpec as P

BLOCK = 128
LANES = 128
FIELD_ROWS = 8
CHUNK = 256
VMEM_LIMIT = 40 * 1024 * 1024


def ids_kernel(width, short_ref, pos_ref, out_ref):
    rows = short_ref.shape[1]
    short = short_ref[...]
    places = pos_ref[...] // BLOCK
    offsets = pos_ref[...] % BLOCK
    targets = jnp.zeros_like(places)
    for j in range(short.shape[0]):
        targets = targets + jnp.where(places == j, short[j : j + 1, :], 0)
    fields = jnp.concatenate([short, targets, offsets], axis=0)
    groups = [
        fields[at : at + FIELD_ROWS] for at in range(0, fields.shape[0], FIELD_ROWS)
    ]
    groups.append(jnp.zeros((FIELD_ROWS, width - rows * len(groups)), jnp.int32))
    meta = jnp.concatenate(groups, axis=1)
    out_ref[...] = meta.astype(jnp.float32).astype(jnp.bfloat16)


def instance_ids(shortlist, positives, width):
    return pl.pallas_call(
        functools.partial(ids_kernel, width),
        out_shape=jax.ShapeDtypeStruct((FIELD_ROWS, width), jnp.bfloat16),
        in_specs=[pl.BlockSpec(memory_space=pltpu.VMEM)] * 2,
        compiler_params=pltpu.CompilerParams(vmem_limit_bytes=VMEM_LIMIT),
        name="instance_ids",
    )(shortlist.T, positives.T)


def live_kernel(size_ref, w_ref, live_ref):
    lane = lax.broadcasted_iota(jnp.int32, (LANES, BLOCK), 1)
    row = lax.broadcasted_iota(jnp.int32, (LANES, BLOCK), 0)
    for c in range(size_ref.shape[0]):
        live = jnp.where((row == c) & (lane < size_ref[c]), 2.0, 0.0)
        live_ref[:, c * BLOCK : (c + 1) * BLOCK] = live.astype(jnp.bfloat16)


def live_labels(cluster_sizes, weights):
    return pl.pallas_call(
        live_kernel,
        out_shape=jax.ShapeDtypeStruct((LANES, cluster_sizes.shape[0] * BLOCK), jnp.bfloat16),
        in_specs=[
            pl.BlockSpec(memory_space=pltpu.SMEM),
            pl.BlockSpec(memory_space=pltpu.VMEM),
        ],
        compiler_params=pltpu.CompilerParams(vmem_limit_bytes=VMEM_LIMIT),
        name="live_labels",
    )(cluster_sizes, weights)


def block_kernel(piece_rows, top_count, pos_count, *refs):
    block_count = len(piece_rows)
    piece_count = sum(len(pieces) for pieces in piece_rows)
    x_refs = refs[:piece_count]
    w_ref, live_ref = refs[piece_count : piece_count + 2]
    grad_refs = refs[piece_count + 2 : len(refs) - block_count]
    slope_refs = refs[len(refs) - block_count :]
    labels, width = w_ref.shape
    local_count = labels // BLOCK
    rows = slope_refs[0].shape[0]
    first = (lax.axis_index("clus") * local_count).astype(jnp.float32)

    named, pieces = [], []
    cluster = lax.broadcasted_iota(jnp.int32, (FIELD_ROWS, rows), 0).astype(jnp.float32) + first
    at = 0
    for b in range(block_count):
        block_refs = x_refs[at : at + len(piece_rows[b])]
        at += len(piece_rows[b])
        pieces += [ref[:count, :] for ref, count in zip(block_refs, piece_rows[b])]
        groups = -(-(top_count + 2 * pos_count) // FIELD_ROWS)
        meta = block_refs[0][piece_rows[b][0] :, : groups * rows].astype(jnp.float32)
        field = [
            meta[f % FIELD_ROWS : f % FIELD_ROWS + 1, f // FIELD_ROWS * rows : (f // FIELD_ROWS + 1) * rows]
            for f in range(top_count + 2 * pos_count)
        ]
        member = jnp.zeros((FIELD_ROWS, rows), jnp.float32)
        for j in range(top_count):
            member = jnp.where(cluster == field[j], 1.0, member)
        target = [
            (field[top_count + q] - first) * BLOCK + field[top_count + pos_count + q]
            for q in range(pos_count)
        ]
        rest = jnp.zeros((LANES - FIELD_ROWS - pos_count, rows), jnp.float32)
        named.append(jnp.concatenate([member] + target + [rest], axis=0).T)

    x = jnp.concatenate(pieces, axis=0) if len(pieces) > 1 else pieces[0]
    named = jnp.concatenate(named, axis=0) if block_count > 1 else named[0]
    target = [named[:, FIELD_ROWS + q : FIELD_ROWS + q + 1] for q in range(pos_count)]
    member = jnp.where(
        lax.broadcasted_iota(jnp.int32, named.shape, 1) < FIELD_ROWS, named, 0.0
    ).astype(jnp.bfloat16)
    for start in range(0, labels, CHUNK):
        logits = lax.dot_general(
            x,
            w_ref[start : start + CHUNK, :],
            (((1,), (1,)), ((), ())),
            preferred_element_type=jnp.float32,
        )
        live = jnp.dot(
            member, live_ref[:, start : start + CHUNK], preferred_element_type=jnp.float32
        )
        label = (
            lax.broadcasted_iota(jnp.int32, (1, CHUNK), 1) + start
        ).astype(jnp.float32)
        positive = target[0] == label
        for q in range(1, pos_count):
            positive = positive | (target[q] == label)
        turned = jnp.where(positive, -1.0, 1.0)
        slope = (turned * live * jnp.maximum(1.0 + turned * logits, 0.0)).astype(jnp.bfloat16)
        for b, ref in enumerate(slope_refs):
            ref[:, start : start + CHUNK] = slope[b * rows : (b + 1) * rows]
    slope = [ref[...] for ref in slope_refs]
    slope = jnp.concatenate(slope, axis=0) if block_count > 1 else slope[0]
    for start in range(0, width, CHUNK):
        part = jnp.dot(
            slope, w_ref[:, start : start + CHUNK], preferred_element_type=jnp.float32
        ).astype(jnp.bfloat16)
        at = 0
        for ref in grad_refs:
            ref[:, start : start + CHUNK] = part[at : at + ref.shape[0]]
            at += ref.shape[0]


def block_work(blocks, weights, live_table, top_count, pos_count, grad_rows=None):
    labels, width = weights.shape
    piece_rows = [
        [piece.shape[0] - (FIELD_ROWS if p == 0 else 0) for p, piece in enumerate(pieces)]
        for pieces in blocks
    ]
    flat_rows = sum(piece_rows, [])
    grad_rows = grad_rows or flat_rows
    out = pl.pallas_call(
        functools.partial(block_kernel, piece_rows, top_count, pos_count),
        out_shape=[jax.ShapeDtypeStruct((rows, width), jnp.bfloat16) for rows in grad_rows]
        + [jax.ShapeDtypeStruct((sum(rows), labels), jnp.bfloat16) for rows in piece_rows],
        in_specs=[pl.BlockSpec(memory_space=pltpu.VMEM)] * (len(flat_rows) + 2),
        compiler_params=pltpu.CompilerParams(vmem_limit_bytes=VMEM_LIMIT),
        cost_estimate=pl.CostEstimate(
            flops=4 * sum(flat_rows) * labels * width,
            bytes_accessed=2 * labels * width + 6 * sum(flat_rows) * width,
            transcendentals=0,
        ),
        name="block_work",
    )(*[piece for pieces in blocks for piece in pieces], weights, live_table)
    return list(out[: len(grad_rows)]), list(out[len(grad_rows) :])


def weight_kernel(piece_rows, column_blocks, scale, *refs):
    piece_count = len(piece_rows)
    out_refs = refs[len(refs) - len(column_blocks) :]
    x_refs, s_refs = refs[:piece_count], refs[piece_count : len(refs) - len(column_blocks)]
    part_width = out_refs[0].shape[1]
    slopes = jnp.concatenate([ref[...] for ref in s_refs], axis=0)
    for ref, q in zip(out_refs, column_blocks):
        at = pl.multiple_of((lax.axis_index("seq") ^ q) * part_width, part_width)
        x = jnp.concatenate(
            [r[:rows, pl.ds(at, part_width)] for r, rows in zip(x_refs, piece_rows)], axis=0
        )
        part = lax.dot_general(
            slopes, x, (((0,), (0,)), ((), ())), preferred_element_type=jnp.float32
        )
        ref[...] = (part * scale).astype(jnp.bfloat16)


def weight_work(blocks, slopes, column_blocks, part_width, scale):
    pieces = [piece for block in blocks for piece in block]
    piece_rows = [
        piece.shape[0] - (FIELD_ROWS if p == 0 else 0)
        for block in blocks
        for p, piece in enumerate(block)
    ]
    labels = slopes[0].shape[1]
    rows = sum(piece_rows)
    return pl.pallas_call(
        functools.partial(weight_kernel, piece_rows, column_blocks, scale),
        out_shape=[jax.ShapeDtypeStruct((labels, part_width), jnp.bfloat16)] * len(column_blocks),
        in_specs=[pl.BlockSpec(memory_space=pltpu.VMEM)] * (len(pieces) + len(slopes)),
        compiler_params=pltpu.CompilerParams(vmem_limit_bytes=VMEM_LIMIT),
        cost_estimate=pl.CostEstimate(
            flops=2 * rows * labels * part_width * len(column_blocks),
            bytes_accessed=2 * rows * (labels + 1024) + 2 * labels * part_width,
            transcendentals=0,
        ),
        name="weight_work",
    )(*pieces, *slopes)


def add(*parts):
    total = parts[0].astype(jnp.float32)
    for part in parts[1:]:
        total = total + part.astype(jnp.float32)
    return total.astype(jnp.bfloat16)


def total_of(refs, at):
    total = refs[0][at, :].astype(jnp.float32)
    for ref in refs[1:]:
        total = total + ref[at, :].astype(jnp.float32)
    return total.astype(jnp.bfloat16)


def sum_kernel(*refs):
    *in_refs, out_ref = refs
    out_ref[...] = total_of(in_refs, slice(None))


def weight_sum(parts):
    return pl.pallas_call(
        sum_kernel,
        out_shape=jax.ShapeDtypeStruct(parts[0].shape, jnp.bfloat16),
        in_specs=[pl.BlockSpec(memory_space=pltpu.VMEM)] * len(parts),
        compiler_params=pltpu.CompilerParams(vmem_limit_bytes=VMEM_LIMIT),
        cost_estimate=pl.CostEstimate(
            flops=len(parts) * parts[0].size,
            bytes_accessed=2 * (len(parts) + 1) * parts[0].size,
            transcendentals=0,
        ),
        name="weight_sum",
    )(*parts)


def final_kernel(pieces, weight_ref, *refs):
    *in_refs, feature_out, weight_out, held, sems = refs
    copies = [pltpu.make_async_copy(weight_ref, weight_out, sems.at[pieces])]
    copies[0].start()
    rows = held.shape[0] // pieces
    for p in range(pieces):
        at = pl.ds(p * rows, rows)
        held[at, :] = total_of(in_refs, at)
        copies.append(pltpu.make_async_copy(held.at[at], feature_out.at[at], sems.at[p]))
        copies[-1].start()
    for copy in copies:
        copy.wait()


def finish(weight_grad, parts, pieces):
    shape = parts[0].shape
    return pl.pallas_call(
        functools.partial(final_kernel, pieces),
        out_shape=[
            jax.ShapeDtypeStruct(shape, jnp.bfloat16),
            jax.ShapeDtypeStruct(weight_grad.shape, jnp.bfloat16),
        ],
        in_specs=[pl.BlockSpec(memory_space=pltpu.VMEM)] * (len(parts) + 1),
        out_specs=[pl.BlockSpec(memory_space=pl.ANY)] * 2,
        scratch_shapes=[
            pltpu.VMEM(shape, jnp.bfloat16),
            pltpu.SemaphoreType.DMA((pieces + 1,)),
        ],
        compiler_params=pltpu.CompilerParams(vmem_limit_bytes=VMEM_LIMIT),
        cost_estimate=pl.CostEstimate(
            flops=len(parts) * parts[0].size,
            bytes_accessed=2 * (len(parts) + 1) * parts[0].size + 4 * weight_grad.size,
            transcendentals=0,
        ),
        name="finish",
    )(weight_grad, *parts)


def after(array, *others):
    return lax.optimization_barrier((array, *others))[0]


def local(features, shortlist, positives, cluster_sizes, weights):
    inst_rows, width = features.shape
    top_count, pos_count = shortlist.shape[1], positives.shape[1]
    clus_count, seq_count = lax.axis_size("clus"), lax.axis_size("seq")
    local_count = cluster_sizes.shape[0]
    part_width = width // seq_count
    first_part, half, steps = inst_rows * 3 // 4, inst_rows // 2, clus_count // 2

    ring = list(range(0, clus_count, 2)) + list(range(1, clus_count, 2))[::-1]
    up = list(zip(ring, ring[1:] + ring[:1]))
    down = [(b, a) for a, b in up]

    def send_up(array):
        return lax.ppermute(array, "clus", up)

    def send_down(array):
        return lax.ppermute(array, "clus", down)

    used, slopes = [], []

    def take(*blocks, grad_rows=None):
        grads, found = block_work(blocks, weights, live_table, top_count, pos_count, grad_rows)
        used.extend(blocks)
        slopes.extend(found)
        return grads

    ids = instance_ids(shortlist, positives, width)
    live_table = live_labels(cluster_sizes, weights)
    own = jnp.concatenate([features, ids], axis=0)
    below, below_ids = send_up(features), send_up(ids)
    above, above_ids = send_down(features), send_down(ids)
    below = jnp.concatenate([after(below, live_table), below_ids], axis=0)
    above = jnp.concatenate([after(above, live_table), above_ids], axis=0)
    below_grad, above_grad = {}, {}
    for k in range(2, steps + 1):
        if k > 2:
            before = below_grad[k - 2]
            below, above = after(below, before), after(above, before)
        if k < steps:
            arriving = send_up(below), send_down(above)
        else:
            ends = jnp.concatenate([below[:first_part], below[inst_rows:]], axis=0)
            arriving = send_up(ends), send_down(above[first_part:inst_rows])
        if k == 3 or steps < 3:
            below_grad[k - 1], above_grad[k - 1], own_grad = take([below], [above], [own])
        else:
            below_grad[k - 1], above_grad[k - 1] = take([below], [above])
        below, above = arriving
    opposite = [after(below, below_grad[steps - 1]), above]
    to_down, to_up = take(opposite, grad_rows=[half, half])

    scale = 1.0 / math.sqrt(inst_rows * seq_count * top_count // local_count)

    def seq_send(array, bit):
        return lax.ppermute(array, "seq", [(k, k ^ bit) for k in range(seq_count)])

    slots = list(range(seq_count))[::-1]
    parts = weight_work(used, slopes, slots, part_width, scale)
    terms = {q: [part] for q, part in zip(slots, parts)}
    bit = 1
    while bit < seq_count:
        for q in [q for q in sorted(terms, reverse=True) if q & bit]:
            values = terms.pop(q)
            terms[q ^ bit].append(seq_send(add(*values) if len(values) > 1 else values[0], bit))
        bit *= 2

    for k in range(steps, 0, -1):
        from_above, from_below = send_down(to_down), send_up(to_up)
        if k == steps:
            near_below, near_above = below_grad[k - 1], above_grad[k - 1]
            to_down = jnp.concatenate([add(near_below[:half], from_above), near_below[half:]], axis=0)
            to_up = jnp.concatenate([near_above[:half], add(near_above[half:], from_below)], axis=0)
        elif k > 1:
            to_down, to_up = add(below_grad[k - 1], from_above), add(above_grad[k - 1], from_below)
    feature_grad, weight_grad = finish(weight_sum(terms[0]), [own_grad, from_above, from_below], 2)
    return (feature_grad, weight_grad)


def solution(mesh):
    return jax.shard_map(
        local,
        mesh=mesh,
        in_specs=(
            P(("seq", "clus"), None),
            P(("seq", "clus"), None),
            P(("seq", "clus"), None),
            P("clus"),
            P("clus", None),
        ),
        out_specs=(P(("seq", "clus"), None), P("clus", "seq")),
        check_vma=False,
    )
```

```python
import functools
import math

import jax
import jax.numpy as jnp
from jax import lax
from jax.experimental import pallas as pl
from jax.experimental.pallas import tpu as pltpu
from jax.sharding import PartitionSpec as P

BLOCK = 128
LANES = 128
FIELD_ROWS = 8
CHUNK = 256
VMEM_LIMIT = 40 * 1024 * 1024


def ids_kernel(width, short_ref, pos_ref, out_ref):
    rows = short_ref.shape[1]
    short = short_ref[...]
    places = pos_ref[...] // BLOCK
    offsets = pos_ref[...] % BLOCK
    targets = jnp.zeros_like(places)
    for j in range(short.shape[0]):
        targets = targets + jnp.where(places == j, short[j : j + 1, :], 0)
    fields = jnp.concatenate([short, targets, offsets], axis=0)
    groups = [
        fields[at : at + FIELD_ROWS] for at in range(0, fields.shape[0], FIELD_ROWS)
    ]
    groups.append(jnp.zeros((FIELD_ROWS, width - rows * len(groups)), jnp.int32))
    meta = jnp.concatenate(groups, axis=1)
    out_ref[...] = meta.astype(jnp.float32).astype(jnp.bfloat16)


def instance_ids(shortlist, positives, width):
    return pl.pallas_call(
        functools.partial(ids_kernel, width),
        out_shape=jax.ShapeDtypeStruct((FIELD_ROWS, width), jnp.bfloat16),
        in_specs=[pl.BlockSpec(memory_space=pltpu.VMEM)] * 2,
        compiler_params=pltpu.CompilerParams(vmem_limit_bytes=VMEM_LIMIT),
        name="instance_ids",
    )(shortlist.T, positives.T)


def live_kernel(size_ref, w_ref, live_ref):
    lane = lax.broadcasted_iota(jnp.int32, (LANES, BLOCK), 1)
    row = lax.broadcasted_iota(jnp.int32, (LANES, BLOCK), 0)
    for c in range(size_ref.shape[0]):
        live = jnp.where((row == c) & (lane < size_ref[c]), 2.0, 0.0)
        live_ref[:, c * BLOCK : (c + 1) * BLOCK] = live.astype(jnp.bfloat16)


def live_labels(cluster_sizes, weights):
    return pl.pallas_call(
        live_kernel,
        out_shape=jax.ShapeDtypeStruct((LANES, cluster_sizes.shape[0] * BLOCK), jnp.bfloat16),
        in_specs=[
            pl.BlockSpec(memory_space=pltpu.SMEM),
            pl.BlockSpec(memory_space=pltpu.VMEM),
        ],
        compiler_params=pltpu.CompilerParams(vmem_limit_bytes=VMEM_LIMIT),
        name="live_labels",
    )(cluster_sizes, weights)


def block_kernel(piece_rows, top_count, pos_count, *refs):
    block_count = len(piece_rows)
    piece_count = sum(len(pieces) for pieces in piece_rows)
    x_refs = refs[:piece_count]
    w_ref, live_ref = refs[piece_count : piece_count + 2]
    grad_refs = refs[piece_count + 2 : len(refs) - block_count]
    slope_refs = refs[len(refs) - block_count :]
    labels, width = w_ref.shape
    local_count = labels // BLOCK
    rows = slope_refs[0].shape[0]
    first = (lax.axis_index("clus") * local_count).astype(jnp.float32)

    named, pieces = [], []
    cluster = lax.broadcasted_iota(jnp.int32, (FIELD_ROWS, rows), 0).astype(jnp.float32) + first
    at = 0
    for b in range(block_count):
        block_refs = x_refs[at : at + len(piece_rows[b])]
        at += len(piece_rows[b])
        pieces += [ref[:count, :] for ref, count in zip(block_refs, piece_rows[b])]
        groups = -(-(top_count + 2 * pos_count) // FIELD_ROWS)
        meta = block_refs[0][piece_rows[b][0] :, : groups * rows].astype(jnp.float32)
        field = [
            meta[f % FIELD_ROWS : f % FIELD_ROWS + 1, f // FIELD_ROWS * rows : (f // FIELD_ROWS + 1) * rows]
            for f in range(top_count + 2 * pos_count)
        ]
        member = jnp.zeros((FIELD_ROWS, rows), jnp.float32)
        for j in range(top_count):
            member = jnp.where(cluster == field[j], 1.0, member)
        target = [
            (field[top_count + q] - first) * BLOCK + field[top_count + pos_count + q]
            for q in range(pos_count)
        ]
        rest = jnp.zeros((LANES - FIELD_ROWS - pos_count, rows), jnp.float32)
        named.append(jnp.concatenate([member] + target + [rest], axis=0).T)

    x = jnp.concatenate(pieces, axis=0) if len(pieces) > 1 else pieces[0]
    named = jnp.concatenate(named, axis=0) if block_count > 1 else named[0]
    target = [named[:, FIELD_ROWS + q : FIELD_ROWS + q + 1] for q in range(pos_count)]
    member = jnp.where(
        lax.broadcasted_iota(jnp.int32, named.shape, 1) < FIELD_ROWS, named, 0.0
    ).astype(jnp.bfloat16)
    for start in range(0, labels, CHUNK):
        logits = lax.dot_general(
            x,
            w_ref[start : start + CHUNK, :],
            (((1,), (1,)), ((), ())),
            preferred_element_type=jnp.float32,
        )
        live = jnp.dot(
            member, live_ref[:, start : start + CHUNK], preferred_element_type=jnp.float32
        )
        label = (
            lax.broadcasted_iota(jnp.int32, (1, CHUNK), 1) + start
        ).astype(jnp.float32)
        positive = target[0] == label
        for q in range(1, pos_count):
            positive = positive | (target[q] == label)
        turned = jnp.where(positive, -1.0, 1.0)
        slope = (turned * live * jnp.maximum(1.0 + turned * logits, 0.0)).astype(jnp.bfloat16)
        for b, ref in enumerate(slope_refs):
            ref[:, start : start + CHUNK] = slope[b * rows : (b + 1) * rows]
    slope = [ref[...] for ref in slope_refs]
    slope = jnp.concatenate(slope, axis=0) if block_count > 1 else slope[0]
    for start in range(0, width, CHUNK):
        part = jnp.dot(
            slope, w_ref[:, start : start + CHUNK], preferred_element_type=jnp.float32
        ).astype(jnp.bfloat16)
        at = 0
        for ref in grad_refs:
            ref[:, start : start + CHUNK] = part[at : at + ref.shape[0]]
            at += ref.shape[0]


def block_work(blocks, weights, live_table, top_count, pos_count, grad_rows=None):
    labels, width = weights.shape
    piece_rows = [
        [piece.shape[0] - (FIELD_ROWS if p == 0 else 0) for p, piece in enumerate(pieces)]
        for pieces in blocks
    ]
    flat_rows = sum(piece_rows, [])
    grad_rows = grad_rows or flat_rows
    out = pl.pallas_call(
        functools.partial(block_kernel, piece_rows, top_count, pos_count),
        out_shape=[jax.ShapeDtypeStruct((rows, width), jnp.bfloat16) for rows in grad_rows]
        + [jax.ShapeDtypeStruct((sum(rows), labels), jnp.bfloat16) for rows in piece_rows],
        in_specs=[pl.BlockSpec(memory_space=pltpu.VMEM)] * (len(flat_rows) + 2),
        compiler_params=pltpu.CompilerParams(vmem_limit_bytes=VMEM_LIMIT),
        cost_estimate=pl.CostEstimate(
            flops=4 * sum(flat_rows) * labels * width,
            bytes_accessed=2 * labels * width + 6 * sum(flat_rows) * width,
            transcendentals=0,
        ),
        name="block_work",
    )(*[piece for pieces in blocks for piece in pieces], weights, live_table)
    return list(out[: len(grad_rows)]), list(out[len(grad_rows) :])


def weight_kernel(piece_rows, column_blocks, scale, *refs):
    piece_count = len(piece_rows)
    out_refs = refs[len(refs) - len(column_blocks) :]
    x_refs, s_refs = refs[:piece_count], refs[piece_count : len(refs) - len(column_blocks)]
    part_width = out_refs[0].shape[1]
    slopes = jnp.concatenate([ref[...] for ref in s_refs], axis=0)
    for ref, q in zip(out_refs, column_blocks):
        at = pl.multiple_of((lax.axis_index("seq") ^ q) * part_width, part_width)
        x = jnp.concatenate(
            [r[:rows, pl.ds(at, part_width)] for r, rows in zip(x_refs, piece_rows)], axis=0
        )
        part = lax.dot_general(
            slopes, x, (((0,), (0,)), ((), ())), preferred_element_type=jnp.float32
        )
        ref[...] = (part * scale).astype(jnp.bfloat16)


def weight_work(blocks, slopes, column_blocks, part_width, scale):
    pieces = [piece for block in blocks for piece in block]
    piece_rows = [
        piece.shape[0] - (FIELD_ROWS if p == 0 else 0)
        for block in blocks
        for p, piece in enumerate(block)
    ]
    labels = slopes[0].shape[1]
    rows = sum(piece_rows)
    return pl.pallas_call(
        functools.partial(weight_kernel, piece_rows, column_blocks, scale),
        out_shape=[jax.ShapeDtypeStruct((labels, part_width), jnp.bfloat16)] * len(column_blocks),
        in_specs=[pl.BlockSpec(memory_space=pltpu.VMEM)] * (len(pieces) + len(slopes)),
        compiler_params=pltpu.CompilerParams(vmem_limit_bytes=VMEM_LIMIT),
        cost_estimate=pl.CostEstimate(
            flops=2 * rows * labels * part_width * len(column_blocks),
            bytes_accessed=2 * rows * (labels + 1024) + 2 * labels * part_width,
            transcendentals=0,
        ),
        name="weight_work",
    )(*pieces, *slopes)


def add(*parts):
    total = parts[0].astype(jnp.float32)
    for part in parts[1:]:
        total = total + part.astype(jnp.float32)
    return total.astype(jnp.bfloat16)


def total_of(refs, at):
    total = refs[0][at, :].astype(jnp.float32)
    for ref in refs[1:]:
        total = total + ref[at, :].astype(jnp.float32)
    return total.astype(jnp.bfloat16)


def sum_kernel(*refs):
    *in_refs, out_ref = refs
    out_ref[...] = total_of(in_refs, slice(None))


def weight_sum(parts):
    return pl.pallas_call(
        sum_kernel,
        out_shape=jax.ShapeDtypeStruct(parts[0].shape, jnp.bfloat16),
        in_specs=[pl.BlockSpec(memory_space=pltpu.VMEM)] * len(parts),
        compiler_params=pltpu.CompilerParams(vmem_limit_bytes=VMEM_LIMIT),
        cost_estimate=pl.CostEstimate(
            flops=len(parts) * parts[0].size,
            bytes_accessed=2 * (len(parts) + 1) * parts[0].size,
            transcendentals=0,
        ),
        name="weight_sum",
    )(*parts)


def final_kernel(pieces, weight_ref, *refs):
    *in_refs, feature_out, weight_out, held, sems = refs
    copies = [pltpu.make_async_copy(weight_ref, weight_out, sems.at[pieces])]
    copies[0].start()
    rows = held.shape[0] // pieces
    for p in range(pieces):
        at = pl.ds(p * rows, rows)
        held[at, :] = total_of(in_refs, at)
        copies.append(pltpu.make_async_copy(held.at[at], feature_out.at[at], sems.at[p]))
        copies[-1].start()
    for copy in copies:
        copy.wait()


def finish(weight_grad, parts, pieces):
    shape = parts[0].shape
    return pl.pallas_call(
        functools.partial(final_kernel, pieces),
        out_shape=[
            jax.ShapeDtypeStruct(shape, jnp.bfloat16),
            jax.ShapeDtypeStruct(weight_grad.shape, jnp.bfloat16),
        ],
        in_specs=[pl.BlockSpec(memory_space=pltpu.VMEM)] * (len(parts) + 1),
        out_specs=[pl.BlockSpec(memory_space=pl.ANY)] * 2,
        scratch_shapes=[
            pltpu.VMEM(shape, jnp.bfloat16),
            pltpu.SemaphoreType.DMA((pieces + 1,)),
        ],
        compiler_params=pltpu.CompilerParams(vmem_limit_bytes=VMEM_LIMIT),
        cost_estimate=pl.CostEstimate(
            flops=len(parts) * parts[0].size,
            bytes_accessed=2 * (len(parts) + 1) * parts[0].size + 4 * weight_grad.size,
            transcendentals=0,
        ),
        name="finish",
    )(weight_grad, *parts)


def after(array, *others):
    return lax.optimization_barrier((array, *others))[0]


def local(features, shortlist, positives, cluster_sizes, weights):
    inst_rows, width = features.shape
    top_count, pos_count = shortlist.shape[1], positives.shape[1]
    clus_count, seq_count = lax.axis_size("clus"), lax.axis_size("seq")
    local_count = cluster_sizes.shape[0]
    part_width = width // seq_count
    first_part, half, steps = inst_rows * 5 // 8, inst_rows // 2, clus_count // 2

    ring = list(range(0, clus_count, 2)) + list(range(1, clus_count, 2))[::-1]
    up = list(zip(ring, ring[1:] + ring[:1]))
    down = [(b, a) for a, b in up]

    def send_up(array):
        return lax.ppermute(array, "clus", up)

    def send_down(array):
        return lax.ppermute(array, "clus", down)

    used, slopes = [], []

    def take(*blocks, grad_rows=None):
        grads, found = block_work(blocks, weights, live_table, top_count, pos_count, grad_rows)
        used.extend(blocks)
        slopes.extend(found)
        return grads

    ids = instance_ids(shortlist, positives, width)
    live_table = live_labels(cluster_sizes, weights)
    own = jnp.concatenate([features, ids], axis=0)
    below, below_ids = send_up(features), send_up(ids)
    above, above_ids = send_down(features), send_down(ids)
    below = jnp.concatenate([after(below, live_table), below_ids], axis=0)
    above = jnp.concatenate([after(above, live_table), above_ids], axis=0)
    below_grad, above_grad = {}, {}
    for k in range(2, steps + 1):
        if k > 2:
            before = below_grad[k - 2]
            below, above = after(below, before), after(above, before)
        if k < steps:
            arriving = send_up(below), send_down(above)
        else:
            ends = jnp.concatenate([below[:first_part], below[inst_rows:]], axis=0)
            arriving = send_up(ends), send_down(above[first_part:inst_rows])
        if k == 3 or steps < 3:
            below_grad[k - 1], above_grad[k - 1], own_grad = take([below], [above], [own])
        else:
            below_grad[k - 1], above_grad[k - 1] = take([below], [above])
        below, above = arriving
    opposite = [after(below, below_grad[steps - 1]), above]
    to_down, to_up = take(opposite, grad_rows=[half, half])

    scale = 1.0 / math.sqrt(inst_rows * seq_count * top_count // local_count)

    def seq_send(array, bit):
        return lax.ppermute(array, "seq", [(k, k ^ bit) for k in range(seq_count)])

    slots = list(range(seq_count))[::-1]
    parts = weight_work(used, slopes, slots, part_width, scale)
    terms = {q: [part] for q, part in zip(slots, parts)}
    for k in range(steps, 0, -1):
        if k == max(steps - 2, 1):
            third = to_down
        from_above, from_below = send_down(to_down), send_up(to_up)
        if k == steps:
            near_below, near_above = below_grad[k - 1], above_grad[k - 1]
            to_down = jnp.concatenate([add(near_below[:half], from_above), near_below[half:]], axis=0)
            to_up = jnp.concatenate([near_above[:half], add(near_above[half:], from_below)], axis=0)
        elif k > 1:
            to_down, to_up = add(below_grad[k - 1], from_above), add(above_grad[k - 1], from_below)

    bit = 1
    while bit < seq_count:
        for q in [q for q in sorted(terms, reverse=True) if q & bit]:
            values = terms.pop(q)
            if bit == 1 and q < seq_count // 2:
                values = [after(values[0], third)]
            terms[q ^ bit].append(seq_send(add(*values) if len(values) > 1 else values[0], bit))
        bit *= 2

    feature_grad, weight_grad = finish(weight_sum(terms[0]), [own_grad, from_above, from_below], 2)
    return (feature_grad, weight_grad)


def solution(mesh):
    return jax.shard_map(
        local,
        mesh=mesh,
        in_specs=(
            P(("seq", "clus"), None),
            P(("seq", "clus"), None),
            P(("seq", "clus"), None),
            P("clus"),
            P("clus", None),
        ),
        out_specs=(P(("seq", "clus"), None), P("clus", "seq")),
        check_vma=False,
    )
```

```python
import functools
import math

import jax
import jax.numpy as jnp
from jax import lax
from jax.experimental import pallas as pl
from jax.experimental.pallas import tpu as pltpu
from jax.sharding import PartitionSpec as P

BLOCK = 128
LANES = 128
FIELD_ROWS = 8
CHUNK = 256
VMEM_LIMIT = 40 * 1024 * 1024


def ids_kernel(width, short_ref, pos_ref, out_ref):
    rows = short_ref.shape[1]
    short = short_ref[...]
    places = pos_ref[...] // BLOCK
    offsets = pos_ref[...] % BLOCK
    targets = jnp.zeros_like(places)
    for j in range(short.shape[0]):
        targets = targets + jnp.where(places == j, short[j : j + 1, :], 0)
    fields = jnp.concatenate([short, targets, offsets], axis=0)
    groups = [
        fields[at : at + FIELD_ROWS] for at in range(0, fields.shape[0], FIELD_ROWS)
    ]
    groups.append(jnp.zeros((FIELD_ROWS, width - rows * len(groups)), jnp.int32))
    meta = jnp.concatenate(groups, axis=1)
    out_ref[...] = meta.astype(jnp.float32).astype(jnp.bfloat16)


def instance_ids(shortlist, positives, width):
    return pl.pallas_call(
        functools.partial(ids_kernel, width),
        out_shape=jax.ShapeDtypeStruct((FIELD_ROWS, width), jnp.bfloat16),
        in_specs=[pl.BlockSpec(memory_space=pltpu.VMEM)] * 2,
        compiler_params=pltpu.CompilerParams(vmem_limit_bytes=VMEM_LIMIT),
        name="instance_ids",
    )(shortlist.T, positives.T)


def live_kernel(size_ref, w_ref, live_ref):
    lane = lax.broadcasted_iota(jnp.int32, (LANES, BLOCK), 1)
    row = lax.broadcasted_iota(jnp.int32, (LANES, BLOCK), 0)
    for c in range(size_ref.shape[0]):
        live = jnp.where((row == c) & (lane < size_ref[c]), 2.0, 0.0)
        live_ref[:, c * BLOCK : (c + 1) * BLOCK] = live.astype(jnp.bfloat16)


def live_labels(cluster_sizes, weights):
    return pl.pallas_call(
        live_kernel,
        out_shape=jax.ShapeDtypeStruct((LANES, cluster_sizes.shape[0] * BLOCK), jnp.bfloat16),
        in_specs=[
            pl.BlockSpec(memory_space=pltpu.SMEM),
            pl.BlockSpec(memory_space=pltpu.VMEM),
        ],
        compiler_params=pltpu.CompilerParams(vmem_limit_bytes=VMEM_LIMIT),
        name="live_labels",
    )(cluster_sizes, weights)


def block_kernel(piece_rows, top_count, pos_count, *refs):
    block_count = len(piece_rows)
    piece_count = sum(len(pieces) for pieces in piece_rows)
    x_refs = refs[:piece_count]
    w_ref, live_ref = refs[piece_count : piece_count + 2]
    grad_refs = refs[piece_count + 2 : len(refs) - block_count]
    slope_refs = refs[len(refs) - block_count :]
    labels, width = w_ref.shape
    local_count = labels // BLOCK
    rows = slope_refs[0].shape[0]
    first = (lax.axis_index("clus") * local_count).astype(jnp.float32)

    named, pieces = [], []
    cluster = lax.broadcasted_iota(jnp.int32, (FIELD_ROWS, rows), 0).astype(jnp.float32) + first
    at = 0
    for b in range(block_count):
        block_refs = x_refs[at : at + len(piece_rows[b])]
        at += len(piece_rows[b])
        pieces += [ref[:count, :] for ref, count in zip(block_refs, piece_rows[b])]
        groups = -(-(top_count + 2 * pos_count) // FIELD_ROWS)
        meta = block_refs[0][piece_rows[b][0] :, : groups * rows].astype(jnp.float32)
        field = [
            meta[f % FIELD_ROWS : f % FIELD_ROWS + 1, f // FIELD_ROWS * rows : (f // FIELD_ROWS + 1) * rows]
            for f in range(top_count + 2 * pos_count)
        ]
        member = jnp.zeros((FIELD_ROWS, rows), jnp.float32)
        for j in range(top_count):
            member = jnp.where(cluster == field[j], 1.0, member)
        target = [
            (field[top_count + q] - first) * BLOCK + field[top_count + pos_count + q]
            for q in range(pos_count)
        ]
        rest = jnp.zeros((LANES - FIELD_ROWS - pos_count, rows), jnp.float32)
        named.append(jnp.concatenate([member] + target + [rest], axis=0).T)

    x = jnp.concatenate(pieces, axis=0) if len(pieces) > 1 else pieces[0]
    named = jnp.concatenate(named, axis=0) if block_count > 1 else named[0]
    target = [named[:, FIELD_ROWS + q : FIELD_ROWS + q + 1] for q in range(pos_count)]
    member = jnp.where(
        lax.broadcasted_iota(jnp.int32, named.shape, 1) < FIELD_ROWS, named, 0.0
    ).astype(jnp.bfloat16)
    for start in range(0, labels, CHUNK):
        logits = lax.dot_general(
            x,
            w_ref[start : start + CHUNK, :],
            (((1,), (1,)), ((), ())),
            preferred_element_type=jnp.float32,
        )
        live = jnp.dot(
            member, live_ref[:, start : start + CHUNK], preferred_element_type=jnp.float32
        )
        label = (
            lax.broadcasted_iota(jnp.int32, (1, CHUNK), 1) + start
        ).astype(jnp.float32)
        positive = target[0] == label
        for q in range(1, pos_count):
            positive = positive | (target[q] == label)
        turned = jnp.where(positive, -1.0, 1.0)
        slope = (turned * live * jnp.maximum(1.0 + turned * logits, 0.0)).astype(jnp.bfloat16)
        for b, ref in enumerate(slope_refs):
            ref[:, start : start + CHUNK] = slope[b * rows : (b + 1) * rows]
    slope = [ref[...] for ref in slope_refs]
    slope = jnp.concatenate(slope, axis=0) if block_count > 1 else slope[0]
    for start in range(0, width, CHUNK):
        part = jnp.dot(
            slope, w_ref[:, start : start + CHUNK], preferred_element_type=jnp.float32
        ).astype(jnp.bfloat16)
        at = 0
        for ref in grad_refs:
            ref[:, start : start + CHUNK] = part[at : at + ref.shape[0]]
            at += ref.shape[0]


def block_work(blocks, weights, live_table, top_count, pos_count, grad_rows=None):
    labels, width = weights.shape
    piece_rows = [
        [piece.shape[0] - (FIELD_ROWS if p == 0 else 0) for p, piece in enumerate(pieces)]
        for pieces in blocks
    ]
    flat_rows = sum(piece_rows, [])
    grad_rows = grad_rows or flat_rows
    out = pl.pallas_call(
        functools.partial(block_kernel, piece_rows, top_count, pos_count),
        out_shape=[jax.ShapeDtypeStruct((rows, width), jnp.bfloat16) for rows in grad_rows]
        + [jax.ShapeDtypeStruct((sum(rows), labels), jnp.bfloat16) for rows in piece_rows],
        in_specs=[pl.BlockSpec(memory_space=pltpu.VMEM)] * (len(flat_rows) + 2),
        compiler_params=pltpu.CompilerParams(vmem_limit_bytes=VMEM_LIMIT),
        cost_estimate=pl.CostEstimate(
            flops=4 * sum(flat_rows) * labels * width,
            bytes_accessed=2 * labels * width + 6 * sum(flat_rows) * width,
            transcendentals=0,
        ),
        name="block_work",
    )(*[piece for pieces in blocks for piece in pieces], weights, live_table)
    return list(out[: len(grad_rows)]), list(out[len(grad_rows) :])


def weight_kernel(piece_rows, column_blocks, scale, *refs):
    piece_count = len(piece_rows)
    out_refs = refs[len(refs) - len(column_blocks) :]
    x_refs, s_refs = refs[:piece_count], refs[piece_count : len(refs) - len(column_blocks)]
    part_width = out_refs[0].shape[1]
    slopes = jnp.concatenate([ref[...] for ref in s_refs], axis=0)
    for ref, q in zip(out_refs, column_blocks):
        at = pl.multiple_of((lax.axis_index("seq") ^ q) * part_width, part_width)
        x = jnp.concatenate(
            [r[:rows, pl.ds(at, part_width)] for r, rows in zip(x_refs, piece_rows)], axis=0
        )
        part = lax.dot_general(
            slopes, x, (((0,), (0,)), ((), ())), preferred_element_type=jnp.float32
        )
        ref[...] = (part * scale).astype(jnp.bfloat16)


def weight_work(blocks, slopes, column_blocks, part_width, scale):
    pieces = [piece for block in blocks for piece in block]
    piece_rows = [
        piece.shape[0] - (FIELD_ROWS if p == 0 else 0)
        for block in blocks
        for p, piece in enumerate(block)
    ]
    labels = slopes[0].shape[1]
    rows = sum(piece_rows)
    return pl.pallas_call(
        functools.partial(weight_kernel, piece_rows, column_blocks, scale),
        out_shape=[jax.ShapeDtypeStruct((labels, part_width), jnp.bfloat16)] * len(column_blocks),
        in_specs=[pl.BlockSpec(memory_space=pltpu.VMEM)] * (len(pieces) + len(slopes)),
        compiler_params=pltpu.CompilerParams(vmem_limit_bytes=VMEM_LIMIT),
        cost_estimate=pl.CostEstimate(
            flops=2 * rows * labels * part_width * len(column_blocks),
            bytes_accessed=2 * rows * (labels + 1024) + 2 * labels * part_width,
            transcendentals=0,
        ),
        name="weight_work",
    )(*pieces, *slopes)


def add(*parts):
    total = parts[0].astype(jnp.float32)
    for part in parts[1:]:
        total = total + part.astype(jnp.float32)
    return total.astype(jnp.bfloat16)


def total_of(refs, at):
    total = refs[0][at, :].astype(jnp.float32)
    for ref in refs[1:]:
        total = total + ref[at, :].astype(jnp.float32)
    return total.astype(jnp.bfloat16)


def sum_kernel(*refs):
    *in_refs, out_ref = refs
    out_ref[...] = total_of(in_refs, slice(None))


def weight_sum(parts):
    return pl.pallas_call(
        sum_kernel,
        out_shape=jax.ShapeDtypeStruct(parts[0].shape, jnp.bfloat16),
        in_specs=[pl.BlockSpec(memory_space=pltpu.VMEM)] * len(parts),
        compiler_params=pltpu.CompilerParams(vmem_limit_bytes=VMEM_LIMIT),
        cost_estimate=pl.CostEstimate(
            flops=len(parts) * parts[0].size,
            bytes_accessed=2 * (len(parts) + 1) * parts[0].size,
            transcendentals=0,
        ),
        name="weight_sum",
    )(*parts)


def final_kernel(pieces, weight_ref, *refs):
    *in_refs, feature_out, weight_out, held, sems = refs
    copies = [pltpu.make_async_copy(weight_ref, weight_out, sems.at[pieces])]
    copies[0].start()
    rows = held.shape[0] // pieces
    for p in range(pieces):
        at = pl.ds(p * rows, rows)
        held[at, :] = total_of(in_refs, at)
        copies.append(pltpu.make_async_copy(held.at[at], feature_out.at[at], sems.at[p]))
        copies[-1].start()
    for copy in copies:
        copy.wait()


def finish(weight_grad, parts, pieces):
    shape = parts[0].shape
    return pl.pallas_call(
        functools.partial(final_kernel, pieces),
        out_shape=[
            jax.ShapeDtypeStruct(shape, jnp.bfloat16),
            jax.ShapeDtypeStruct(weight_grad.shape, jnp.bfloat16),
        ],
        in_specs=[pl.BlockSpec(memory_space=pltpu.VMEM)] * (len(parts) + 1),
        out_specs=[pl.BlockSpec(memory_space=pl.ANY)] * 2,
        scratch_shapes=[
            pltpu.VMEM(shape, jnp.bfloat16),
            pltpu.SemaphoreType.DMA((pieces + 1,)),
        ],
        compiler_params=pltpu.CompilerParams(vmem_limit_bytes=VMEM_LIMIT),
        cost_estimate=pl.CostEstimate(
            flops=len(parts) * parts[0].size,
            bytes_accessed=2 * (len(parts) + 1) * parts[0].size + 4 * weight_grad.size,
            transcendentals=0,
        ),
        name="finish",
    )(weight_grad, *parts)


def after(array, *others):
    return lax.optimization_barrier((array, *others))[0]


def local(features, shortlist, positives, cluster_sizes, weights):
    inst_rows, width = features.shape
    top_count, pos_count = shortlist.shape[1], positives.shape[1]
    clus_count, seq_count = lax.axis_size("clus"), lax.axis_size("seq")
    local_count = cluster_sizes.shape[0]
    part_width = width // seq_count
    first_part, half, steps = inst_rows * 5 // 8, inst_rows // 2, clus_count // 2

    ring = list(range(0, clus_count, 2)) + list(range(1, clus_count, 2))[::-1]
    up = list(zip(ring, ring[1:] + ring[:1]))
    down = [(b, a) for a, b in up]

    def send_up(array):
        return lax.ppermute(array, "clus", up)

    def send_down(array):
        return lax.ppermute(array, "clus", down)

    used, slopes = [], []

    def take(*blocks, grad_rows=None):
        grads, found = block_work(blocks, weights, live_table, top_count, pos_count, grad_rows)
        used.extend(blocks)
        slopes.extend(found)
        return grads

    ids = instance_ids(shortlist, positives, width)
    live_table = live_labels(cluster_sizes, weights)
    own = jnp.concatenate([features, ids], axis=0)
    below, below_ids = send_up(features), send_up(ids)
    above, above_ids = send_down(features), send_down(ids)
    below = jnp.concatenate([after(below, live_table), below_ids], axis=0)
    above = jnp.concatenate([after(above, live_table), above_ids], axis=0)
    below_grad, above_grad = {}, {}
    for k in range(2, steps + 1):
        if k > 2:
            before = below_grad[k - 2]
            below, above = after(below, before), after(above, before)
        if k < steps:
            arriving = send_up(below), send_down(above)
        else:
            ends = jnp.concatenate([below[:first_part], below[inst_rows:]], axis=0)
            arriving = send_up(ends), send_down(above[first_part:inst_rows])
        if k == 3 or steps < 3:
            below_grad[k - 1], above_grad[k - 1], own_grad = take([below], [above], [own])
        else:
            below_grad[k - 1], above_grad[k - 1] = take([below], [above])
        below, above = arriving
    opposite = [after(below, below_grad[steps - 1]), above]
    to_down, to_up = take(opposite, grad_rows=[half, half])

    scale = 1.0 / math.sqrt(inst_rows * seq_count * top_count // local_count)

    def seq_send(array, bit):
        return lax.ppermute(array, "seq", [(k, k ^ bit) for k in range(seq_count)])

    far, near = list(range(seq_count // 2, seq_count))[::-1], list(range(seq_count // 2))[::-1]
    terms = {}
    for slots in (far, near):
        parts = weight_work(used, slopes, slots, part_width, scale)
        terms.update({q: [part] for q, part in zip(slots, parts)})
    bit = 1
    while bit < seq_count:
        for q in [q for q in sorted(terms, reverse=True) if q & bit]:
            values = terms.pop(q)
            terms[q ^ bit].append(seq_send(add(*values) if len(values) > 1 else values[0], bit))
        bit *= 2

    for k in range(steps, 0, -1):
        from_above, from_below = send_down(to_down), send_up(to_up)
        if k == steps:
            near_below, near_above = below_grad[k - 1], above_grad[k - 1]
            to_down = jnp.concatenate([add(near_below[:half], from_above), near_below[half:]], axis=0)
            to_up = jnp.concatenate([near_above[:half], add(near_above[half:], from_below)], axis=0)
        elif k > 1:
            to_down, to_up = add(below_grad[k - 1], from_above), add(above_grad[k - 1], from_below)
    feature_grad, weight_grad = finish(weight_sum(terms[0]), [own_grad, from_above, from_below], 2)
    return (feature_grad, weight_grad)


def solution(mesh):
    return jax.shard_map(
        local,
        mesh=mesh,
        in_specs=(
            P(("seq", "clus"), None),
            P(("seq", "clus"), None),
            P(("seq", "clus"), None),
            P("clus"),
            P("clus", None),
        ),
        out_specs=(P(("seq", "clus"), None), P("clus", "seq")),
        check_vma=False,
    )
```
